128 devices in a mesh: gx: 8 (over x, z_lo), gy: 16 (over y, z_hi, core).
Axes of the slice: x: 4, y: 4, z: 4 (z_hi: 2, z_lo: 2; z = z_hi * 2 + z_lo), core: 2. Of those that a mesh axis runs over, the one named last changes fastest.
Arguments:
- initial_fields: float32 [5, 32, 64, 2048], P(None, 'gx', 'gy'), may hold values from -6 to 6
- velocity: float32 [3, 32, 64, 2048], P(None, 'gx', 'gy'), may hold values from -0.16 to 0.16
- diffusivity: float32 [32, 64, 2048], P('gx', 'gy'), may hold values from 0.08 to 0.16
- patch_anchor: int32 [8, 16, 2], P('gx', 'gy'), may hold values from 0 to 56
- patch_count: int32 [8, 16], P('gx', 'gy'), may hold values from 1 to 2, as said below
- weight_one: float32 [32, 5, 3, 3, 3], replicated, may hold values from -0.5 to 0.5
- bias_one: float32 [32], replicated, may hold values from -3 to 3
- weight_two: float32 [32, 32, 3, 3, 3], replicated, may hold values from -0.21875 to 0.21875
- bias_two: float32 [32], replicated, may hold values from -3 to 3
- weight_three: float32 [5, 32, 3, 3, 3], replicated, may hold values from -0.21875 to 0.21875
- bias_three: float32 [5], replicated, may hold values from -3 to 3
Outputs:
- final_fields: float32 [5, 32, 64, 2048], P(None, 'gx', 'gy')
- grad_weight_one: float32 [32, 5, 3, 3, 3], replicated
- grad_bias_one: float32 [32], replicated
- grad_weight_two: float32 [32, 32, 3, 3, 3], replicated
- grad_bias_two: float32 [32], replicated
- grad_weight_three: float32 [5, 32, 3, 3, 3], replicated
- grad_bias_three: float32 [5], replicated
- loss: float32 [], replicated
The draws below stay inside these ranges and needn't reach their ends.
Inputs may be any that keep to these rules, and one draw needn't show every extreme that they name: `patch_count`: slots 0 to count - 1 of a shard are live; at least one shard has all 2 slots live in every draw.
All inputs are finite; a program needn't handle non-finite values.
Results may differ from the reference program's by a relative error of at most 0.005.
Values sent between devices are 32-bit elements; how exact they have to be, the bound alone decides.
No kernel may reach another device: no remote copies, remote signals or barrier semaphores. Data moves between devices by JAX's collectives and lax.ppermute only.
A program may use at most 128 MiB of HBM per device.

```python
import jax
import jax.numpy as jnp
from jax import lax

FIELDS = 5
CHANNELS = 32
STEPS = 3
CX = 4
SLAB_Z = 128
PY = 8
PATCHES = 2
NX = 32
NY = 64
NZ = 2048
N_GX = 8
N_GY = 16


def draw_patch_count(key, part):
    key = jax.random.fold_in(key, 7)
    counts = jax.random.randint(key, (N_GX, N_GY), 1, PATCHES + 1)
    return counts.at[0, 0].set(PATCHES).astype(jnp.int32)


def place_ends(values, own_key, least, largest):
    longest = values.shape.index(max(values.shape))
    spots = []
    for shift in (0, 1):
        where = [jax.random.randint(jax.random.fold_in(own_key, axis), (), 0, length) for axis, length in enumerate(values.shape)]
        where[longest] = (where[longest] + shift) % values.shape[longest]
        spots.append(tuple(where))
    return values.at[spots[0]].set(least).at[spots[1]].set(largest)


def levels(rng, dims, shards, smallest, largest):
    gain = 1.0
    for position, shards_of in shards:
        heights = jax.random.uniform(jax.random.fold_in(jax.random.fold_in(rng, 6), position), (shards_of,), jnp.float32, smallest / len(shards), largest / len(shards))
        gain = gain * jnp.repeat(jnp.exp(heights), dims[position] // shards_of).reshape((-1,) + (1,) * (len(dims) - 1 - position))
    return gain


def scatter_about(stream_key, dims, width, most, split=(), kind=jnp.bfloat16):
    loudness = levels(stream_key, dims, split, -0.22, 0.18) if split else 1.0
    entries = jax.random.normal(stream_key, dims, jnp.float32) * width * loudness
    return jnp.minimum(jnp.maximum(entries, -most), most).astype(kind)


def setup_inputs(seed: int = 0) -> dict:
    arg_keys = jax.random.split(jax.random.key(seed), 12)
    initial_fields = scatter_about(arg_keys[0], (FIELDS, NX, NY, NZ), 1.0, 6.0, ((1, 8), (2, 16)), jnp.float32)
    velocity = jnp.clip(jax.random.uniform(arg_keys[1], (3, NX, NY, NZ), jnp.float32, -0.16, 0.16) * levels(arg_keys[1], (3, NX, NY, NZ), ((1, 8), (2, 16)), -0.4, 0.0), -0.16, 0.16)
    diffusivity = jnp.clip(0.08 + 0.08 * jax.random.uniform(arg_keys[2], (NX, NY, NZ), jnp.float32) ** levels(arg_keys[2], (NX, NY, NZ), ((0, 8), (1, 16)), -0.2, 0.2), 0.08, 0.16)
    patch_anchor = place_ends(jax.random.randint(arg_keys[3], (N_GX, N_GY, PATCHES), 0, NY - PY + 1), jax.random.fold_in(arg_keys[3], 1), 0, NY - PY).astype(jnp.int32)
    patch_count = draw_patch_count(jax.random.fold_in(arg_keys[11], 71), 0)
    weight_one = scatter_about(arg_keys[5], (CHANNELS, FIELDS, 3, 3, 3), (27 * FIELDS) ** -0.5, 0.5, (), jnp.float32)
    bias_one = scatter_about(arg_keys[6], (CHANNELS,), 0.5, 3.0, (), jnp.float32)
    weight_two = scatter_about(arg_keys[7], (CHANNELS, CHANNELS, 3, 3, 3), (27 * CHANNELS) ** -0.5, 0.21875, (), jnp.float32)
    bias_two = scatter_about(arg_keys[8], (CHANNELS,), 0.5, 3.0, (), jnp.float32)
    weight_three = scatter_about(arg_keys[9], (FIELDS, CHANNELS, 3, 3, 3), (27 * CHANNELS) ** -0.5, 0.21875, (), jnp.float32)
    bias_three = scatter_about(arg_keys[10], (FIELDS,), 0.5, 3.0, (), jnp.float32)
    return {"initial_fields": initial_fields, "velocity": velocity, "diffusivity": diffusivity, "patch_anchor": patch_anchor, "patch_count": patch_count, "weight_one": weight_one, "bias_one": bias_one, "weight_two": weight_two, "bias_two": bias_two, "weight_three": weight_three, "bias_three": bias_three}


def transport(extended, velocity, diffusivity):
    padded = jnp.pad(extended, ((0, 0), (0, 0), (0, 0), (1, 1)))
    middle = padded[:, 1:-1, 1:-1, 1:-1]
    x_plus = padded[:, 2:, 1:-1, 1:-1]
    x_minus = padded[:, :-2, 1:-1, 1:-1]
    y_plus = padded[:, 1:-1, 2:, 1:-1]
    y_minus = padded[:, 1:-1, :-2, 1:-1]
    z_plus = padded[:, 1:-1, 1:-1, 2:]
    z_minus = padded[:, 1:-1, 1:-1, :-2]
    carried = velocity[0] * (x_plus - x_minus) + velocity[1] * (y_plus - y_minus) + velocity[2] * (z_plus - z_minus)
    spread = x_plus + x_minus + y_plus + y_minus + z_plus + z_minus - 6.0 * middle
    return middle - 0.5 * carried + diffusivity * spread

def convolve(inputs, kernel):
    return lax.conv_general_dilated(inputs, kernel.astype(jnp.bfloat16), (1, 1, 1), 'SAME', dimension_numbers=('NCDHW', 'OIDHW', 'NCDHW'), preferred_element_type=jnp.float32)

def patch_loss(params, inputs, delta, live):
    weight_one, bias_one, weight_two, bias_two, weight_three, bias_three = params
    hidden_one = jax.nn.silu(convolve(inputs, weight_one) + bias_one[None, :, None, None, None]).astype(jnp.bfloat16)
    hidden_two = jax.nn.silu(convolve(hidden_one, weight_two) + bias_two[None, :, None, None, None]).astype(jnp.bfloat16)
    predicted = convolve(hidden_two, weight_three) + bias_three[None, :, None, None, None]
    error = predicted - delta
    cells = delta.shape[1] * delta.shape[2] * delta.shape[3] * delta.shape[4]
    return jnp.sum(live[:, None, None, None, None] * error * error) / cells

def reference(initial_fields, velocity, diffusivity, patch_anchor, patch_count, weight_one, bias_one, weight_two, bias_two, weight_three, bias_three):
    fields = initial_fields
    for step in range(STEPS):
        fields = transport(jnp.pad(fields, ((0, 0), (1, 1), (1, 1), (0, 0))), velocity, diffusivity)
    final_fields = fields
    params = (weight_one, bias_one, weight_two, bias_two, weight_three, bias_three)
    zero = jnp.zeros((), jnp.int32)

    def visit(carry, index):
        row = index // N_GY
        col = index % N_GY
        starts = (zero, (row * CX).astype(jnp.int32), zero, (col * SLAB_Z).astype(jnp.int32))
        first = lax.dynamic_slice(initial_fields, starts, (FIELDS, CX, NY, SLAB_Z))
        last = lax.dynamic_slice(final_fields, starts, (FIELDS, CX, NY, SLAB_Z))
        anchors = patch_anchor[row, col].astype(jnp.int32)
        count = patch_count[row, col]
        first_patches = jax.vmap(lambda o: lax.dynamic_slice_in_dim(first, o, PY, 2))(anchors)
        last_patches = jax.vmap(lambda o: lax.dynamic_slice_in_dim(last, o, PY, 2))(anchors)
        delta = last_patches - first_patches
        live = (jnp.arange(PATCHES, dtype=jnp.int32) < count).astype(jnp.float32)
        value, pullback = jax.vjp(lambda p: patch_loss(p, first_patches.astype(jnp.bfloat16), delta, live), params)
        grads = pullback(jnp.ones((), jnp.float32))[0]
        sums = tuple((c + g for c, g in zip(carry[0], grads)))
        return ((sums, carry[1] + value, carry[2] + count.astype(jnp.float32)), None)
    start = (tuple((jnp.zeros_like(p) for p in params)), jnp.zeros((), jnp.float32), jnp.zeros((), jnp.float32))
    result, unused = lax.scan(visit, start, jnp.arange(N_GX * N_GY, dtype=jnp.int32))
    grads, loss_sum, total = result
    g = tuple((x / total for x in grads))
    return (final_fields, g[0], g[1], g[2], g[3], g[4], g[5], loss_sum / total)
```

```python
import jax
import jax.numpy as jnp
from jax import lax
from jax.experimental import pallas as pl
from jax.experimental.pallas import tpu as pltpu
from jax.sharding import PartitionSpec as P

STEPS = 3
F = 5
C = 32
X = 4
PY = 8
Z = 128
ROWS = 24
TAPS = 9
CELLS = 20480.0
BF = jnp.bfloat16
F32 = jnp.float32
VMEM = pl.BlockSpec(memory_space=pltpu.VMEM)
SMEM = pl.BlockSpec(memory_space=pltpu.SMEM)
LIMIT = 48 * 1024 * 1024


def call(kernel, outs, scratch=(), flops=0, nbytes=0, ins=()):
    return pl.pallas_call(
        kernel,
        out_shape=[jax.ShapeDtypeStruct(s, d) for s, d in outs],
        in_specs=list(ins),
        out_specs=[VMEM] * len(outs),
        scratch_shapes=list(scratch),
        compiler_params=pltpu.CompilerParams(vmem_limit_bytes=LIMIT),
        cost_estimate=pl.CostEstimate(flops=flops, bytes_accessed=nbytes, transcendentals=0),
    )


def pack_slabs(get, out_ref):
    for row in range(F * X):
        cells = get(row)
        for y in range(4):
            for j in range(16):
                out_ref[j, y // 2, pl.ds((y % 2) * F * X + row, 1), :] = cells[y : y + 1, j * Z : (j + 1) * Z]


def write_edges(get, odd_x, odd_y, xa_ref, xb_ref, ya_ref, yb_ref):
    for f in range(F):
        head, tail = get(f * X), get(f * X + X - 1)
        xa_ref[f] = jnp.where(odd_x, head, tail)
        xb_ref[f] = jnp.where(odd_x, tail, head)
    for row in range(F * X):
        cells = get(row)
        head, tail = cells[0:1], cells[3:4]
        ya_ref[pl.ds(row, 1), :] = jnp.where(odd_y, head, tail)
        yb_ref[pl.ds(row, 1), :] = jnp.where(odd_y, tail, head)


def start_kernel(place, u_ref, slabs_ref, xa_ref, xb_ref, ya_ref, yb_ref):
    get = lambda row: u_ref[row]
    write_edges(get, place[0] % 2 == 1, place[1] % 2 == 1, xa_ref, xb_ref, ya_ref, yb_ref)
    pack_slabs(get, slabs_ref)


def step_kernel(last, place, u_ref, rxa, rxb, rya, ryb, vel_ref, dif_ref, new_ref, *outs):
    gx, gy = place[0], place[1]
    odd_x, odd_y = gx % 2 == 1, gy % 2 == 1
    lane = lax.broadcasted_iota(jnp.int32, (4, 2048), 1)
    not_first, not_last = lane > 0, lane < 2047
    for x in range(X):
        v0, v1, v2, dif = vel_ref[x], vel_ref[X + x], vel_ref[2 * X + x], dif_ref[x]
        for f in range(F):
            row = f * X + x
            middle = u_ref[row]
            if x < X - 1:
                x_plus = u_ref[row + 1]
            else:
                x_plus = jnp.where(odd_x, rxb[f], rxa[f])
                x_plus = jnp.where(gx == 7, 0.0, x_plus)
            if x > 0:
                x_minus = u_ref[row - 1]
            else:
                x_minus = jnp.where(odd_x, rxa[f], rxb[f])
                x_minus = jnp.where(gx == 0, 0.0, x_minus)
            a, b = rya[pl.ds(row, 1), :], ryb[pl.ds(row, 1), :]
            above = jnp.where(gy == 15, 0.0, jnp.where(odd_y, b, a))
            below = jnp.where(gy == 0, 0.0, jnp.where(odd_y, a, b))
            y_plus = jnp.concatenate([middle[1:4], above], axis=0)
            y_minus = jnp.concatenate([below, middle[0:3]], axis=0)
            z_plus = jnp.where(not_last, pltpu.roll(middle, 2047, 1), 0.0)
            z_minus = jnp.where(not_first, pltpu.roll(middle, 1, 1), 0.0)
            carried = v0 * (x_plus - x_minus) + v1 * (y_plus - y_minus) + v2 * (z_plus - z_minus)
            spread = x_plus + x_minus + y_plus + y_minus + z_plus + z_minus - 6.0 * middle
            new_ref[row] = middle - 0.5 * carried + dif * spread
    get = lambda row: new_ref[row]
    if last:
        pack_slabs(get, outs[0])
    else:
        write_edges(get, odd_x, odd_y, *outs)


EDGES = [((F, X, 2048), F32)] * 2 + [((F * X, 2048), F32)] * 2
SLABS = ((16, 2, 2 * F * X, Z), F32)


def exchange(edges):
    def pairs(n, second):
        partner = lambda i: (i ^ 1) if not second else ((i + 1) if i % 2 else (i - 1)) % n
        return [(i, partner(i)) for i in range(n)]

    xa, xb, ya, yb = edges
    return (
        lax.ppermute(xa, "gx", pairs(8, False)),
        lax.ppermute(xb, "gx", pairs(8, True)),
        lax.ppermute(ya, "gy", pairs(16, False)),
        lax.ppermute(yb, "gy", pairs(16, True)),
    )


def patch_rows(slabs_ref, anchor, out_ref):
    out_ref[...] = jnp.zeros_like(out_ref)
    for k in range(PY):
        y = anchor + k
        both = slabs_ref[y // 2]
        rows = jnp.where(y % 2 == 1, both[F * X :], both[: F * X])
        out_ref[0 : F * X, k * Z : (k + 1) * Z] = rows


def z_shifted(cells, dz, lane):
    if dz == 0:
        return cells
    moved = pltpu.roll(cells, (-dz) % Z, 1)
    return jnp.where(lane == (Z - 1 if dz > 0 else 0), 0.0, moved)


def fill_taps(cells_ref, out_ref, sign):
    rows = cells_ref.shape[0]
    lane = lax.broadcasted_iota(jnp.int32, (rows, Z), 1)
    zero = jnp.zeros((rows, Z), F32)
    shifted = [[z_shifted(cells_ref[:, k * Z : (k + 1) * Z], sign * (dz - 1), lane) for dz in range(3)] for k in range(PY)]
    for k in range(PY):
        parts = []
        for dy in range(3):
            at = k + sign * (dy - 1)
            for dz in range(3):
                parts.append(shifted[at][dz] if 0 <= at < PY else zero)
        out_ref[:, k * Z : (k + 1) * Z] = jnp.concatenate(parts, axis=0).astype(BF)


def fill_z(cells, k, out_ref, sign):
    lane = lax.broadcasted_iota(jnp.int32, cells.shape, 1)
    for dz in range(3):
        moved = z_shifted(cells, sign * (dz - 1), lane)
        out_ref[dz * 128 : (dz + 1) * 128, (k + 1) * Z : (k + 2) * Z] = moved.astype(BF)


def clear_ends(ref):
    ref[:, 0:Z] = jnp.zeros((ref.shape[0], Z), ref.dtype)
    ref[:, (PY + 1) * Z :] = jnp.zeros((ref.shape[0], Z), ref.dtype)


def dot(a, b):
    return jnp.dot(a, b, preferred_element_type=F32)


def dot_t(a, b):
    return lax.dot_general(a, b, (((1,), (1,)), ((), ())), preferred_element_type=F32)


def activate(y):
    sig = 1.0 / (1.0 + jnp.exp(-y))
    return y * sig, sig * (1.0 + y * (1.0 - sig))


def bands_kernel(w2_ref, fwd_ref, bwd_ref):
    zero = jnp.zeros((C, C), F32)
    for dy in range(3):
        for dz in range(3):
            rows = []
            for xo in range(X):
                parts = []
                for xi in range(X):
                    dx = xi - xo + 1
                    parts.append(w2_ref[dx * 9 + dy * 3 + dz] if 0 <= dx < 3 else zero)
                rows.append(jnp.concatenate(parts, axis=1))
            block = jnp.concatenate(rows, axis=0)
            fwd_ref[dy, :, dz * 128 : (dz + 1) * 128] = block.astype(BF)
            bwd_ref[dy, :, dz * 128 : (dz + 1) * 128] = block.T.astype(BF)


def forward_kernel(
    anchors, slabs_ref, w1_ref, w2_ref, w3_ref, b1_ref, b2_ref, b3_ref,
    first_ref, taps_ref, a1_ref, d1_ref, a2_ref, d2_ref, pred_ref,
):
    for p in range(2):
        patch_rows(slabs_ref, anchors[p], first_ref.at[p])
        fill_taps(first_ref.at[p], taps_ref.at[p], 1)
        y1 = dot(w1_ref[...], taps_ref[p])
        act, slope = activate(y1 + b1_ref[...])
        d1_ref[p] = slope
        clear_ends(a1_ref.at[p])
        for k in range(PY):
            fill_z(act[:, k * Z : (k + 1) * Z], k, a1_ref.at[p], 1)
        y2 = b2_ref[...] + dot(w2_ref[0], a1_ref[p, :, 0 : PY * Z])
        for dy in range(1, 3):
            y2 = y2 + dot(w2_ref[dy], a1_ref[p, :, dy * Z : (dy + PY) * Z])
        act, slope = activate(y2)
        d2_ref[p] = slope
        a2_ref[p] = act.astype(BF)
        terms = dot(w3_ref[...], a2_ref[p])
        lane = lax.broadcasted_iota(jnp.int32, (ROWS, Z), 1)
        for k in range(PY):
            out = b3_ref[...] + jnp.zeros((ROWS, Z), F32)
            for dz in range(3):
                part = None
                for dy in range(3):
                    at = k + dy - 1
                    if 0 <= at < PY:
                        t = (dy * 3 + dz) * ROWS
                        term = terms[t : t + ROWS, at * Z : (at + 1) * Z]
                        part = term if part is None else part + term
                out = out + z_shifted(part, dz - 1, lane)
            pred_ref[p, :, k * Z : (k + 1) * Z] = out


def band_sum(full):
    lane = lax.broadcasted_iota(jnp.int32, (C, 256), 1)
    total = None
    for x in range(X):
        block = full[x * C : (x + 1) * C]
        block = jnp.concatenate([block, jnp.zeros((C, 256 - TAPS * ROWS), F32)], axis=1)
        moved = pltpu.roll(block, (1 - x) % 256, 1)
        e = lane % 4
        ok = (e < 3) & (x + e - 1 >= 0) & (x + e - 1 < X) & (lane < TAPS * ROWS)
        moved = jnp.where(ok, moved, 0.0)
        total = moved if total is None else total + moved
    out = None
    for f in range(F):
        part = jnp.where((lane % ROWS) // 4 == f, total, 0.0)
        part = pltpu.roll(part, (256 - f) % 256, 1)
        out = part if out is None else out + part
    return out


def backward_kernel(
    place, anchors, count, slabs_ref, first_ref, taps_ref, a1_ref, d1_ref, a2_ref, d2_ref, pred_ref, w2_ref, w3_ref,
    keep_ref, send_ref,
    last_ref, err_ref, g_ref, b_ref, grads_ref,
):
    db1 = jnp.zeros((128, 1), F32)
    db2 = jnp.zeros((128, 1), F32)
    db3 = jnp.zeros((ROWS, 1), F32)
    loss = jnp.zeros((ROWS, 1), F32)
    dw1 = jnp.zeros((128, TAPS * ROWS), F32)
    dw3 = jnp.zeros((128, TAPS * ROWS), F32)
    dw2 = [jnp.zeros((128, 384), F32) for _ in range(3)]
    clear_ends(b_ref)
    for p in range(2):
        live = jnp.where(p < count[0], 1.0, 0.0).astype(F32)
        patch_rows(slabs_ref, anchors[p], last_ref)
        err = pred_ref[p] - (last_ref[...] - first_ref[p])
        loss = loss + live * jnp.sum(err * err, axis=1, keepdims=True)
        err = err * (live * (2.0 / CELLS))
        err_ref[...] = err
        db3 = db3 + jnp.sum(err, axis=1, keepdims=True)
        fill_taps(err_ref, g_ref, -1)
        da2 = dot(w3_ref[...], g_ref[...])
        dw3 = dw3 + dot_t(a2_ref[p], g_ref[...])
        dy2 = da2 * d2_ref[p]
        db2 = db2 + jnp.sum(dy2, axis=1, keepdims=True)
        for k in range(PY):
            fill_z(dy2[:, k * Z : (k + 1) * Z], k, b_ref, -1)
        middle = b_ref[128:256, Z : (PY + 1) * Z]
        da1 = None
        for dy in range(3):
            dw2[dy] = dw2[dy] + dot_t(middle, a1_ref[p, :, dy * Z : (dy + PY) * Z])
            term = dot(w2_ref[dy], b_ref[:, (2 - dy) * Z : (2 - dy + PY) * Z])
            da1 = term if da1 is None else da1 + term
        dy1 = da1 * d1_ref[p]
        db1 = db1 + jnp.sum(dy1, axis=1, keepdims=True)
        dw1 = dw1 + dot_t(dy1.astype(BF), taps_ref[p])

    lane = lax.broadcasted_iota(jnp.int32, (C, 128), 1)
    small1, small3 = band_sum(dw1), band_sum(dw3)
    fold = lambda v: v[0:C] + v[C : 2 * C] + v[2 * C : 3 * C] + v[3 * C : 4 * C]
    grow = lambda v: jnp.concatenate([v, jnp.zeros((C - ROWS, 1), F32)], axis=0)
    extras = {0: (fold(db1), fold(db2)), 1: (grow(db3), grow(loss)), 2: (jnp.full((C, 1), 1.0, F32) * count[0].astype(F32), None)}
    for t in range(TAPS):
        dy, dz = t // 3, t % 3
        total = jnp.zeros((C, 128), F32)
        for xo in range(X):
            block = dw2[dy][xo * C : (xo + 1) * C, dz * 128 : (dz + 1) * 128]
            moved = pltpu.roll(block, ((1 - xo) * C) % 128, 1)
            dx = lane // C
            ok = (dx < 3) & (xo + dx - 1 >= 0) & (xo + dx - 1 < X)
            total = total + jnp.where(ok, moved, 0.0)
        one = pltpu.roll(small1, (96 - ROWS * t) % 256, 1)[:, 0:128]
        three = pltpu.roll(small3, (111 - ROWS * t) % 256, 1)[:, 0:128]
        total = jnp.where((lane >= 96) & (lane < 111), one, total)
        total = jnp.where((lane >= 111) & (lane < 126), three, total)
        if t in extras:
            a, b = extras[t]
            total = jnp.where(lane == 126, a, total)
            if b is not None:
                total = jnp.where(lane == 127, b, total)
        grads_ref[t * C : (t + 1) * C] = total
    core = place[1] % 2
    low, high = grads_ref[0:144], grads_ref[144:288]
    keep_ref[...] = jnp.where(core == 0, low, high)
    send_ref[...] = jnp.where(core == 0, high, low)


def reduce_steps():
    def near(c):
        return c ^ 1

    def far(c):
        return 3 - c

    orders = (("x", "y", "z"), ("y", "z", "x"))
    steps = []
    for n in range(6):
        pairs = []
        for gx in range(8):
            for gy in range(16):
                at = {"x": gx // 2, "y": gy // 4, "z": (gy // 2 % 2) * 2 + gx % 2}
                core = gy % 2
                axis = orders[core][n // 2]
                at[axis] = (near, far)[n % 2](at[axis])
                to = (at["x"] * 2 + at["z"] % 2) * 16 + at["y"] * 4 + (at["z"] // 2) * 2 + core
                pairs.append((gx * 16 + gy, to))
        steps.append(pairs)
    return steps


def sum_all(keep, send):
    both = ("gx", "gy")
    cores = [(i, i ^ 1) for i in range(16)]
    mine = keep + lax.ppermute(send, "gy", cores)
    for pairs in reduce_steps():
        mine = mine + lax.ppermute(mine, both, pairs)
    return mine, lax.ppermute(mine, "gy", cores)


def banded(w, flip):
    bands = []
    for x in range(X):
        if flip:
            w_ = w[:, ::-1]
        else:
            w_ = w
        padded = jnp.pad(w_, ((0, 0), (x, X - 1 - x), (0, 0), (0, 0), (0, 0)))
        bands.append(padded[:, 1 : X + 1])
    all_x = jnp.stack(bands, axis=4)
    rows = jnp.transpose(all_x, (2, 3, 0, 1, 4, 5)).reshape(TAPS, F * X, X * C)
    return jnp.pad(rows, ((0, 0), (0, ROWS - F * X), (0, 0))).reshape(TAPS * ROWS, X * C).astype(BF)


def on_device(
    initial_fields, velocity, diffusivity, patch_anchor, patch_count,
    weight_one, bias_one, weight_two, bias_two, weight_three, bias_three,
):
    place = jnp.stack([lax.axis_index("gx"), lax.axis_index("gy")]).astype(jnp.int32)
    u = initial_fields.reshape(F * X, 4, 2048)
    vel = velocity.reshape(3 * X, 4, 2048)
    anchors = patch_anchor.reshape(2)
    count = patch_count.reshape(1)

    slabs, *edges = call(start_kernel, [SLABS] + EDGES, ins=[SMEM, VMEM], nbytes=1_500_000)(place, u)
    first_slabs = lax.all_to_all(slabs, "gy", 0, 0, tiled=True).reshape(32, 2 * F * X, Z)

    w2 = jnp.transpose(weight_two, (2, 3, 4, 0, 1)).reshape(27, C, C)
    w2_fwd, w2_bwd = call(bands_kernel, [((3, 128, 384), BF)] * 2, ins=[VMEM], nbytes=1_000_000)(w2)
    w1_band = banded(jnp.transpose(weight_one, (1, 2, 3, 4, 0)), False)
    w3_band = banded(jnp.transpose(weight_three, (0, 2, 3, 4, 1)), True)
    b1 = jnp.tile(bias_one, X).reshape(128, 1)
    b2 = jnp.tile(bias_two, X).reshape(128, 1)
    b3 = jnp.pad(jnp.repeat(bias_three, X), (0, ROWS - F * X)).reshape(ROWS, 1)

    for step in range(STEPS):
        last = step == STEPS - 1
        outs = [((F * X, 4, 2048), F32)] + ([SLABS] if last else EDGES)
        received = exchange(edges)
        kernel = lambda *refs, last=last: step_kernel(last, *refs)
        u, *edges = call(kernel, outs, ins=[SMEM] + [VMEM] * 7, nbytes=4_000_000)(
            place, u, *received, vel, diffusivity
        )

    learned = call(
        forward_kernel,
        [
            ((2, ROWS, PY * Z), F32),
            ((2, TAPS * ROWS, PY * Z), BF),
            ((2, 384, (PY + 2) * Z), BF),
            ((2, 128, PY * Z), F32),
            ((2, 128, PY * Z), BF),
            ((2, 128, PY * Z), F32),
            ((2, ROWS, PY * Z), F32),
        ],
        ins=[SMEM] + [VMEM] * 7,
        flops=2_000_000_000,
        nbytes=8_000_000,
    )(anchors, first_slabs, w1_band.T, w2_fwd, w3_band, b1, b2, b3)

    last_slabs = lax.all_to_all(edges[0], "gy", 0, 0, tiled=True).reshape(32, 2 * F * X, Z)
    keep, send = call(
        backward_kernel,
        [((144, 128), F32)] * 2,
        scratch=[
            pltpu.VMEM((ROWS, PY * Z), F32),
            pltpu.VMEM((ROWS, PY * Z), F32),
            pltpu.VMEM((TAPS * ROWS, PY * Z), BF),
            pltpu.VMEM((384, (PY + 2) * Z), BF),
            pltpu.VMEM((288, 128), F32),
        ],
        ins=[SMEM] * 3 + [VMEM] * 10,
        flops=4_000_000_000,
        nbytes=10_000_000,
    )(place, anchors, count, last_slabs, *learned, w2_bwd, w3_band.T)

    mine, other = sum_all(keep, send)
    core = place[1] % 2
    grads = jnp.where(core == 0, jnp.concatenate([mine, other]), jnp.concatenate([other, mine]))
    grads = grads.reshape(TAPS, C, 128)
    total = grads[2, 0, 126]
    grads = grads / total
    g2 = jnp.transpose(grads[:, :, 0:96].reshape(3, 3, C, 3, C), (2, 4, 3, 0, 1))
    g1 = jnp.transpose(grads[:, :, 96:111].reshape(3, 3, C, F, 3), (2, 3, 4, 0, 1))
    g3 = jnp.transpose(grads[:, :, 111:126].reshape(3, 3, C, F, 3), (3, 2, 4, 0, 1))[:, :, ::-1]
    gb1, gb2 = grads[0, :, 126], grads[0, :, 127]
    gb3 = grads[1, 0 : F * X, 126].reshape(F, X).sum(1)
    loss = grads[1, 0 : F * X, 127].sum() / CELLS
    return u.reshape(F, X, 4, 2048), g1, gb1, g2, gb2, g3, gb3, loss


def solution(mesh):
    return jax.shard_map(
        on_device,
        mesh=mesh,
        in_specs=(
            P(None, "gx", "gy", None),
            P(None, "gx", "gy", None),
            P("gx", "gy", None),
            P("gx", "gy", None),
            P("gx", "gy"),
            P(),
            P(),
            P(),
            P(),
            P(),
            P(),
        ),
        out_specs=(P(None, "gx", "gy", None), P(), P(), P(), P(), P(), P(), P()),
        check_vma=False,
    )
```

```python
import jax
import jax.numpy as jnp
from jax import lax
from jax.experimental import pallas as pl
from jax.experimental.pallas import tpu as pltpu
from jax.sharding import PartitionSpec as P

STEPS = 3
F = 5
C = 32
X = 4
PY = 8
Z = 128
ROWS = 24
TAPS = 9
CELLS = 20480.0
BF = jnp.bfloat16
F32 = jnp.float32
VMEM = pl.BlockSpec(memory_space=pltpu.VMEM)
SMEM = pl.BlockSpec(memory_space=pltpu.SMEM)
MIB = 1024 * 1024


def call(kernel, outs, scratch=(), flops=0, nbytes=0, ins=(), mib=12):
    return pl.pallas_call(
        kernel,
        out_shape=[jax.ShapeDtypeStruct(s, d) for s, d in outs],
        in_specs=list(ins),
        out_specs=[VMEM] * len(outs),
        scratch_shapes=list(scratch),
        compiler_params=pltpu.CompilerParams(vmem_limit_bytes=mib * MIB),
        cost_estimate=pl.CostEstimate(flops=flops, bytes_accessed=nbytes, transcendentals=0),
    )


def pack_slabs(get, out_ref):
    for row in range(F * X):
        cells = get(row)
        for y in range(4):
            for j in range(16):
                out_ref[j, y // 2, pl.ds((y % 2) * F * X + row, 1), :] = cells[y : y + 1, j * Z : (j + 1) * Z]


def write_edges(get, odd_x, odd_y, xa_ref, xb_ref, ya_ref, yb_ref):
    for f in range(F):
        head, tail = get(f * X), get(f * X + X - 1)
        xa_ref[f] = jnp.where(odd_x, head, tail)
        xb_ref[f] = jnp.where(odd_x, tail, head)
    for row in range(F * X):
        cells = get(row)
        head, tail = cells[0:1], cells[3:4]
        ya_ref[pl.ds(row, 1), :] = jnp.where(odd_y, head, tail)
        yb_ref[pl.ds(row, 1), :] = jnp.where(odd_y, tail, head)


def edges_kernel(place, u_ref, xa_ref, xb_ref, ya_ref, yb_ref):
    get = lambda row: u_ref[row]
    write_edges(get, place[0] % 2 == 1, place[1] % 2 == 1, xa_ref, xb_ref, ya_ref, yb_ref)


def slabs_kernel(u_ref, slabs_ref):
    pack_slabs(lambda row: u_ref[row], slabs_ref)


def step_kernel(last, place, u_ref, rxa, rxb, rya, ryb, vel_ref, dif_ref, new_ref, *outs):
    gx, gy = place[0], place[1]
    odd_x, odd_y = gx % 2 == 1, gy % 2 == 1
    lane = lax.broadcasted_iota(jnp.int32, (4, 2048), 1)
    not_first, not_last = lane > 0, lane < 2047
    for x in range(X):
        v0, v1, v2, dif = vel_ref[x], vel_ref[X + x], vel_ref[2 * X + x], dif_ref[x]
        for f in range(F):
            row = f * X + x
            middle = u_ref[row]
            if x < X - 1:
                x_plus = u_ref[row + 1]
            else:
                x_plus = jnp.where(odd_x, rxb[f], rxa[f])
                x_plus = jnp.where(gx == 7, 0.0, x_plus)
            if x > 0:
                x_minus = u_ref[row - 1]
            else:
                x_minus = jnp.where(odd_x, rxa[f], rxb[f])
                x_minus = jnp.where(gx == 0, 0.0, x_minus)
            a, b = rya[pl.ds(row, 1), :], ryb[pl.ds(row, 1), :]
            above = jnp.where(gy == 15, 0.0, jnp.where(odd_y, b, a))
            below = jnp.where(gy == 0, 0.0, jnp.where(odd_y, a, b))
            y_plus = jnp.concatenate([middle[1:4], above], axis=0)
            y_minus = jnp.concatenate([below, middle[0:3]], axis=0)
            z_plus = jnp.where(not_last, pltpu.roll(middle, 2047, 1), 0.0)
            z_minus = jnp.where(not_first, pltpu.roll(middle, 1, 1), 0.0)
            carried = v0 * (x_plus - x_minus) + v1 * (y_plus - y_minus) + v2 * (z_plus - z_minus)
            spread = x_plus + x_minus + y_plus + y_minus + z_plus + z_minus - 6.0 * middle
            new_ref[row] = middle - 0.5 * carried + dif * spread
    get = lambda row: new_ref[row]
    if last:
        pack_slabs(get, outs[0])
    else:
        write_edges(get, odd_x, odd_y, *outs)


EDGES = [((F, X, 2048), F32)] * 2 + [((F * X, 2048), F32)] * 2
SLABS = ((16, 2, 2 * F * X, Z), F32)


def exchange(edges):
    def pairs(n, second):
        partner = lambda i: (i ^ 1) if not second else ((i + 1) if i % 2 else (i - 1)) % n
        return [(i, partner(i)) for i in range(n)]

    xa, xb, ya, yb = edges
    return (
        lax.ppermute(xa, "gx", pairs(8, False)),
        lax.ppermute(xb, "gx", pairs(8, True)),
        lax.ppermute(ya, "gy", pairs(16, False)),
        lax.ppermute(yb, "gy", pairs(16, True)),
    )


def patch_rows(slabs_ref, anchor, out_ref):
    out_ref[...] = jnp.zeros_like(out_ref)
    for k in range(PY):
        y = anchor + k
        both = slabs_ref[y // 2]
        rows = jnp.where(y % 2 == 1, both[F * X :], both[: F * X])
        out_ref[0 : F * X, k * Z : (k + 1) * Z] = rows


def z_shifted(cells, dz, lane):
    if dz == 0:
        return cells
    moved = pltpu.roll(cells, (-dz) % Z, 1)
    return jnp.where(lane == (Z - 1 if dz > 0 else 0), 0.0, moved)


def fill_taps(cells_ref, out_ref, sign):
    rows = cells_ref.shape[0]
    lane = lax.broadcasted_iota(jnp.int32, (rows, Z), 1)
    zero = jnp.zeros((rows, Z), F32)
    shifted = [[z_shifted(cells_ref[:, k * Z : (k + 1) * Z], sign * (dz - 1), lane) for dz in range(3)] for k in range(PY)]
    for k in range(PY):
        parts = []
        for dy in range(3):
            at = k + sign * (dy - 1)
            for dz in range(3):
                parts.append(shifted[at][dz] if 0 <= at < PY else zero)
        out_ref[:, k * Z : (k + 1) * Z] = jnp.concatenate(parts, axis=0).astype(BF)


def fill_z(cells, k, out_ref, sign):
    lane = lax.broadcasted_iota(jnp.int32, cells.shape, 1)
    for dz in range(3):
        moved = z_shifted(cells, sign * (dz - 1), lane)
        out_ref[dz * 128 : (dz + 1) * 128, (k + 1) * Z : (k + 2) * Z] = moved.astype(BF)


def clear_ends(ref):
    ref[:, 0:Z] = jnp.zeros((ref.shape[0], Z), ref.dtype)
    ref[:, (PY + 1) * Z :] = jnp.zeros((ref.shape[0], Z), ref.dtype)


def dot(a, b):
    return jnp.dot(a, b, preferred_element_type=F32)


def dot_t(a, b):
    return lax.dot_general(a, b, (((1,), (1,)), ((), ())), preferred_element_type=F32)


def activate(y):
    sig = 1.0 / (1.0 + jnp.exp(-y))
    return y * sig, sig * (1.0 + y * (1.0 - sig))


def bands_kernel(w2_ref, fwd_ref, bwd_ref):
    zero = jnp.zeros((C, C), F32)
    for dy in range(3):
        for dz in range(3):
            rows = []
            for xo in range(X):
                parts = []
                for xi in range(X):
                    dx = xi - xo + 1
                    parts.append(w2_ref[dx * 9 + dy * 3 + dz] if 0 <= dx < 3 else zero)
                rows.append(jnp.concatenate(parts, axis=1))
            block = jnp.concatenate(rows, axis=0)
            fwd_ref[dy, :, dz * 128 : (dz + 1) * 128] = block.astype(BF)
            bwd_ref[dy, :, dz * 128 : (dz + 1) * 128] = block.T.astype(BF)


def forward_kernel(
    anchors, slabs_ref, w1_ref, w2_ref, w3_ref, b1_ref, b2_ref, b3_ref,
    first_ref, taps_ref, a1_ref, d1_ref, a2_ref, d2_ref, pred_ref,
):
    for p in range(2):
        patch_rows(slabs_ref, anchors[p], first_ref.at[p])
        fill_taps(first_ref.at[p], taps_ref.at[p], 1)
        y1 = dot(w1_ref[...], taps_ref[p])
        act, slope = activate(y1 + b1_ref[...])
        d1_ref[p] = slope
        clear_ends(a1_ref.at[p])
        for k in range(PY):
            fill_z(act[:, k * Z : (k + 1) * Z], k, a1_ref.at[p], 1)
        y2 = b2_ref[...] + dot(w2_ref[0], a1_ref[p, :, 0 : PY * Z])
        for dy in range(1, 3):
            y2 = y2 + dot(w2_ref[dy], a1_ref[p, :, dy * Z : (dy + PY) * Z])
        act, slope = activate(y2)
        d2_ref[p] = slope
        a2_ref[p] = act.astype(BF)
        terms = dot(w3_ref[...], a2_ref[p])
        lane = lax.broadcasted_iota(jnp.int32, (ROWS, Z), 1)
        for k in range(PY):
            out = b3_ref[...] + jnp.zeros((ROWS, Z), F32)
            for dz in range(3):
                part = None
                for dy in range(3):
                    at = k + dy - 1
                    if 0 <= at < PY:
                        t = (dy * 3 + dz) * ROWS
                        term = terms[t : t + ROWS, at * Z : (at + 1) * Z]
                        part = term if part is None else part + term
                out = out + z_shifted(part, dz - 1, lane)
            pred_ref[p, :, k * Z : (k + 1) * Z] = out


def band_sum(full):
    lane = lax.broadcasted_iota(jnp.int32, (C, 256), 1)
    total = None
    for x in range(X):
        block = full[x * C : (x + 1) * C]
        block = jnp.concatenate([block, jnp.zeros((C, 256 - TAPS * ROWS), F32)], axis=1)
        moved = pltpu.roll(block, (1 - x) % 256, 1)
        e = lane % 4
        ok = (e < 3) & (x + e - 1 >= 0) & (x + e - 1 < X) & (lane < TAPS * ROWS)
        moved = jnp.where(ok, moved, 0.0)
        total = moved if total is None else total + moved
    out = None
    for f in range(F):
        part = jnp.where((lane % ROWS) // 4 == f, total, 0.0)
        part = pltpu.roll(part, (256 - f) % 256, 1)
        out = part if out is None else out + part
    return out


def backward_kernel(
    anchors, count, slabs_ref, first_ref, taps_ref, a1_ref, d1_ref, a2_ref, d2_ref, pred_ref, w2_ref, w3_ref,
    grads_ref,
    last_ref, err_ref, g_ref, b_ref,
):
    db1 = jnp.zeros((128, 1), F32)
    db2 = jnp.zeros((128, 1), F32)
    db3 = jnp.zeros((ROWS, 1), F32)
    loss = jnp.zeros((ROWS, 1), F32)
    dw1 = jnp.zeros((128, TAPS * ROWS), F32)
    dw3 = jnp.zeros((128, TAPS * ROWS), F32)
    dw2 = [jnp.zeros((128, 384), F32) for _ in range(3)]
    clear_ends(b_ref)
    for p in range(2):
        live = jnp.where(p < count[0], 1.0, 0.0).astype(F32)
        patch_rows(slabs_ref, anchors[p], last_ref)
        err = pred_ref[p] - (last_ref[...] - first_ref[p])
        loss = loss + live * jnp.sum(err * err, axis=1, keepdims=True)
        err = err * (live * (2.0 / CELLS))
        err_ref[...] = err
        db3 = db3 + jnp.sum(err, axis=1, keepdims=True)
        fill_taps(err_ref, g_ref, -1)
        da2 = dot(w3_ref[...], g_ref[...])
        dw3 = dw3 + dot_t(a2_ref[p], g_ref[...])
        dy2 = da2 * d2_ref[p]
        db2 = db2 + jnp.sum(dy2, axis=1, keepdims=True)
        for k in range(PY):
            fill_z(dy2[:, k * Z : (k + 1) * Z], k, b_ref, -1)
        middle = b_ref[128:256, Z : (PY + 1) * Z]
        da1 = None
        for dy in range(3):
            dw2[dy] = dw2[dy] + dot_t(middle, a1_ref[p, :, dy * Z : (dy + PY) * Z])
            term = dot(w2_ref[dy], b_ref[:, (2 - dy) * Z : (2 - dy + PY) * Z])
            da1 = term if da1 is None else da1 + term
        dy1 = da1 * d1_ref[p]
        db1 = db1 + jnp.sum(dy1, axis=1, keepdims=True)
        dw1 = dw1 + dot_t(dy1.astype(BF), taps_ref[p])

    lane = lax.broadcasted_iota(jnp.int32, (C, 128), 1)
    small1, small3 = band_sum(dw1), band_sum(dw3)
    fold = lambda v: v[0:C] + v[C : 2 * C] + v[2 * C : 3 * C] + v[3 * C : 4 * C]
    by_field = [jnp.sum(db3[f * X : (f + 1) * X], axis=0, keepdims=True) for f in range(F)]
    db3 = jnp.concatenate(by_field + [jnp.zeros((C - F, 1), F32)], axis=0)
    loss = jnp.sum(loss, axis=0, keepdims=True) * (1.0 / CELLS)
    extras = {0: (fold(db1), fold(db2)), 1: (db3, loss), 2: (jnp.full((C, 1), 1.0, F32) * count[0].astype(F32), None)}
    for t in range(TAPS):
        dy, dz = t // 3, t % 3
        total = jnp.zeros((C, 128), F32)
        for xo in range(X):
            block = dw2[dy][xo * C : (xo + 1) * C, dz * 128 : (dz + 1) * 128]
            moved = pltpu.roll(block, ((1 - xo) * C) % 128, 1)
            dx = lane // C
            ok = (dx < 3) & (xo + dx - 1 >= 0) & (xo + dx - 1 < X)
            total = total + jnp.where(ok, moved, 0.0)
        one = pltpu.roll(small1, (96 - ROWS * t) % 256, 1)[:, 0:128]
        three = pltpu.roll(small3, (111 - ROWS * t) % 256, 1)[:, 0:128]
        total = jnp.where((lane >= 96) & (lane < 111), one, total)
        total = jnp.where((lane >= 111) & (lane < 126), three, total)
        if t in extras:
            a, b = extras[t]
            total = jnp.where(lane == 126, a, total)
            if b is not None:
                total = jnp.where(lane == 127, b, total)
        grads_ref[t * C : (t + 1) * C] = total


def finish_kernel(place, mine_ref, other_ref, g1_ref, gb1_ref, g2_ref, gb2_ref, g3_ref, gb3_ref, loss_ref):
    first = place[1] % 2 == 0
    rows = lambda t: jnp.where(first, other_ref[t * C : (t + 1) * C], mine_ref[t * C : (t + 1) * C])
    total = rows(2)[0:1, 126:127]
    for t in range(TAPS):
        dy, dz = t // 3, t % 3
        block = rows(t) / total
        for dx in range(3):
            g2_ref[dx * TAPS + t] = block[:, dx * C : (dx + 1) * C]
        turned = block.T
        for f in range(F):
            for dx in range(3):
                to = (f * 3 + dx) * 3 + dy
                at = 96 + f * 3 + dx
                g1_ref[to, dz : dz + 1, :] = turned[at : at + 1]
                at = 111 + f * 3 + 2 - dx
                g3_ref[to, dz : dz + 1, :] = turned[at : at + 1]
        if t == 0:
            gb1_ref[...] = turned[126:127]
            gb2_ref[...] = turned[127:128]
        if t == 1:
            gb3_ref[...] = turned[126:127, 0:F]
            loss_ref[...] = turned[127:128, 0:1]


def reduce_steps():
    def near(c):
        return c ^ 1

    def far(c):
        return 3 - c

    steps = []
    for n in range(6):
        pairs = []
        for gx in range(8):
            for gy in range(1, 16, 2):
                at = {"x": gx // 2, "y": gy // 4, "z": (gy // 2 % 2) * 2 + gx % 2}
                axis = "zyx"[n // 2]
                at[axis] = (near, far)[n % 2](at[axis])
                to = (at["x"] * 2 + at["z"] % 2) * 16 + at["y"] * 4 + (at["z"] // 2) * 2 + 1
                pairs.append((gx * 16 + gy, to))
        steps.append(pairs)
    return steps


def sum_all(mine):
    mine = mine + lax.ppermute(mine, "gy", [(i, i + 1) for i in range(0, 16, 2)])
    for pairs in reduce_steps():
        mine = mine + lax.ppermute(mine, ("gx", "gy"), pairs)
    return mine, lax.ppermute(mine, "gy", [(i + 1, i) for i in range(0, 16, 2)])


def banded(w, flip):
    bands = []
    for x in range(X):
        if flip:
            w_ = w[:, ::-1]
        else:
            w_ = w
        padded = jnp.pad(w_, ((0, 0), (x, X - 1 - x), (0, 0), (0, 0), (0, 0)))
        bands.append(padded[:, 1 : X + 1])
    all_x = jnp.stack(bands, axis=4)
    rows = jnp.transpose(all_x, (2, 3, 0, 1, 4, 5)).reshape(TAPS, F * X, X * C)
    return jnp.pad(rows, ((0, 0), (0, ROWS - F * X), (0, 0))).reshape(TAPS * ROWS, X * C).astype(BF)


def on_device(
    initial_fields, velocity, diffusivity, patch_anchor, patch_count,
    weight_one, bias_one, weight_two, bias_two, weight_three, bias_three,
):
    place = jnp.stack([lax.axis_index("gx"), lax.axis_index("gy")]).astype(jnp.int32)
    u = initial_fields.reshape(F * X, 4, 2048)
    vel = velocity.reshape(3 * X, 4, 2048)
    anchors = patch_anchor.reshape(2)
    count = patch_count.reshape(1)

    edges = call(edges_kernel, EDGES, ins=[SMEM, VMEM], nbytes=1_000_000)(place, u)
    (slabs,) = call(slabs_kernel, [SLABS], ins=[VMEM], nbytes=1_500_000)(u)
    first_slabs = lax.all_to_all(slabs, "gy", 0, 0, tiled=True).reshape(32, 2 * F * X, Z)

    w2 = jnp.transpose(weight_two, (2, 3, 4, 0, 1)).reshape(27, C, C)
    w2_fwd, w2_bwd = call(bands_kernel, [((3, 128, 384), BF)] * 2, ins=[VMEM], nbytes=1_000_000)(w2)
    w1_band = banded(jnp.transpose(weight_one, (1, 2, 3, 4, 0)), False)
    w3_band = banded(jnp.transpose(weight_three, (0, 2, 3, 4, 1)), True)
    b1 = jnp.tile(bias_one, X).reshape(128, 1)
    b2 = jnp.tile(bias_two, X).reshape(128, 1)
    b3 = jnp.pad(jnp.repeat(bias_three, X), (0, ROWS - F * X)).reshape(ROWS, 1)

    for step in range(STEPS):
        last = step == STEPS - 1
        outs = [((F * X, 4, 2048), F32)] + ([SLABS] if last else EDGES)
        received = exchange(edges)
        kernel = lambda *refs, last=last: step_kernel(last, *refs)
        u, *edges = call(kernel, outs, ins=[SMEM] + [VMEM] * 7, nbytes=4_000_000)(
            place, u, *received, vel, diffusivity
        )

    learned = call(
        forward_kernel,
        [
            ((2, ROWS, PY * Z), F32),
            ((2, TAPS * ROWS, PY * Z), BF),
            ((2, 384, (PY + 2) * Z), BF),
            ((2, 128, PY * Z), F32),
            ((2, 128, PY * Z), BF),
            ((2, 128, PY * Z), F32),
            ((2, ROWS, PY * Z), F32),
        ],
        ins=[SMEM] + [VMEM] * 7,
        flops=2_000_000_000,
        nbytes=8_000_000,
        mib=24,
    )(anchors, first_slabs, w1_band.T, w2_fwd, w3_band, b1, b2, b3)

    last_slabs = lax.all_to_all(edges[0], "gy", 0, 0, tiled=True).reshape(32, 2 * F * X, Z)
    (grads,) = call(
        backward_kernel,
        [((TAPS * C, 128), F32)],
        scratch=[
            pltpu.VMEM((ROWS, PY * Z), F32),
            pltpu.VMEM((ROWS, PY * Z), F32),
            pltpu.VMEM((TAPS * ROWS, PY * Z), BF),
            pltpu.VMEM((384, (PY + 2) * Z), BF),
        ],
        ins=[SMEM] * 2 + [VMEM] * 10,
        flops=4_000_000_000,
        nbytes=10_000_000,
        mib=24,
    )(anchors, count, last_slabs, *learned, w2_bwd, w3_band.T)

    mine, other = sum_all(grads)
    g1, gb1, g2, gb2, g3, gb3, loss = call(
        finish_kernel,
        [((45, 3, C), F32), ((1, C), F32), ((27, C, C), F32), ((1, C), F32), ((45, 3, C), F32), ((1, F), F32), ((1, 1), F32)],
        ins=[SMEM, VMEM, VMEM],
        nbytes=1_000_000,
    )(place, mine, other)
    g1 = jnp.transpose(g1.reshape(F, 3, 3, 3, C), (4, 0, 1, 2, 3))
    g2 = jnp.transpose(g2.reshape(3, 3, 3, C, C), (3, 4, 0, 1, 2))
    g3 = jnp.transpose(g3.reshape(F, 3, 3, 3, C), (0, 4, 1, 2, 3))
    gb1, gb2, gb3, loss = gb1.reshape(C), gb2.reshape(C), gb3.reshape(F), loss.reshape(())
    return u.reshape(F, X, 4, 2048), g1, gb1, g2, gb2, g3, gb3, loss


def solution(mesh):
    return jax.shard_map(
        on_device,
        mesh=mesh,
        in_specs=(
            P(None, "gx", "gy", None),
            P(None, "gx", "gy", None),
            P("gx", "gy", None),
            P("gx", "gy", None),
            P("gx", "gy"),
            P(),
            P(),
            P(),
            P(),
            P(),
            P(),
        ),
        out_specs=(P(None, "gx", "gy", None), P(), P(), P(), P(), P(), P(), P()),
        check_vma=False,
    )
```

```python
import jax
import jax.numpy as jnp
from jax import lax
from jax.experimental import pallas as pl
from jax.experimental.pallas import tpu as pltpu
from jax.sharding import PartitionSpec as P

STEPS = 3
F = 5
C = 32
X = 4
PY = 8
Z = 128
ROWS = 24
HALF = 144
TAPS = 9
TALL = 224
CELLS = 20480.0
BF = jnp.bfloat16
F32 = jnp.float32
VMEM = pl.BlockSpec(memory_space=pltpu.VMEM)
SMEM = pl.BlockSpec(memory_space=pltpu.SMEM)
HBM = pl.BlockSpec(memory_space=pltpu.HBM)
MIB = 1024 * 1024


def call(kernel, outs, scratch=(), flops=0, nbytes=0, ins=(), mib=12, out_space=None):
    return pl.pallas_call(
        kernel,
        out_shape=[jax.ShapeDtypeStruct(s, d) for s, d in outs],
        in_specs=list(ins),
        out_specs=[out_space or VMEM] * len(outs),
        scratch_shapes=list(scratch),
        compiler_params=pltpu.CompilerParams(vmem_limit_bytes=mib * MIB),
        cost_estimate=pl.CostEstimate(flops=flops, bytes_accessed=nbytes, transcendentals=0),
    )


def pack_slabs(get, out_ref):
    for row in range(F * X):
        cells = get(row)
        for y in range(4):
            for j in range(16):
                out_ref[j, y // 2, pl.ds((y % 2) * F * X + row, 1), :] = cells[y : y + 1, j * Z : (j + 1) * Z]


def write_edges(get, odd_x, odd_y, xa_ref, xb_ref, ya_ref, yb_ref):
    for f in range(F):
        head, tail = get(f * X), get(f * X + X - 1)
        xa_ref[f] = jnp.where(odd_x, head, tail)
        xb_ref[f] = jnp.where(odd_x, tail, head)
    for row in range(F * X):
        cells = get(row)
        head, tail = cells[0:1], cells[3:4]
        ya_ref[pl.ds(row, 1), :] = jnp.where(odd_y, head, tail)
        yb_ref[pl.ds(row, 1), :] = jnp.where(odd_y, tail, head)


def edges_kernel(place, u_ref, xa_ref, xb_ref, ya_ref, yb_ref):
    get = lambda row: u_ref[row]
    write_edges(get, place[0] % 2 == 1, place[1] % 2 == 1, xa_ref, xb_ref, ya_ref, yb_ref)


def slabs_kernel(u_ref, slabs_ref):
    pack_slabs(lambda row: u_ref[row], slabs_ref)


def inner_kernel(u_ref, vel_ref, dif_ref, part_ref):
    lane = lax.broadcasted_iota(jnp.int32, (4, 2048), 1)
    not_first, not_last = lane > 0, lane < 2047
    zero_row = jnp.zeros((1, 2048), F32)
    for x in range(X):
        v0, v1, v2, dif = vel_ref[x], vel_ref[X + x], vel_ref[2 * X + x], dif_ref[x]
        for f in range(F):
            row = f * X + x
            middle = u_ref[row]
            x_plus = u_ref[row + 1] if x < X - 1 else 0.0
            x_minus = u_ref[row - 1] if x > 0 else 0.0
            y_plus = jnp.concatenate([middle[1:4], zero_row], axis=0)
            y_minus = jnp.concatenate([zero_row, middle[0:3]], axis=0)
            z_plus = jnp.where(not_last, pltpu.roll(middle, 2047, 1), 0.0)
            z_minus = jnp.where(not_first, pltpu.roll(middle, 1, 1), 0.0)
            carried = v0 * (x_plus - x_minus) + v1 * (y_plus - y_minus) + v2 * (z_plus - z_minus)
            spread = x_plus + x_minus + y_plus + y_minus + z_plus + z_minus - 6.0 * middle
            part_ref[row] = middle - 0.5 * carried + dif * spread


def outer_kernel(last, place, part_ref, rxa, rxb, rya, ryb, vel_ref, dif_ref, new_ref, *outs):
    gx, gy = place[0], place[1]
    odd_x, odd_y = gx % 2 == 1, gy % 2 == 1
    y_at = lax.broadcasted_iota(jnp.int32, (4, 2048), 0)
    up_on = (y_at == 3) & (gy != 15)
    down_on = (y_at == 0) & (gy != 0)
    for x in range(X):
        v0, v1, dif = vel_ref[x], vel_ref[X + x], dif_ref[x]
        up = jnp.where(up_on, dif - 0.5 * v1, 0.0)
        down = jnp.where(down_on, dif + 0.5 * v1, 0.0)
        side = None
        if x == X - 1:
            side = jnp.where(gx == 7, 0.0, dif - 0.5 * v0)
        if x == 0:
            side = jnp.where(gx == 0, 0.0, dif + 0.5 * v0)
        from_a = jnp.where(odd_y, down, up)
        from_b = jnp.where(odd_y, up, down)
        for f in range(F):
            row = f * X + x
            new = part_ref[row] + rya[pl.ds(row, 1), :] * from_a + ryb[pl.ds(row, 1), :] * from_b
            if x == X - 1:
                new = new + jnp.where(odd_x, rxb[f], rxa[f]) * side
            if x == 0:
                new = new + jnp.where(odd_x, rxa[f], rxb[f]) * side
            new_ref[row] = new
    get = lambda row: new_ref[row]
    if last:
        pack_slabs(get, outs[0])
    else:
        write_edges(get, odd_x, odd_y, *outs)


EDGES = [((F, X, 2048), F32)] * 2 + [((F * X, 2048), F32)] * 2
SLABS = ((16, 2, 2 * F * X, Z), F32)


def exchange(edges):
    def pairs(n, second):
        partner = lambda i: (i ^ 1) if not second else ((i + 1) if i % 2 else (i - 1)) % n
        return [(i, partner(i)) for i in range(n)]

    xa, xb, ya, yb = edges
    return (
        lax.ppermute(xa, "gx", pairs(8, False)),
        lax.ppermute(xb, "gx", pairs(8, True)),
        lax.ppermute(ya, "gy", pairs(16, False)),
        lax.ppermute(yb, "gy", pairs(16, True)),
    )


def patch_rows(slabs_ref, anchor, out_ref):
    out_ref[...] = jnp.zeros_like(out_ref)
    for k in range(PY):
        y = anchor + k
        both = slabs_ref[y // 2]
        rows = jnp.where(y % 2 == 1, both[F * X :], both[: F * X])
        out_ref[0 : F * X, k * Z : (k + 1) * Z] = rows


def z_shifted(cells, dz, lane):
    if dz == 0:
        return cells
    moved = pltpu.roll(cells, (-dz) % Z, 1)
    return jnp.where(lane == (Z - 1 if dz > 0 else 0), 0.0, moved)


def fill_taps(cells_ref, out_ref, sign):
    rows = cells_ref.shape[0]
    lane = lax.broadcasted_iota(jnp.int32, (rows, Z), 1)
    zero = jnp.zeros((rows, Z), F32)
    shifted = [[z_shifted(cells_ref[:, k * Z : (k + 1) * Z], sign * (dz - 1), lane) for dz in range(3)] for k in range(PY)]
    for k in range(PY):
        parts = []
        for dy in range(3):
            at = k + sign * (dy - 1)
            for dz in range(3):
                parts.append(shifted[at][dz] if 0 <= at < PY else zero)
        parts.append(jnp.zeros((TALL - TAPS * rows, Z), F32))
        out_ref[:, k * Z : (k + 1) * Z] = jnp.concatenate(parts, axis=0).astype(BF)


def fill_z(cells, k, out_ref, sign):
    lane = lax.broadcasted_iota(jnp.int32, cells.shape, 1)
    for dz in range(3):
        moved = z_shifted(cells, sign * (dz - 1), lane)
        out_ref[dz * 128 : (dz + 1) * 128, (k + 1) * Z : (k + 2) * Z] = moved.astype(BF)


def clear_ends(ref):
    ref[:, 0:Z] = jnp.zeros((ref.shape[0], Z), ref.dtype)
    ref[:, (PY + 1) * Z :] = jnp.zeros((ref.shape[0], Z), ref.dtype)


def dot(a, b):
    return jnp.dot(a, b, preferred_element_type=F32)


def dot_t(a, b):
    return lax.dot_general(a, b, (((1,), (1,)), ((), ())), preferred_element_type=F32)


def activate(y):
    sig = 1.0 / (1.0 + jnp.exp(-y))
    return y * sig, sig * (1.0 + y * (1.0 - sig))


def bands_kernel(w2_ref, fwd_ref, bwd_ref):
    zero = jnp.zeros((C, C), F32)
    for dy in range(3):
        for dz in range(3):
            rows = []
            for xo in range(X):
                parts = []
                for xi in range(X):
                    dx = xi - xo + 1
                    parts.append(w2_ref[dx * 9 + dy * 3 + dz] if 0 <= dx < 3 else zero)
                rows.append(jnp.concatenate(parts, axis=1))
            block = jnp.concatenate(rows, axis=0)
            fwd_ref[dy, :, dz * 128 : (dz + 1) * 128] = block.astype(BF)
            bwd_ref[dy, :, dz * 128 : (dz + 1) * 128] = block.T.astype(BF)


KEPT = [
    ((2, ROWS, PY * Z), F32),
    ((2, TALL, PY * Z), BF),
    ((2, 384, (PY + 2) * Z), BF),
    ((2, 128, PY * Z), F32),
    ((2, 128, PY * Z), BF),
    ((2, 128, PY * Z), F32),
    ((2, ROWS, PY * Z), F32),
]
SAVED = len(KEPT)
HELD = [pltpu.VMEM(s, d) for s, d in KEPT] + [pltpu.SemaphoreType.DMA((SAVED, 2))]


def forward_kernel(
    anchors, slabs_ref, w1_ref, w2_ref, w3_ref, b1_ref, b2_ref, b3_ref,
    *refs,
):
    kept, held, sems = refs[:SAVED], refs[SAVED : 2 * SAVED], refs[2 * SAVED]
    first_ref, taps_ref, a1_ref, d1_ref, a2_ref, d2_ref, pred_ref = held
    copies = []

    def keep(n, p):
        copy = pltpu.make_async_copy(held[n].at[p], kept[n].at[p], sems.at[n, p])
        copy.start()
        copies.append(copy)

    for p in range(2):
        patch_rows(slabs_ref, anchors[p], first_ref.at[p])
        fill_taps(first_ref.at[p], taps_ref.at[p], 1)
        keep(0, p)
        keep(1, p)
        y1 = dot(w1_ref[...], taps_ref[p])
        act, slope = activate(y1 + b1_ref[...])
        d1_ref[p] = slope
        clear_ends(a1_ref.at[p])
        for k in range(PY):
            fill_z(act[:, k * Z : (k + 1) * Z], k, a1_ref.at[p], 1)
        keep(2, p)
        keep(3, p)
        y2 = b2_ref[...] + dot(w2_ref[0], a1_ref[p, :, 0 : PY * Z])
        for dy in range(1, 3):
            y2 = y2 + dot(w2_ref[dy], a1_ref[p, :, dy * Z : (dy + PY) * Z])
        act, slope = activate(y2)
        d2_ref[p] = slope
        a2_ref[p] = act.astype(BF)
        keep(4, p)
        keep(5, p)
        terms = dot(w3_ref[...], a2_ref[p])
        lane = lax.broadcasted_iota(jnp.int32, (ROWS, Z), 1)
        for k in range(PY):
            out = b3_ref[...] + jnp.zeros((ROWS, Z), F32)
            for dz in range(3):
                part = None
                for dy in range(3):
                    at = k + dy - 1
                    if 0 <= at < PY:
                        t = (dy * 3 + dz) * ROWS
                        term = terms[t : t + ROWS, at * Z : (at + 1) * Z]
                        part = term if part is None else part + term
                out = out + z_shifted(part, dz - 1, lane)
            pred_ref[p, :, k * Z : (k + 1) * Z] = out
        keep(6, p)
    for copy in copies:
        copy.wait()


def band_sum(full):
    lane = lax.broadcasted_iota(jnp.int32, (C, 256), 1)
    total = None
    for x in range(X):
        block = full[x * C : (x + 1) * C]
        block = jnp.concatenate([block, jnp.zeros((C, 256 - TALL), F32)], axis=1)
        moved = pltpu.roll(block, (1 - x) % 256, 1)
        e = lane % 4
        ok = (e < 3) & (x + e - 1 >= 0) & (x + e - 1 < X) & (lane < TAPS * ROWS)
        moved = jnp.where(ok, moved, 0.0)
        total = moved if total is None else total + moved
    out = None
    for f in range(F):
        part = jnp.where((lane % ROWS) // 4 == f, total, 0.0)
        part = pltpu.roll(part, (256 - f) % 256, 1)
        out = part if out is None else out + part
    return out


def backward_kernel(
    place, anchors, count, slabs_ref, w2_ref, w3_ref, *refs,
):
    kept, (keep_ref, send_ref) = refs[:SAVED], refs[SAVED : SAVED + 2]
    held, sems = refs[SAVED + 2 : 2 * SAVED + 2], refs[2 * SAVED + 2]
    last_ref, err_ref, g_ref, b_ref, grads_ref = refs[2 * SAVED + 3 :]
    first_ref, taps_ref, a1_ref, d1_ref, a2_ref, d2_ref, pred_ref = held
    copies = {}
    for p in range(2):
        for n in (6, 0, 4, 5, 2, 3, 1):
            copies[n, p] = pltpu.make_async_copy(kept[n].at[p], held[n].at[p], sems.at[n, p])
            copies[n, p].start()
    db1 = jnp.zeros((128, 1), F32)
    db2 = jnp.zeros((128, 1), F32)
    db3 = jnp.zeros((ROWS, 1), F32)
    loss = jnp.zeros((ROWS, 1), F32)
    dw1 = jnp.zeros((128, TALL), F32)
    dw3 = jnp.zeros((128, TALL), F32)
    dw2 = [jnp.zeros((128, 384), F32) for _ in range(3)]
    clear_ends(b_ref)
    for p in range(2):
        live = jnp.where(p < count[0], 1.0, 0.0).astype(F32)
        patch_rows(slabs_ref, anchors[p], last_ref)
        copies[6, p].wait()
        copies[0, p].wait()
        err = pred_ref[p] - (last_ref[...] - first_ref[p])
        loss = loss + live * jnp.sum(err * err, axis=1, keepdims=True)
        err = err * (live * (2.0 / CELLS))
        err_ref[...] = err
        db3 = db3 + jnp.sum(err, axis=1, keepdims=True)
        fill_taps(err_ref, g_ref, -1)
        da2 = dot(w3_ref[...], g_ref[...])
        copies[4, p].wait()
        dw3 = dw3 + dot_t(a2_ref[p], g_ref[...])
        copies[5, p].wait()
        dy2 = da2 * d2_ref[p]
        db2 = db2 + jnp.sum(dy2, axis=1, keepdims=True)
        for k in range(PY):
            fill_z(dy2[:, k * Z : (k + 1) * Z], k, b_ref, -1)
        middle = b_ref[128:256, Z : (PY + 1) * Z]
        da1 = None
        copies[2, p].wait()
        for dy in range(3):
            dw2[dy] = dw2[dy] + dot_t(middle, a1_ref[p, :, dy * Z : (dy + PY) * Z])
            term = dot(w2_ref[dy], b_ref[:, (2 - dy) * Z : (2 - dy + PY) * Z])
            da1 = term if da1 is None else da1 + term
        copies[3, p].wait()
        dy1 = da1 * d1_ref[p]
        db1 = db1 + jnp.sum(dy1, axis=1, keepdims=True)
        copies[1, p].wait()
        dw1 = dw1 + dot_t(dy1.astype(BF), taps_ref[p])

    lane = lax.broadcasted_iota(jnp.int32, (C, 128), 1)
    small1, small3 = band_sum(dw1), band_sum(dw3)
    fold = lambda v: v[0:C] + v[C : 2 * C] + v[2 * C : 3 * C] + v[3 * C : 4 * C]
    by_field = [jnp.sum(db3[f * X : (f + 1) * X], axis=0, keepdims=True) for f in range(F)]
    db3 = jnp.concatenate(by_field + [jnp.zeros((C - F, 1), F32)], axis=0)
    loss = jnp.sum(loss, axis=0, keepdims=True) * (1.0 / CELLS)
    extras = {0: (fold(db1), fold(db2)), 1: (db3, loss), 2: (jnp.full((C, 1), 1.0, F32) * count[0].astype(F32), None)}
    for t in range(TAPS):
        dy, dz = t // 3, t % 3
        total = jnp.zeros((C, 128), F32)
        for xo in range(X):
            block = dw2[dy][xo * C : (xo + 1) * C, dz * 128 : (dz + 1) * 128]
            moved = pltpu.roll(block, ((1 - xo) * C) % 128, 1)
            dx = lane // C
            ok = (dx < 3) & (xo + dx - 1 >= 0) & (xo + dx - 1 < X)
            total = total + jnp.where(ok, moved, 0.0)
        one = pltpu.roll(small1, (96 - ROWS * t) % 256, 1)[:, 0:128]
        three = pltpu.roll(small3, (111 - ROWS * t) % 256, 1)[:, 0:128]
        total = jnp.where((lane >= 96) & (lane < 111), one, total)
        total = jnp.where((lane >= 111) & (lane < 126), three, total)
        if t in extras:
            a, b = extras[t]
            total = jnp.where(lane == 126, a, total)
            if b is not None:
                total = jnp.where(lane == 127, b, total)
        grads_ref[t * C : (t + 1) * C] = total
    second = place[1] % 2 == 1
    low, high = grads_ref[0:HALF], grads_ref[HALF:]
    keep_ref[...] = jnp.where(second, high, low)
    send_ref[...] = jnp.where(second, low, high)


def finish_kernel(
    place, mine_ref, other_ref, g1_ref, gb1_ref, g2_ref, gb2_ref, g3_ref, gb3_ref, loss_ref, grads_ref
):
    second = place[1] % 2 == 1
    mine, other = mine_ref[...], other_ref[...]
    grads_ref[0:HALF] = jnp.where(second, other, mine)
    grads_ref[HALF:] = jnp.where(second, mine, other)
    rows = lambda t: grads_ref[t * C : (t + 1) * C]
    total = rows(2)[0:1, 126:127]
    for t in range(TAPS):
        dy, dz = t // 3, t % 3
        block = rows(t) / total
        for dx in range(3):
            g2_ref[dx * TAPS + t] = block[:, dx * C : (dx + 1) * C]
        turned = block.T
        for f in range(F):
            for dx in range(3):
                to = (f * 3 + dx) * 3 + dy
                at = 96 + f * 3 + dx
                g1_ref[to, dz : dz + 1, :] = turned[at : at + 1]
                at = 111 + f * 3 + 2 - dx
                g3_ref[to, dz : dz + 1, :] = turned[at : at + 1]
        if t == 0:
            gb1_ref[...] = turned[126:127]
            gb2_ref[...] = turned[127:128]
        if t == 1:
            gb3_ref[...] = turned[126:127, 0:F]
            loss_ref[...] = turned[127:128, 0:1]


def reduce_steps():
    def near(c):
        return c ^ 1

    def far(c):
        return 3 - c

    steps = []
    for n in range(6):
        pairs = []
        for gx in range(8):
            for gy in range(16):
                at = {"x": gx // 2, "y": gy // 4, "z": (gy // 2 % 2) * 2 + gx % 2}
                axis = "zyx"[n // 2]
                at[axis] = (near, far)[n % 2](at[axis])
                to = (at["x"] * 2 + at["z"] % 2) * 16 + at["y"] * 4 + (at["z"] // 2) * 2 + gy % 2
                pairs.append((gx * 16 + gy, to))
        steps.append(pairs)
    return steps


def sum_all(keep, send):
    cores = [(i, i ^ 1) for i in range(16)]
    mine = keep + lax.ppermute(send, "gy", cores)
    for pairs in reduce_steps():
        mine = mine + lax.ppermute(mine, ("gx", "gy"), pairs)
    return mine, lax.ppermute(mine, "gy", cores)


def banded(w, flip):
    bands = []
    for x in range(X):
        if flip:
            w_ = w[:, ::-1]
        else:
            w_ = w
        padded = jnp.pad(w_, ((0, 0), (x, X - 1 - x), (0, 0), (0, 0), (0, 0)))
        bands.append(padded[:, 1 : X + 1])
    all_x = jnp.stack(bands, axis=4)
    rows = jnp.transpose(all_x, (2, 3, 0, 1, 4, 5)).reshape(TAPS, F * X, X * C)
    rows = jnp.pad(rows, ((0, 0), (0, ROWS - F * X), (0, 0))).reshape(TAPS * ROWS, X * C)
    return jnp.pad(rows, ((0, TALL - TAPS * ROWS), (0, 0))).astype(BF)


def on_device(
    initial_fields, velocity, diffusivity, patch_anchor, patch_count,
    weight_one, bias_one, weight_two, bias_two, weight_three, bias_three,
):
    place = jnp.stack([lax.axis_index("gx"), lax.axis_index("gy")]).astype(jnp.int32)
    u = initial_fields.reshape(F * X, 4, 2048)
    vel = velocity.reshape(3 * X, 4, 2048)
    anchors = patch_anchor.reshape(2)
    count = patch_count.reshape(1)

    edges = call(edges_kernel, EDGES, ins=[SMEM, VMEM], nbytes=1_000_000)(place, u)
    (slabs,) = call(slabs_kernel, [SLABS], ins=[VMEM], nbytes=1_500_000)(u)
    first_slabs = lax.all_to_all(slabs, "gy", 0, 0, tiled=True).reshape(32, 2 * F * X, Z)

    w2 = jnp.transpose(weight_two, (2, 3, 4, 0, 1)).reshape(27, C, C)
    w2_fwd, w2_bwd = call(bands_kernel, [((3, 128, 384), BF)] * 2, ins=[VMEM], nbytes=1_000_000)(w2)
    w1_band = banded(jnp.transpose(weight_one, (1, 2, 3, 4, 0)), False)
    w3_band = banded(jnp.transpose(weight_three, (0, 2, 3, 4, 1)), True)
    b1 = jnp.tile(bias_one, X).reshape(128, 1)
    b2 = jnp.tile(bias_two, X).reshape(128, 1)
    b3 = jnp.pad(jnp.repeat(bias_three, X), (0, ROWS - F * X)).reshape(ROWS, 1)

    for step in range(STEPS):
        last = step == STEPS - 1
        outs = [((F * X, 4, 2048), F32)] + ([SLABS] if last else EDGES)
        received = exchange(edges)
        (part,) = call(inner_kernel, [((F * X, 4, 2048), F32)], ins=[VMEM] * 3, nbytes=4_000_000)(u, vel, diffusivity)
        kernel = lambda *refs, last=last: outer_kernel(last, *refs)
        u, *edges = call(kernel, outs, ins=[SMEM] + [VMEM] * 7, nbytes=3_000_000)(
            place, part, *received, vel, diffusivity
        )

    learned = call(
        forward_kernel,
        KEPT,
        scratch=HELD,
        ins=[SMEM] + [VMEM] * 7,
        flops=2_000_000_000,
        nbytes=8_000_000,
        mib=24,
        out_space=HBM,
    )(anchors, first_slabs, w1_band.T, w2_fwd, w3_band, b1, b2, b3)

    last_slabs = lax.all_to_all(edges[0], "gy", 0, 0, tiled=True).reshape(32, 2 * F * X, Z)
    keep, send = call(
        backward_kernel,
        [((HALF, 128), F32)] * 2,
        scratch=HELD
        + [
            pltpu.VMEM((ROWS, PY * Z), F32),
            pltpu.VMEM((ROWS, PY * Z), F32),
            pltpu.VMEM((TALL, PY * Z), BF),
            pltpu.VMEM((384, (PY + 2) * Z), BF),
            pltpu.VMEM((2 * HALF, 128), F32),
        ],
        ins=[SMEM] * 3 + [VMEM] * 3 + [HBM] * SAVED,
        flops=4_000_000_000,
        nbytes=10_000_000,
        mib=24,
    )(place, anchors, count, last_slabs, w2_bwd, w3_band.T, *learned)

    g1, gb1, g2, gb2, g3, gb3, loss = call(
        finish_kernel,
        [((45, 3, C), F32), ((1, C), F32), ((27, C, C), F32), ((1, C), F32), ((45, 3, C), F32), ((1, F), F32), ((1, 1), F32)],
        scratch=[pltpu.VMEM((2 * HALF, 128), F32)],
        ins=[SMEM, VMEM, VMEM],
        nbytes=1_000_000,
    )(place, *sum_all(keep, send))
    g1 = jnp.transpose(g1.reshape(F, 3, 3, 3, C), (4, 0, 1, 2, 3))
    g2 = jnp.transpose(g2.reshape(3, 3, 3, C, C), (3, 4, 0, 1, 2))
    g3 = jnp.transpose(g3.reshape(F, 3, 3, 3, C), (0, 4, 1, 2, 3))
    gb1, gb2, gb3, loss = gb1.reshape(C), gb2.reshape(C), gb3.reshape(F), loss.reshape(())
    return u.reshape(F, X, 4, 2048), g1, gb1, g2, gb2, g3, gb3, loss


def solution(mesh):
    return jax.shard_map(
        on_device,
        mesh=mesh,
        in_specs=(
            P(None, "gx", "gy", None),
            P(None, "gx", "gy", None),
            P("gx", "gy", None),
            P("gx", "gy", None),
            P("gx", "gy"),
            P(),
            P(),
            P(),
            P(),
            P(),
            P(),
        ),
        out_specs=(P(None, "gx", "gy", None), P(), P(), P(), P(), P(), P(), P()),
        check_vma=False,
    )
```

```python
import jax
import jax.numpy as jnp
from jax import lax
from jax.experimental import pallas as pl
from jax.experimental.pallas import tpu as pltpu
from jax.sharding import PartitionSpec as P

STEPS = 3
F = 5
C = 32
X = 4
PY = 8
Z = 128
ROWS = 24
HALF = 144
TAPS = 9
TALL = 224
CELLS = 20480.0
BF = jnp.bfloat16
F32 = jnp.float32
VMEM = pl.BlockSpec(memory_space=pltpu.VMEM)
SMEM = pl.BlockSpec(memory_space=pltpu.SMEM)
HBM = pl.BlockSpec(memory_space=pltpu.HBM)
MIB = 1024 * 1024


def call(kernel, outs, scratch=(), flops=0, nbytes=0, ins=(), mib=12, out_space=None):
    return pl.pallas_call(
        kernel,
        out_shape=[jax.ShapeDtypeStruct(s, d) for s, d in outs],
        in_specs=list(ins),
        out_specs=[out_space or VMEM] * len(outs),
        scratch_shapes=list(scratch),
        compiler_params=pltpu.CompilerParams(vmem_limit_bytes=mib * MIB),
        cost_estimate=pl.CostEstimate(flops=flops, bytes_accessed=nbytes, transcendentals=0),
    )


def pack_slabs(get, out_ref):
    for row in range(F * X):
        cells = get(row)
        for y in range(4):
            for j in range(16):
                out_ref[j, y // 2, pl.ds((y % 2) * F * X + row, 1), :] = cells[y : y + 1, j * Z : (j + 1) * Z]


def write_edges(get, odd_x, odd_y, xa_ref, xb_ref, ya_ref, yb_ref):
    for f in range(F):
        head, tail = get(f * X), get(f * X + X - 1)
        xa_ref[f] = jnp.where(odd_x, head, tail)
        xb_ref[f] = jnp.where(odd_x, tail, head)
    for row in range(F * X):
        cells = get(row)
        head, tail = cells[0:1], cells[3:4]
        ya_ref[pl.ds(row, 1), :] = jnp.where(odd_y, head, tail)
        yb_ref[pl.ds(row, 1), :] = jnp.where(odd_y, tail, head)


def edges_kernel(place, u_ref, xa_ref, xb_ref, ya_ref, yb_ref):
    get = lambda row: u_ref[row]
    write_edges(get, place[0] % 2 == 1, place[1] % 2 == 1, xa_ref, xb_ref, ya_ref, yb_ref)


def slabs_kernel(u_ref, slabs_ref):
    pack_slabs(lambda row: u_ref[row], slabs_ref)


def inner_kernel(u_ref, vel_ref, dif_ref, part_ref):
    lane = lax.broadcasted_iota(jnp.int32, (4, 2048), 1)
    not_first, not_last = lane > 0, lane < 2047
    zero_row = jnp.zeros((1, 2048), F32)
    for x in range(X):
        v0, v1, v2, dif = vel_ref[x], vel_ref[X + x], vel_ref[2 * X + x], dif_ref[x]
        for f in range(F):
            row = f * X + x
            middle = u_ref[row]
            x_plus = u_ref[row + 1] if x < X - 1 else 0.0
            x_minus = u_ref[row - 1] if x > 0 else 0.0
            y_plus = jnp.concatenate([middle[1:4], zero_row], axis=0)
            y_minus = jnp.concatenate([zero_row, middle[0:3]], axis=0)
            z_plus = jnp.where(not_last, pltpu.roll(middle, 2047, 1), 0.0)
            z_minus = jnp.where(not_first, pltpu.roll(middle, 1, 1), 0.0)
            carried = v0 * (x_plus - x_minus) + v1 * (y_plus - y_minus) + v2 * (z_plus - z_minus)
            spread = x_plus + x_minus + y_plus + y_minus + z_plus + z_minus - 6.0 * middle
            part_ref[row] = middle - 0.5 * carried + dif * spread


def outer_kernel(last, place, part_ref, rxa, rxb, rya, ryb, vel_ref, dif_ref, new_ref, *outs):
    gx, gy = place[0], place[1]
    odd_x, odd_y = gx % 2 == 1, gy % 2 == 1
    y_at = lax.broadcasted_iota(jnp.int32, (4, 2048), 0)
    up_on = (y_at == 3) & (gy != 15)
    down_on = (y_at == 0) & (gy != 0)
    for x in range(X):
        v0, v1, dif = vel_ref[x], vel_ref[X + x], dif_ref[x]
        up = jnp.where(up_on, dif - 0.5 * v1, 0.0)
        down = jnp.where(down_on, dif + 0.5 * v1, 0.0)
        side = None
        if x == X - 1:
            side = jnp.where(gx == 7, 0.0, dif - 0.5 * v0)
        if x == 0:
            side = jnp.where(gx == 0, 0.0, dif + 0.5 * v0)
        from_a = jnp.where(odd_y, down, up)
        from_b = jnp.where(odd_y, up, down)
        for f in range(F):
            row = f * X + x
            new = part_ref[row] + rya[pl.ds(row, 1), :] * from_a + ryb[pl.ds(row, 1), :] * from_b
            if x == X - 1:
                new = new + jnp.where(odd_x, rxb[f], rxa[f]) * side
            if x == 0:
                new = new + jnp.where(odd_x, rxa[f], rxb[f]) * side
            new_ref[row] = new
    get = lambda row: new_ref[row]
    if last:
        pack_slabs(get, outs[0])
    else:
        write_edges(get, odd_x, odd_y, *outs)


EDGES = [((F, X, 2048), F32)] * 2 + [((F * X, 2048), F32)] * 2
SLABS = ((16, 2, 2 * F * X, Z), F32)


def exchange(edges):
    def pairs(n, second):
        partner = lambda i: (i ^ 1) if not second else ((i + 1) if i % 2 else (i - 1)) % n
        return [(i, partner(i)) for i in range(n)]

    xa, xb, ya, yb = edges
    return (
        lax.ppermute(xa, "gx", pairs(8, False)),
        lax.ppermute(xb, "gx", pairs(8, True)),
        lax.ppermute(ya, "gy", pairs(16, False)),
        lax.ppermute(yb, "gy", pairs(16, True)),
    )


def patch_rows(slabs_ref, anchor, out_ref):
    out_ref[...] = jnp.zeros_like(out_ref)
    for k in range(PY):
        y = anchor + k
        both = slabs_ref[y // 2]
        rows = jnp.where(y % 2 == 1, both[F * X :], both[: F * X])
        out_ref[0 : F * X, k * Z : (k + 1) * Z] = rows


def z_shifted(cells, dz, lane):
    if dz == 0:
        return cells
    moved = pltpu.roll(cells, (-dz) % Z, 1)
    return jnp.where(lane == (Z - 1 if dz > 0 else 0), 0.0, moved)


def fill_taps(cells, out_ref, sign):
    rows = cells.shape[0]
    lane = lax.broadcasted_iota(jnp.int32, (rows, Z), 1)
    zero = jnp.zeros((rows, Z), F32)
    shifted = [[z_shifted(cells[:, k * Z : (k + 1) * Z], sign * (dz - 1), lane) for dz in range(3)] for k in range(PY)]
    for k in range(PY):
        parts = []
        for dy in range(3):
            at = k + sign * (dy - 1)
            for dz in range(3):
                parts.append(shifted[at][dz] if 0 <= at < PY else zero)
        parts.append(jnp.zeros((TALL - TAPS * rows, Z), F32))
        out_ref[:, k * Z : (k + 1) * Z] = jnp.concatenate(parts, axis=0).astype(BF)


def fill_z(cells, k, out_ref, sign):
    lane = lax.broadcasted_iota(jnp.int32, cells.shape, 1)
    for dz in range(3):
        moved = z_shifted(cells, sign * (dz - 1), lane)
        out_ref[dz * 128 : (dz + 1) * 128, (k + 1) * Z : (k + 2) * Z] = moved.astype(BF)


def clear_ends(ref):
    ref[:, 0:Z] = jnp.zeros((ref.shape[0], Z), ref.dtype)
    ref[:, (PY + 1) * Z :] = jnp.zeros((ref.shape[0], Z), ref.dtype)


def dot(a, b):
    return jnp.dot(a, b, preferred_element_type=F32)


def dot_t(a, b):
    return lax.dot_general(a, b, (((1,), (1,)), ((), ())), preferred_element_type=F32)


def activate(y):
    sig = 1.0 / (1.0 + jnp.exp(-y))
    return y * sig, sig * (1.0 + y * (1.0 - sig))


def bands_kernel(w2_ref, fwd_ref, bwd_ref):
    zero = jnp.zeros((C, C), F32)
    for dy in range(3):
        for dz in range(3):
            rows = []
            for xo in range(X):
                parts = []
                for xi in range(X):
                    dx = xi - xo + 1
                    parts.append(w2_ref[dx * 9 + dy * 3 + dz] if 0 <= dx < 3 else zero)
                rows.append(jnp.concatenate(parts, axis=1))
            block = jnp.concatenate(rows, axis=0)
            fwd_ref[dy, :, dz * 128 : (dz + 1) * 128] = block.astype(BF)
            bwd_ref[dy, :, dz * 128 : (dz + 1) * 128] = block.T.astype(BF)


PARTS = 80
AT = {"sum": (0, PARTS), "first": (80, 32), "a1": (112, 128), "a2": (240, 128), "d1": (368, 128), "d2": (496, 128)}
KEPT = ((2, 16384, PY * Z), BF)
NAMES = ("sum", "d2", "a2", "a1", "first", "d1")
HELD = [pltpu.VMEM((2, AT[name][1], PY * Z), BF) for name in NAMES] + [pltpu.SemaphoreType.DMA((len(NAMES), 2))]


def transfers(kept_ref, held, sems):
    out = {}
    for n, name in enumerate(NAMES):
        for p in range(2):
            start, size = AT[name]
            out[name, p] = (kept_ref.at[p, pl.ds(start, size)], held[n].at[p], sems.at[n, p])
    return out


def forward_kernel(
    anchors, slabs_ref, w1_ref, w2_ref, w3_ref, b1_ref, b2_ref, b3_ref, kept_ref, *refs,
):
    held, sems, (first_ref, taps_ref, a1_ref) = refs[: len(NAMES)], refs[len(NAMES)], refs[len(NAMES) + 1 :]
    sum_ref, d2_ref, a2_ref, a1_kept, cells_ref, d1_ref = held
    plan = transfers(kept_ref, held, sems)
    copies = []

    def keep(name, p):
        to, of, sem = plan[name, p]
        copies.append(pltpu.make_async_copy(of, to, sem))
        copies[-1].start()

    for p in range(2):
        patch_rows(slabs_ref, anchors[p], first_ref.at[p])
        cells_ref[p] = jnp.concatenate([first_ref[p], jnp.zeros((32 - ROWS, PY * Z), F32)], axis=0).astype(BF)
        keep("first", p)
        fill_taps(first_ref[p], taps_ref.at[p], 1)
        y1 = dot(w1_ref[...], taps_ref[p])
        act, slope = activate(y1 + b1_ref[...])
        d1_ref[p] = slope.astype(BF)
        keep("d1", p)
        a1_kept[p] = act.astype(BF)
        keep("a1", p)
        clear_ends(a1_ref.at[p])
        for k in range(PY):
            fill_z(act[:, k * Z : (k + 1) * Z], k, a1_ref.at[p], 1)
        y2 = b2_ref[...] + dot(w2_ref[0], a1_ref[p, :, 0 : PY * Z])
        for dy in range(1, 3):
            y2 = y2 + dot(w2_ref[dy], a1_ref[p, :, dy * Z : (dy + PY) * Z])
        act, slope = activate(y2)
        d2_ref[p] = slope.astype(BF)
        a2_ref[p] = act.astype(BF)
        keep("d2", p)
        keep("a2", p)
        terms = dot(w3_ref[...], a2_ref[p])
        lane = lax.broadcasted_iota(jnp.int32, (ROWS, Z), 1)
        for k in range(PY):
            out = b3_ref[...] + first_ref[p, :, k * Z : (k + 1) * Z]
            for dz in range(3):
                part = None
                for dy in range(3):
                    at = k + dy - 1
                    if 0 <= at < PY:
                        t = (dy * 3 + dz) * ROWS
                        term = terms[t : t + ROWS, at * Z : (at + 1) * Z]
                        part = term if part is None else part + term
                out = out + z_shifted(part, dz - 1, lane)
            high = out.astype(BF).astype(F32)
            mid = (out - high).astype(BF).astype(F32)
            low = out - high - mid
            pad = jnp.zeros((PARTS - 3 * ROWS, Z), F32)
            sum_ref[p, :, k * Z : (k + 1) * Z] = jnp.concatenate([high, mid, low, pad], axis=0).astype(BF)
        keep("sum", p)
    for copy in copies:
        copy.wait()


def band_sum(full):
    lane = lax.broadcasted_iota(jnp.int32, (C, 256), 1)
    total = None
    for x in range(X):
        block = full[x * C : (x + 1) * C]
        block = jnp.concatenate([block, jnp.zeros((C, 256 - TALL), F32)], axis=1)
        moved = pltpu.roll(block, (1 - x) % 256, 1)
        e = lane % 4
        ok = (e < 3) & (x + e - 1 >= 0) & (x + e - 1 < X) & (lane < TAPS * ROWS)
        moved = jnp.where(ok, moved, 0.0)
        total = moved if total is None else total + moved
    out = None
    for f in range(F):
        part = jnp.where((lane % ROWS) // 4 == f, total, 0.0)
        part = pltpu.roll(part, (256 - f) % 256, 1)
        out = part if out is None else out + part
    return out


def backward_kernel(place, anchors, count, slabs_ref, w2_ref, w3_ref, kept_ref, keep_ref, send_ref, *refs):
    held, sems = refs[: len(NAMES)], refs[len(NAMES)]
    last_ref, taps_ref, a1_ref, g_ref, b_ref, grads_ref = refs[len(NAMES) + 1 :]
    sum_ref, d2_ref, a2_ref, a1_kept, cells_ref, d1_ref = held
    plan = transfers(kept_ref, held, sems)
    copies = {key: pltpu.make_async_copy(of, to, sem) for key, (of, to, sem) in plan.items()}
    for p in range(2):
        for name in NAMES:
            copies[name, p].start()
    db1 = jnp.zeros((128, 1), F32)
    db2 = jnp.zeros((128, 1), F32)
    db3 = jnp.zeros((ROWS, 1), F32)
    loss = jnp.zeros((ROWS, 1), F32)
    dw1 = jnp.zeros((128, TALL), F32)
    dw3 = jnp.zeros((128, TALL), F32)
    dw2 = [jnp.zeros((128, 384), F32) for _ in range(3)]
    for name in NAMES[:3]:
        for p in range(2):
            copies[name, p].wait()
    for p in range(2):
        live = jnp.where(p < count[0], 1.0, 0.0).astype(F32)
        patch_rows(slabs_ref, anchors[p], last_ref.at[p])
        parts = sum_ref[p].astype(F32)
        err = parts[0:ROWS] + parts[ROWS : 2 * ROWS] + parts[2 * ROWS : 3 * ROWS] - last_ref[p]
        loss = loss + live * jnp.sum(err * err, axis=1, keepdims=True)
        err = err * (live * (2.0 / CELLS))
        db3 = db3 + jnp.sum(err, axis=1, keepdims=True)
        fill_taps(err, g_ref.at[p], -1)
        da2 = dot(w3_ref[...], g_ref[p])
        dw3 = dw3 + dot_t(a2_ref[p], g_ref[p])
        dy2 = da2 * d2_ref[p].astype(F32)
        db2 = db2 + jnp.sum(dy2, axis=1, keepdims=True)
        clear_ends(b_ref.at[p])
        for k in range(PY):
            fill_z(dy2[:, k * Z : (k + 1) * Z], k, b_ref.at[p], -1)
    for name in NAMES[3:]:
        for p in range(2):
            copies[name, p].wait()
    for p in range(2):
        clear_ends(a1_ref.at[p])
        for k in range(PY):
            fill_z(a1_kept[p, :, k * Z : (k + 1) * Z].astype(F32), k, a1_ref.at[p], 1)
        fill_taps(cells_ref[p].astype(F32)[0:ROWS], taps_ref.at[p], 1)
        middle = b_ref[p, 128:256, Z : (PY + 1) * Z]
        da1 = None
        for dy in range(3):
            dw2[dy] = dw2[dy] + dot_t(middle, a1_ref[p, :, dy * Z : (dy + PY) * Z])
            term = dot(w2_ref[dy], b_ref[p, :, (2 - dy) * Z : (2 - dy + PY) * Z])
            da1 = term if da1 is None else da1 + term
        dy1 = da1 * d1_ref[p].astype(F32)
        db1 = db1 + jnp.sum(dy1, axis=1, keepdims=True)
        dw1 = dw1 + dot_t(dy1.astype(BF), taps_ref[p])

    lane = lax.broadcasted_iota(jnp.int32, (C, 128), 1)
    small1, small3 = band_sum(dw1), band_sum(dw3)
    fold = lambda v: v[0:C] + v[C : 2 * C] + v[2 * C : 3 * C] + v[3 * C : 4 * C]
    by_field = [jnp.sum(db3[f * X : (f + 1) * X], axis=0, keepdims=True) for f in range(F)]
    db3 = jnp.concatenate(by_field + [jnp.zeros((C - F, 1), F32)], axis=0)
    loss = jnp.sum(loss, axis=0, keepdims=True) * (1.0 / CELLS)
    extras = {0: (fold(db1), fold(db2)), 1: (db3, loss), 2: (jnp.full((C, 1), 1.0, F32) * count[0].astype(F32), None)}
    for t in range(TAPS):
        dy, dz = t // 3, t % 3
        total = jnp.zeros((C, 128), F32)
        for xo in range(X):
            block = dw2[dy][xo * C : (xo + 1) * C, dz * 128 : (dz + 1) * 128]
            moved = pltpu.roll(block, ((1 - xo) * C) % 128, 1)
            dx = lane // C
            ok = (dx < 3) & (xo + dx - 1 >= 0) & (xo + dx - 1 < X)
            total = total + jnp.where(ok, moved, 0.0)
        one = pltpu.roll(small1, (96 - ROWS * t) % 256, 1)[:, 0:128]
        three = pltpu.roll(small3, (111 - ROWS * t) % 256, 1)[:, 0:128]
        total = jnp.where((lane >= 96) & (lane < 111), one, total)
        total = jnp.where((lane >= 111) & (lane < 126), three, total)
        if t in extras:
            a, b = extras[t]
            total = jnp.where(lane == 126, a, total)
            if b is not None:
                total = jnp.where(lane == 127, b, total)
        grads_ref[t * C : (t + 1) * C] = total
    second = place[1] % 2 == 1
    low, high = grads_ref[0:HALF], grads_ref[HALF:]
    keep_ref[...] = jnp.where(second, high, low)
    send_ref[...] = jnp.where(second, low, high)


def finish_kernel(
    place, mine_ref, other_ref, g1_ref, gb1_ref, g2_ref, gb2_ref, g3_ref, gb3_ref, loss_ref, grads_ref
):
    second = place[1] % 2 == 1
    mine, other = mine_ref[...], other_ref[...]
    grads_ref[0:HALF] = jnp.where(second, other, mine)
    grads_ref[HALF:] = jnp.where(second, mine, other)
    rows = lambda t: grads_ref[t * C : (t + 1) * C]
    total = rows(2)[0:1, 126:127]
    for t in range(TAPS):
        dy, dz = t // 3, t % 3
        block = rows(t) / total
        for dx in range(3):
            g2_ref[dx * TAPS + t] = block[:, dx * C : (dx + 1) * C]
        turned = block.T
        for f in range(F):
            for dx in range(3):
                to = (f * 3 + dx) * 3 + dy
                at = 96 + f * 3 + dx
                g1_ref[to, dz : dz + 1, :] = turned[at : at + 1]
                at = 111 + f * 3 + 2 - dx
                g3_ref[to, dz : dz + 1, :] = turned[at : at + 1]
        if t == 0:
            gb1_ref[...] = turned[126:127]
            gb2_ref[...] = turned[127:128]
        if t == 1:
            gb3_ref[...] = turned[126:127, 0:F]
            loss_ref[...] = turned[127:128, 0:1]


def reduce_steps():
    def near(c):
        return c ^ 1

    def far(c):
        return 3 - c

    steps = []
    for n in range(6):
        pairs = []
        for gx in range(8):
            for gy in range(16):
                at = {"x": gx // 2, "y": gy // 4, "z": (gy // 2 % 2) * 2 + gx % 2}
                axis = "zyx"[n // 2]
                at[axis] = (near, far)[n % 2](at[axis])
                to = (at["x"] * 2 + at["z"] % 2) * 16 + at["y"] * 4 + (at["z"] // 2) * 2 + gy % 2
                pairs.append((gx * 16 + gy, to))
        steps.append(pairs)
    return steps


def sum_all(keep, send):
    cores = [(i, i ^ 1) for i in range(16)]
    mine = keep + lax.ppermute(send, "gy", cores)
    for pairs in reduce_steps():
        mine = mine + lax.ppermute(mine, ("gx", "gy"), pairs)
    return mine, lax.ppermute(mine, "gy", cores)


def banded(w, flip):
    bands = []
    for x in range(X):
        if flip:
            w_ = w[:, ::-1]
        else:
            w_ = w
        padded = jnp.pad(w_, ((0, 0), (x, X - 1 - x), (0, 0), (0, 0), (0, 0)))
        bands.append(padded[:, 1 : X + 1])
    all_x = jnp.stack(bands, axis=4)
    rows = jnp.transpose(all_x, (2, 3, 0, 1, 4, 5)).reshape(TAPS, F * X, X * C)
    rows = jnp.pad(rows, ((0, 0), (0, ROWS - F * X), (0, 0))).reshape(TAPS * ROWS, X * C)
    return jnp.pad(rows, ((0, TALL - TAPS * ROWS), (0, 0))).astype(BF)


def on_device(
    initial_fields, velocity, diffusivity, patch_anchor, patch_count,
    weight_one, bias_one, weight_two, bias_two, weight_three, bias_three,
):
    place = jnp.stack([lax.axis_index("gx"), lax.axis_index("gy")]).astype(jnp.int32)
    u = initial_fields.reshape(F * X, 4, 2048)
    vel = velocity.reshape(3 * X, 4, 2048)
    anchors = patch_anchor.reshape(2)
    count = patch_count.reshape(1)

    edges = call(edges_kernel, EDGES, ins=[SMEM, VMEM], nbytes=1_000_000)(place, u)
    (slabs,) = call(slabs_kernel, [SLABS], ins=[VMEM], nbytes=1_500_000)(u)
    first_slabs = lax.all_to_all(slabs, "gy", 0, 0, tiled=True).reshape(32, 2 * F * X, Z)

    w2 = jnp.transpose(weight_two, (2, 3, 4, 0, 1)).reshape(27, C, C)
    w2_fwd, w2_bwd = call(bands_kernel, [((3, 128, 384), BF)] * 2, ins=[VMEM], nbytes=1_000_000)(w2)
    w1_band = banded(jnp.transpose(weight_one, (1, 2, 3, 4, 0)), False)
    w3_band = banded(jnp.transpose(weight_three, (0, 2, 3, 4, 1)), True)
    b1 = jnp.tile(bias_one, X).reshape(128, 1)
    b2 = jnp.tile(bias_two, X).reshape(128, 1)
    b3 = jnp.pad(jnp.repeat(bias_three, X), (0, ROWS - F * X)).reshape(ROWS, 1)

    for step in range(STEPS):
        last = step == STEPS - 1
        outs = [((F * X, 4, 2048), F32)] + ([SLABS] if last else EDGES)
        received = exchange(edges)
        (part,) = call(inner_kernel, [((F * X, 4, 2048), F32)], ins=[VMEM] * 3, nbytes=4_000_000)(u, vel, diffusivity)
        kernel = lambda *refs, last=last: outer_kernel(last, *refs)
        u, *edges = call(kernel, outs, ins=[SMEM] + [VMEM] * 7, nbytes=3_000_000)(
            place, part, *received, vel, diffusivity
        )

    (kept,) = call(
        forward_kernel,
        [KEPT],
        scratch=HELD
        + [
            pltpu.VMEM((2, ROWS, PY * Z), F32),
            pltpu.VMEM((2, TALL, PY * Z), BF),
            pltpu.VMEM((2, 384, (PY + 2) * Z), BF),
        ],
        ins=[SMEM] + [VMEM] * 7,
        flops=2_000_000_000,
        nbytes=8_000_000,
        mib=24,
        out_space=HBM,
    )(anchors, first_slabs, w1_band.T, w2_fwd, w3_band, b1, b2, b3)

    last_slabs = lax.all_to_all(edges[0], "gy", 0, 0, tiled=True).reshape(32, 2 * F * X, Z)
    keep, send = call(
        backward_kernel,
        [((HALF, 128), F32)] * 2,
        scratch=HELD
        + [
            pltpu.VMEM((2, ROWS, PY * Z), F32),
            pltpu.VMEM((2, TALL, PY * Z), BF),
            pltpu.VMEM((2, 384, (PY + 2) * Z), BF),
            pltpu.VMEM((2, TALL, PY * Z), BF),
            pltpu.VMEM((2, 384, (PY + 2) * Z), BF),
            pltpu.VMEM((2 * HALF, 128), F32),
        ],
        ins=[SMEM] * 3 + [VMEM] * 3 + [HBM],
        flops=4_000_000_000,
        nbytes=10_000_000,
        mib=24,
    )(place, anchors, count, last_slabs, w2_bwd, w3_band.T, kept)

    g1, gb1, g2, gb2, g3, gb3, loss = call(
        finish_kernel,
        [((45, 3, C), F32), ((1, C), F32), ((27, C, C), F32), ((1, C), F32), ((45, 3, C), F32), ((1, F), F32), ((1, 1), F32)],
        scratch=[pltpu.VMEM((2 * HALF, 128), F32)],
        ins=[SMEM, VMEM, VMEM],
        nbytes=1_000_000,
    )(place, *sum_all(keep, send))
    g1 = jnp.transpose(g1.reshape(F, 3, 3, 3, C), (4, 0, 1, 2, 3))
    g2 = jnp.transpose(g2.reshape(3, 3, 3, C, C), (3, 4, 0, 1, 2))
    g3 = jnp.transpose(g3.reshape(F, 3, 3, 3, C), (0, 4, 1, 2, 3))
    gb1, gb2, gb3, loss = gb1.reshape(C), gb2.reshape(C), gb3.reshape(F), loss.reshape(())
    return u.reshape(F, X, 4, 2048), g1, gb1, g2, gb2, g3, gb3, loss


def solution(mesh):
    return jax.shard_map(
        on_device,
        mesh=mesh,
        in_specs=(
            P(None, "gx", "gy", None),
            P(None, "gx", "gy", None),
            P("gx", "gy", None),
            P("gx", "gy", None),
            P("gx", "gy"),
            P(),
            P(),
            P(),
            P(),
            P(),
            P(),
        ),
        out_specs=(P(None, "gx", "gy", None), P(), P(), P(), P(), P(), P(), P()),
        check_vma=False,
    )
```

```python
import jax
import jax.numpy as jnp
from jax import lax
from jax.experimental import pallas as pl
from jax.experimental.pallas import tpu as pltpu
from jax.sharding import PartitionSpec as P

STEPS = 3
F = 5
C = 32
X = 4
PY = 8
Z = 128
ROWS = 24
HALF = 144
TAPS = 9
TALL = 224
CELLS = 20480.0
BF = jnp.bfloat16
F32 = jnp.float32
VMEM = pl.BlockSpec(memory_space=pltpu.VMEM)
SMEM = pl.BlockSpec(memory_space=pltpu.SMEM)
HBM = pl.BlockSpec(memory_space=pltpu.HBM)
ANY = pl.BlockSpec(memory_space=pl.ANY)
MIB = 1024 * 1024
BESIDE = 6_000_000_000


def call(kernel, outs, scratch=(), flops=0, nbytes=0, ins=(), mib=12, out_space=None):
    return pl.pallas_call(
        kernel,
        out_shape=[jax.ShapeDtypeStruct(s, d) for s, d in outs],
        in_specs=list(ins),
        out_specs=[out_space or VMEM] * len(outs),
        scratch_shapes=list(scratch),
        compiler_params=pltpu.CompilerParams(vmem_limit_bytes=mib * MIB),
        cost_estimate=pl.CostEstimate(flops=flops, bytes_accessed=nbytes, transcendentals=0),
    )


def pack_slabs(get, out_ref):
    for row in range(F * X):
        cells = get(row)
        for y in range(4):
            for j in range(16):
                out_ref[j, y // 2, pl.ds((y % 2) * F * X + row, 1), :] = cells[y : y + 1, j * Z : (j + 1) * Z]


def write_edges(get, odd_x, odd_y, xa_ref, xb_ref, ya_ref, yb_ref):
    for f in range(F):
        head, tail = get(f * X), get(f * X + X - 1)
        xa_ref[f] = jnp.where(odd_x, head, tail)
        xb_ref[f] = jnp.where(odd_x, tail, head)
    for row in range(F * X):
        cells = get(row)
        head, tail = cells[0:1], cells[3:4]
        f, x = row // X, row % X
        ya_ref[f, x : x + 1, :] = jnp.where(odd_y, head, tail)
        yb_ref[f, x : x + 1, :] = jnp.where(odd_y, tail, head)


def edges_kernel(place, u_ref, xa_ref, xb_ref, ya_ref, yb_ref):
    get = lambda row: u_ref[row]
    write_edges(get, place[0] % 2 == 1, place[1] % 2 == 1, xa_ref, xb_ref, ya_ref, yb_ref)


def slabs_kernel(u_ref, slabs_ref):
    pack_slabs(lambda row: u_ref[row], slabs_ref)


def inner_kernel(u_ref, vel_ref, dif_ref, part_ref):
    lane = lax.broadcasted_iota(jnp.int32, (4, 2048), 1)
    not_first, not_last = lane > 0, lane < 2047
    zero_row = jnp.zeros((1, 2048), F32)
    for x in range(X):
        v0, v1, v2, dif = vel_ref[x], vel_ref[X + x], vel_ref[2 * X + x], dif_ref[x]
        for f in range(F):
            row = f * X + x
            middle = u_ref[row]
            x_plus = u_ref[row + 1] if x < X - 1 else 0.0
            x_minus = u_ref[row - 1] if x > 0 else 0.0
            y_plus = jnp.concatenate([middle[1:4], zero_row], axis=0)
            y_minus = jnp.concatenate([zero_row, middle[0:3]], axis=0)
            z_plus = jnp.where(not_last, pltpu.roll(middle, 2047, 1), 0.0)
            z_minus = jnp.where(not_first, pltpu.roll(middle, 1, 1), 0.0)
            carried = v0 * (x_plus - x_minus) + v1 * (y_plus - y_minus) + v2 * (z_plus - z_minus)
            spread = x_plus + x_minus + y_plus + y_minus + z_plus + z_minus - 6.0 * middle
            part_ref[row] = middle - 0.5 * carried + dif * spread


def outer_kernel(last, place, part_ref, rxa, rxb, rya, ryb, vel_ref, dif_ref, new_ref, *outs):
    gx, gy = place[0], place[1]
    odd_x, odd_y = gx % 2 == 1, gy % 2 == 1
    y_at = lax.broadcasted_iota(jnp.int32, (4, 2048), 0)
    up_on = (y_at == 3) & (gy != 15)
    down_on = (y_at == 0) & (gy != 0)
    for x in range(X):
        v0, v1, dif = vel_ref[x], vel_ref[X + x], dif_ref[x]
        up = jnp.where(up_on, dif - 0.5 * v1, 0.0)
        down = jnp.where(down_on, dif + 0.5 * v1, 0.0)
        side = None
        if x == X - 1:
            side = jnp.where(gx == 7, 0.0, dif - 0.5 * v0)
        if x == 0:
            side = jnp.where(gx == 0, 0.0, dif + 0.5 * v0)
        from_a = jnp.where(odd_y, down, up)
        from_b = jnp.where(odd_y, up, down)
        for f in range(F):
            row = f * X + x
            new = part_ref[row] + rya[f, x : x + 1, :] * from_a + ryb[f, x : x + 1, :] * from_b
            if x == X - 1:
                new = new + jnp.where(odd_x, rxb[f], rxa[f]) * side
            if x == 0:
                new = new + jnp.where(odd_x, rxa[f], rxb[f]) * side
            new_ref[row] = new
    get = lambda row: new_ref[row]
    if last:
        pack_slabs(get, outs[0])
    else:
        write_edges(get, odd_x, odd_y, *outs)


EDGES = [((F, X, 2048), F32)] * 4
SLABS = ((16, 2, 2 * F * X, Z), F32)


def exchange(edges):
    def pairs(n, second):
        partner = lambda i: (i ^ 1) if not second else ((i + 1) if i % 2 else (i - 1)) % n
        return [(i, partner(i)) for i in range(n)]

    xa, xb, ya, yb = edges
    return (
        lax.ppermute(xa, "gx", pairs(8, False)),
        lax.ppermute(xb, "gx", pairs(8, True)),
        lax.ppermute(ya, "gy", pairs(16, False)),
        lax.ppermute(yb, "gy", pairs(16, True)),
    )


def patch_rows(slabs_ref, anchor, out_ref):
    out_ref[...] = jnp.zeros_like(out_ref)
    for k in range(PY):
        y = anchor + k
        both = slabs_ref[y // 2]
        rows = jnp.where(y % 2 == 1, both[F * X :], both[: F * X])
        out_ref[0 : F * X, k * Z : (k + 1) * Z] = rows


def z_shifted(cells, dz, lane):
    if dz == 0:
        return cells
    moved = pltpu.roll(cells, (-dz) % Z, 1)
    return jnp.where(lane == (Z - 1 if dz > 0 else 0), 0.0, moved)


def fill_taps(cells, out_ref, sign):
    rows = cells.shape[0]
    lane = lax.broadcasted_iota(jnp.int32, (rows, Z), 1)
    zero = jnp.zeros((rows, Z), F32)
    shifted = [[z_shifted(cells[:, k * Z : (k + 1) * Z], sign * (dz - 1), lane) for dz in range(3)] for k in range(PY)]
    for k in range(PY):
        parts = []
        for dy in range(3):
            at = k + sign * (dy - 1)
            for dz in range(3):
                parts.append(shifted[at][dz] if 0 <= at < PY else zero)
        parts.append(jnp.zeros((TALL - TAPS * rows, Z), F32))
        out_ref[:, k * Z : (k + 1) * Z] = jnp.concatenate(parts, axis=0).astype(BF)


def fill_z(cells, k, out_ref, sign):
    lane = lax.broadcasted_iota(jnp.int32, cells.shape, 1)
    for dz in range(3):
        moved = z_shifted(cells, sign * (dz - 1), lane)
        out_ref[dz * 128 : (dz + 1) * 128, (k + 1) * Z : (k + 2) * Z] = moved.astype(BF)


def clear_ends(ref):
    ref[:, 0:Z] = jnp.zeros((ref.shape[0], Z), ref.dtype)
    ref[:, (PY + 1) * Z :] = jnp.zeros((ref.shape[0], Z), ref.dtype)


def dot(a, b):
    return jnp.dot(a, b, preferred_element_type=F32)


def dot_t(a, b):
    return lax.dot_general(a, b, (((1,), (1,)), ((), ())), preferred_element_type=F32)


def activate(y):
    sig = 1.0 / (1.0 + jnp.exp(-y))
    return y * sig, sig * (1.0 + y * (1.0 - sig))


def band_rows(w_ref, flip, out_ref):
    out_ref[...] = jnp.zeros_like(out_ref)
    zero = jnp.zeros((1, C), F32)
    for t in range(TAPS):
        for f in range(F):
            for to in range(X):
                parts = []
                for x in range(X):
                    dx = x - to + 1 if flip else to - x + 1
                    parts.append(w_ref[(f * 3 + dx) * 3 + t // 3, t % 3 : t % 3 + 1, :] if 0 <= dx < 3 else zero)
                out_ref[pl.ds(t * ROWS + f * X + to, 1), :] = jnp.concatenate(parts, axis=1)


def prepare_kernel(*refs):
    params, outs, rows_ref, held, sems = refs[:6], refs[6:12], refs[12], refs[13:19], refs[19]
    w1_ref, w2_ref, w3_ref, b1_ref, b2_ref, b3_ref = held
    w1_out, fwd_ref, bwd_ref, w3_out, w3_turned, bias_ref = outs
    copies = [pltpu.make_async_copy(params[n], held[n], sems.at[n]) for n in range(6)]
    for copy in copies:
        copy.start()
    for copy in copies:
        copy.wait()
    band_rows(w1_ref, False, rows_ref)
    w1_out[...] = rows_ref[...].T[:, 0:TALL].astype(BF)
    band_rows(w3_ref, True, rows_ref)
    w3_out[...] = rows_ref[0:TALL].astype(BF)
    w3_turned[...] = rows_ref[...].T[:, 0:TALL].astype(BF)
    zero = jnp.zeros((C, C), F32)
    for dy in range(3):
        for dz in range(3):
            rows = []
            for xo in range(X):
                parts = []
                for xi in range(X):
                    dx = xi - xo + 1
                    parts.append(w2_ref[dx * 9 + dy * 3 + dz] if 0 <= dx < 3 else zero)
                rows.append(jnp.concatenate(parts, axis=1))
            block = jnp.concatenate(rows, axis=0)
            fwd_ref[dy, :, dz * 128 : (dz + 1) * 128] = block.astype(BF)
            bwd_ref[dy, :, dz * 128 : (dz + 1) * 128] = block.T.astype(BF)
    lane = lax.broadcasted_iota(jnp.int32, (1, 128), 1)
    third = jnp.zeros((1, 128), F32)
    for f in range(F):
        third = jnp.where(lane // X == f, b3_ref[:, f : f + 1], third)
    rows = [jnp.concatenate([b1_ref[...]] * X, axis=1), jnp.concatenate([b2_ref[...]] * X, axis=1), third]
    bias_ref[...] = jnp.concatenate(rows + [jnp.zeros((125, 128), F32)], axis=0).T


PARTS = 80
AT = {"sum": (0, PARTS), "first": (80, 32), "a1": (112, 128), "a2": (240, 128), "d1": (368, 128), "d2": (496, 128)}
KEPT = ((2, 16384, PY * Z), BF)
NAMES = ("sum", "d2", "a2", "a1", "first", "d1")
HELD = [pltpu.VMEM((2, AT[name][1], PY * Z), BF) for name in NAMES] + [pltpu.SemaphoreType.DMA((len(NAMES), 2))]


def transfers(kept_ref, held, sems):
    out = {}
    for n, name in enumerate(NAMES):
        for p in range(2):
            start, size = AT[name]
            out[name, p] = (kept_ref.at[p, pl.ds(start, size)], held[n].at[p], sems.at[n, p])
    return out


def forward_kernel(
    anchors, slabs_ref, w1_ref, w2_ref, w3_ref, bias_ref, kept_ref, *refs,
):
    b1, b2, b3 = bias_ref[:, 0:1], bias_ref[:, 1:2], bias_ref[0:ROWS, 2:3]
    held, sems, (first_ref, taps_ref, a1_ref) = refs[: len(NAMES)], refs[len(NAMES)], refs[len(NAMES) + 1 :]
    sum_ref, d2_ref, a2_ref, a1_kept, cells_ref, d1_ref = held
    plan = transfers(kept_ref, held, sems)
    copies = []

    def keep(name, p):
        to, of, sem = plan[name, p]
        copies.append(pltpu.make_async_copy(of, to, sem))
        copies[-1].start()

    for p in range(2):
        patch_rows(slabs_ref, anchors[p], first_ref.at[p])
        cells_ref[p] = jnp.concatenate([first_ref[p], jnp.zeros((32 - ROWS, PY * Z), F32)], axis=0).astype(BF)
        keep("first", p)
        fill_taps(first_ref[p], taps_ref.at[p], 1)
        y1 = dot(w1_ref[...], taps_ref[p])
        act, slope = activate(y1 + b1)
        d1_ref[p] = slope.astype(BF)
        keep("d1", p)
        a1_kept[p] = act.astype(BF)
        keep("a1", p)
        clear_ends(a1_ref.at[p])
        for k in range(PY):
            fill_z(act[:, k * Z : (k + 1) * Z], k, a1_ref.at[p], 1)
        y2 = b2 + dot(w2_ref[0], a1_ref[p, :, 0 : PY * Z])
        for dy in range(1, 3):
            y2 = y2 + dot(w2_ref[dy], a1_ref[p, :, dy * Z : (dy + PY) * Z])
        act, slope = activate(y2)
        d2_ref[p] = slope.astype(BF)
        a2_ref[p] = act.astype(BF)
        keep("d2", p)
        keep("a2", p)
        terms = dot(w3_ref[...], a2_ref[p])
        lane = lax.broadcasted_iota(jnp.int32, (ROWS, Z), 1)
        for k in range(PY):
            out = b3 + first_ref[p, :, k * Z : (k + 1) * Z]
            for dz in range(3):
                part = None
                for dy in range(3):
                    at = k + dy - 1
                    if 0 <= at < PY:
                        t = (dy * 3 + dz) * ROWS
                        term = terms[t : t + ROWS, at * Z : (at + 1) * Z]
                        part = term if part is None else part + term
                out = out + z_shifted(part, dz - 1, lane)
            high = out.astype(BF).astype(F32)
            mid = (out - high).astype(BF).astype(F32)
            low = out - high - mid
            pad = jnp.zeros((PARTS - 3 * ROWS, Z), F32)
            sum_ref[p, :, k * Z : (k + 1) * Z] = jnp.concatenate([high, mid, low, pad], axis=0).astype(BF)
        keep("sum", p)
    for copy in copies:
        copy.wait()


def half_of(place):
    gx, gy = place[0], place[1]
    return (gx // 2 + gx + gy // 4 + gy) % 2


def band_sum(full):
    lane = lax.broadcasted_iota(jnp.int32, (C, 256), 1)
    total = None
    for x in range(X):
        block = full[x * C : (x + 1) * C]
        block = jnp.concatenate([block, jnp.zeros((C, 256 - TALL), F32)], axis=1)
        moved = pltpu.roll(block, (1 - x) % 256, 1)
        e = lane % 4
        ok = (e < 3) & (x + e - 1 >= 0) & (x + e - 1 < X) & (lane < TAPS * ROWS)
        moved = jnp.where(ok, moved, 0.0)
        total = moved if total is None else total + moved
    out = None
    for f in range(F):
        part = jnp.where((lane % ROWS) // 4 == f, total, 0.0)
        part = pltpu.roll(part, (256 - f) % 256, 1)
        out = part if out is None else out + part
    return out


def backward_kernel(place, anchors, count, slabs_ref, w2_ref, w3_ref, kept_ref, keep_ref, send_ref, *refs):
    held, sems = refs[: len(NAMES)], refs[len(NAMES)]
    last_ref, taps_ref, a1_ref, g_ref, b_ref, grads_ref = refs[len(NAMES) + 1 :]
    sum_ref, d2_ref, a2_ref, a1_kept, cells_ref, d1_ref = held
    plan = transfers(kept_ref, held, sems)
    copies = {key: pltpu.make_async_copy(of, to, sem) for key, (of, to, sem) in plan.items()}
    for p in range(2):
        for name in NAMES:
            copies[name, p].start()
    db1 = jnp.zeros((128, 1), F32)
    db2 = jnp.zeros((128, 1), F32)
    db3 = jnp.zeros((ROWS, 1), F32)
    loss = jnp.zeros((ROWS, 1), F32)
    dw1 = jnp.zeros((128, TALL), F32)
    dw3 = jnp.zeros((128, TALL), F32)
    dw2 = [jnp.zeros((128, 384), F32) for _ in range(3)]
    for p in range(2):
        copies["sum", p].wait()
    for p in range(2):
        live = jnp.where(p < count[0], 1.0, 0.0).astype(F32)
        patch_rows(slabs_ref, anchors[p], last_ref.at[p])
        parts = sum_ref[p].astype(F32)
        err = parts[0:ROWS] + parts[ROWS : 2 * ROWS] + parts[2 * ROWS : 3 * ROWS] - last_ref[p]
        loss = loss + live * jnp.sum(err * err, axis=1, keepdims=True)
        err = err * (live * (2.0 / CELLS))
        db3 = db3 + jnp.sum(err, axis=1, keepdims=True)
        fill_taps(err, g_ref.at[p], -1)
    for name in NAMES[1:]:
        for p in range(2):
            copies[name, p].wait()
    for p in range(2):
        da2 = dot(w3_ref[...], g_ref[p])
        dw3 = dw3 + dot_t(a2_ref[p], g_ref[p])
        dy2 = da2 * d2_ref[p].astype(F32)
        db2 = db2 + jnp.sum(dy2, axis=1, keepdims=True)
        clear_ends(b_ref.at[p])
        for k in range(PY):
            fill_z(dy2[:, k * Z : (k + 1) * Z], k, b_ref.at[p], -1)
        clear_ends(a1_ref.at[p])
        for k in range(PY):
            fill_z(a1_kept[p, :, k * Z : (k + 1) * Z].astype(F32), k, a1_ref.at[p], 1)
        fill_taps(cells_ref[p].astype(F32)[0:ROWS], taps_ref.at[p], 1)
        middle = b_ref[p, 128:256, Z : (PY + 1) * Z]
        da1 = None
        for dy in range(3):
            dw2[dy] = dw2[dy] + dot_t(middle, a1_ref[p, :, dy * Z : (dy + PY) * Z])
            term = dot(w2_ref[dy], b_ref[p, :, (2 - dy) * Z : (2 - dy + PY) * Z])
            da1 = term if da1 is None else da1 + term
        dy1 = da1 * d1_ref[p].astype(F32)
        db1 = db1 + jnp.sum(dy1, axis=1, keepdims=True)
        dw1 = dw1 + dot_t(dy1.astype(BF), taps_ref[p])

    lane = lax.broadcasted_iota(jnp.int32, (C, 128), 1)
    small1, small3 = band_sum(dw1), band_sum(dw3)
    fold = lambda v: v[0:C] + v[C : 2 * C] + v[2 * C : 3 * C] + v[3 * C : 4 * C]
    by_field = [jnp.sum(db3[f * X : (f + 1) * X], axis=0, keepdims=True) for f in range(F)]
    db3 = jnp.concatenate(by_field + [jnp.zeros((C - F, 1), F32)], axis=0)
    loss = jnp.sum(loss, axis=0, keepdims=True) * (1.0 / CELLS)
    extras = {0: (fold(db1), fold(db2)), 1: (db3, loss), 2: (jnp.full((C, 1), 1.0, F32) * count[0].astype(F32), None)}
    for t in range(TAPS):
        dy, dz = t // 3, t % 3
        total = jnp.zeros((C, 128), F32)
        for xo in range(X):
            block = dw2[dy][xo * C : (xo + 1) * C, dz * 128 : (dz + 1) * 128]
            moved = pltpu.roll(block, ((1 - xo) * C) % 128, 1)
            dx = lane // C
            ok = (dx < 3) & (xo + dx - 1 >= 0) & (xo + dx - 1 < X)
            total = total + jnp.where(ok, moved, 0.0)
        one = pltpu.roll(small1, (96 - ROWS * t) % 256, 1)[:, 0:128]
        three = pltpu.roll(small3, (111 - ROWS * t) % 256, 1)[:, 0:128]
        total = jnp.where((lane >= 96) & (lane < 111), one, total)
        total = jnp.where((lane >= 111) & (lane < 126), three, total)
        if t in extras:
            a, b = extras[t]
            total = jnp.where(lane == 126, a, total)
            if b is not None:
                total = jnp.where(lane == 127, b, total)
        grads_ref[t * C : (t + 1) * C] = total
    second = half_of(place) == 1
    low, high = grads_ref[0:HALF], grads_ref[HALF:]
    keep_ref[...] = jnp.where(second, high, low)
    send_ref[...] = jnp.where(second, low, high)


def finish_kernel(
    place, mine_ref, other_ref, g1_ref, gb1_ref, g2_ref, gb2_ref, g3_ref, gb3_ref, loss_ref, grads_ref
):
    second = half_of(place) == 1
    at = jnp.where(second, HALF, 0)
    grads_ref[pl.ds(pl.multiple_of(at, 8), HALF)] = mine_ref[...]
    grads_ref[pl.ds(pl.multiple_of(HALF - at, 8), HALF)] = other_ref[...]
    rows = lambda t: grads_ref[t * C : (t + 1) * C]
    scale = 1.0 / rows(2)[0:1, 126:127]
    for t in range(TAPS):
        dy, dz = t // 3, t % 3
        block = rows(t) * scale
        for dx in range(3):
            g2_ref[dx * TAPS + t] = block[:, dx * C : (dx + 1) * C]
        turned = block.T
        for f in range(F):
            for dx in range(3):
                to = (f * 3 + dx) * 3 + dy
                at = 96 + f * 3 + dx
                g1_ref[to, dz : dz + 1, :] = turned[at : at + 1]
                at = 111 + f * 3 + 2 - dx
                g3_ref[to, dz : dz + 1, :] = turned[at : at + 1]
        if t == 0:
            gb1_ref[...] = turned[126:127]
            gb2_ref[...] = turned[127:128]
        if t == 1:
            gb3_ref[...] = turned[126:127, 0:F]
            loss_ref[...] = turned[127:128, 0:1]


def reduce_steps(order):
    def near(c):
        return c ^ 1

    def far(c):
        return 3 - c

    steps = []
    for n in range(6):
        pairs = []
        for gx in range(8):
            for gy in range(16):
                at = {"x": gx // 2, "y": gy // 4, "z": (gy // 2 % 2) * 2 + gx % 2}
                axis = order[n // 2]
                at[axis] = (near, far)[n % 2](at[axis])
                to = (at["x"] * 2 + at["z"] % 2) * 16 + at["y"] * 4 + (at["z"] // 2) * 2 + (gy + 1) % 2
                pairs.append((gx * 16 + gy, to))
        steps.append(pairs)
    return steps


def sum_all(keep, send):
    cores = [(i, i ^ 1) for i in range(16)]
    mine = keep + lax.ppermute(send, "gy", cores)
    parts = [mine[: HALF // 2], mine[HALF // 2 :]]
    for pairs in zip(reduce_steps("zyx"), reduce_steps("xzy")):
        moved = [lax.ppermute(part, ("gx", "gy"), p) for part, p in zip(parts, pairs)]
        parts = [part + m for part, m in zip(parts, moved)]
    mine = jnp.concatenate(parts)
    return mine, lax.ppermute(mine, "gy", cores)


def on_device(
    initial_fields, velocity, diffusivity, patch_anchor, patch_count,
    weight_one, bias_one, weight_two, bias_two, weight_three, bias_three,
):
    place = jnp.stack([lax.axis_index("gx"), lax.axis_index("gy")]).astype(jnp.int32)
    u = initial_fields.reshape(F * X, 4, 2048)
    vel = velocity.reshape(3 * X, 4, 2048)
    anchors = patch_anchor.reshape(2)
    count = patch_count.reshape(1)

    edges = call(edges_kernel, EDGES, ins=[SMEM, VMEM], nbytes=1_000_000)(place, u)
    params = (
        jnp.transpose(weight_one, (1, 2, 3, 4, 0)).reshape(45, 3, C),
        jnp.transpose(weight_two, (2, 3, 4, 0, 1)).reshape(27, C, C),
        jnp.transpose(weight_three, (0, 2, 3, 4, 1)).reshape(45, 3, C),
        bias_one.reshape(1, C),
        bias_two.reshape(1, C),
        bias_three.reshape(1, F),
    )
    (slabs,) = call(slabs_kernel, [SLABS], ins=[VMEM], nbytes=1_500_000)(u)
    first_slabs = lax.all_to_all(slabs, "gy", 0, 0, tiled=True).reshape(32, 2 * F * X, Z)
    w1_band, w2_fwd, w2_bwd, w3_band, w3_turned, biases = call(
        prepare_kernel,
        [
            ((128, TALL), BF),
            ((3, 128, 384), BF),
            ((3, 128, 384), BF),
            ((TALL, 128), BF),
            ((128, TALL), BF),
            ((128, 128), F32),
        ],
        scratch=[pltpu.VMEM((256, 128), F32)]
        + [pltpu.VMEM(p.shape, F32) for p in params]
        + [pltpu.SemaphoreType.DMA((len(params),))],
        ins=[ANY] * len(params),
        nbytes=1_000_000,
    )(*params)

    for step in range(STEPS):
        last = step == STEPS - 1
        outs = [((F * X, 4, 2048), F32)] + ([SLABS] if last else EDGES)
        received = exchange(edges)
        (part,) = call(inner_kernel, [((F * X, 4, 2048), F32)], ins=[VMEM] * 3, nbytes=4_000_000, flops=BESIDE)(u, vel, diffusivity)
        kernel = lambda *refs, last=last: outer_kernel(last, *refs)
        u, *edges = call(kernel, outs, ins=[SMEM] + [VMEM] * 7, nbytes=3_000_000, flops=BESIDE)(
            place, part, *received, vel, diffusivity
        )

    (kept,) = call(
        forward_kernel,
        [KEPT],
        scratch=HELD
        + [
            pltpu.VMEM((2, ROWS, PY * Z), F32),
            pltpu.VMEM((2, TALL, PY * Z), BF),
            pltpu.VMEM((2, 384, (PY + 2) * Z), BF),
        ],
        ins=[SMEM] + [VMEM] * 5,
        flops=2_000_000_000,
        nbytes=8_000_000,
        mib=24,
        out_space=HBM,
    )(anchors, first_slabs, w1_band, w2_fwd, w3_band, biases)

    last_slabs = lax.all_to_all(edges[0], "gy", 0, 0, tiled=True).reshape(32, 2 * F * X, Z)
    keep, send = call(
        backward_kernel,
        [((HALF, 128), F32)] * 2,
        scratch=HELD
        + [
            pltpu.VMEM((2, ROWS, PY * Z), F32),
            pltpu.VMEM((2, TALL, PY * Z), BF),
            pltpu.VMEM((2, 384, (PY + 2) * Z), BF),
            pltpu.VMEM((2, TALL, PY * Z), BF),
            pltpu.VMEM((2, 384, (PY + 2) * Z), BF),
            pltpu.VMEM((2 * HALF, 128), F32),
        ],
        ins=[SMEM] * 3 + [VMEM] * 3 + [HBM],
        flops=4_000_000_000,
        nbytes=10_000_000,
        mib=24,
    )(place, anchors, count, last_slabs, w2_bwd, w3_turned, kept)

    g1, gb1, g2, gb2, g3, gb3, loss = call(
        finish_kernel,
        [((45, 3, C), F32), ((1, C), F32), ((27, C, C), F32), ((1, C), F32), ((45, 3, C), F32), ((1, F), F32), ((1, 1), F32)],
        scratch=[pltpu.VMEM((2 * HALF, 128), F32)],
        ins=[SMEM, VMEM, VMEM],
        nbytes=1_000_000,
    )(place, *sum_all(keep, send))
    g1 = jnp.transpose(g1.reshape(F, 3, 3, 3, C), (4, 0, 1, 2, 3))
    g2 = jnp.transpose(g2.reshape(3, 3, 3, C, C), (3, 4, 0, 1, 2))
    g3 = jnp.transpose(g3.reshape(F, 3, 3, 3, C), (0, 4, 1, 2, 3))
    gb1, gb2, gb3, loss = gb1.reshape(C), gb2.reshape(C), gb3.reshape(F), loss.reshape(())
    return u.reshape(F, X, 4, 2048), g1, gb1, g2, gb2, g3, gb3, loss


def solution(mesh):
    return jax.shard_map(
        on_device,
        mesh=mesh,
        in_specs=(
            P(None, "gx", "gy", None),
            P(None, "gx", "gy", None),
            P("gx", "gy", None),
            P("gx", "gy", None),
            P("gx", "gy"),
            P(),
            P(),
            P(),
            P(),
            P(),
            P(),
        ),
        out_specs=(P(None, "gx", "gy", None), P(), P(), P(), P(), P(), P(), P()),
        check_vma=False,
    )
```

```python
import jax
import jax.numpy as jnp
from jax import lax
from jax.experimental import pallas as pl
from jax.experimental.pallas import tpu as pltpu
from jax.sharding import PartitionSpec as P

STEPS = 3
F = 5
C = 32
X = 4
PY = 8
Z = 128
ROWS = 24
HALF = 144
TAPS = 9
TALL = 224
CELLS = 20480.0
BF = jnp.bfloat16
F32 = jnp.float32
VMEM = pl.BlockSpec(memory_space=pltpu.VMEM)
SMEM = pl.BlockSpec(memory_space=pltpu.SMEM)
HBM = pl.BlockSpec(memory_space=pltpu.HBM)
ANY = pl.BlockSpec(memory_space=pl.ANY)
MIB = 1024 * 1024
BESIDE = 6_000_000_000


def call(kernel, outs, scratch=(), flops=0, nbytes=0, ins=(), mib=12, out_space=None):
    return pl.pallas_call(
        kernel,
        out_shape=[jax.ShapeDtypeStruct(s, d) for s, d in outs],
        in_specs=list(ins),
        out_specs=[out_space or VMEM] * len(outs),
        scratch_shapes=list(scratch),
        compiler_params=pltpu.CompilerParams(vmem_limit_bytes=mib * MIB),
        cost_estimate=pl.CostEstimate(flops=flops, bytes_accessed=nbytes, transcendentals=0),
    )


def pack_slabs(get, out_ref):
    for row in range(F * X):
        cells = get(row)
        for y in range(4):
            for j in range(16):
                out_ref[j, y // 2, pl.ds((y % 2) * F * X + row, 1), :] = cells[y : y + 1, j * Z : (j + 1) * Z]


def write_edges(get, odd_x, odd_y, xa_ref, xb_ref, ya_ref, yb_ref):
    for f in range(F):
        head, tail = get(f * X), get(f * X + X - 1)
        xa_ref[f] = jnp.where(odd_x, head, tail)
        xb_ref[f] = jnp.where(odd_x, tail, head)
    for row in range(F * X):
        cells = get(row)
        head, tail = cells[0:1], cells[3:4]
        f, x = row // X, row % X
        ya_ref[f, x : x + 1, :] = jnp.where(odd_y, head, tail)
        yb_ref[f, x : x + 1, :] = jnp.where(odd_y, tail, head)


def edges_kernel(place, u_ref, xa_ref, xb_ref, ya_ref, yb_ref):
    get = lambda row: u_ref[row]
    write_edges(get, place[0] % 2 == 1, place[1] % 2 == 1, xa_ref, xb_ref, ya_ref, yb_ref)


def slabs_kernel(u_ref, slabs_ref):
    pack_slabs(lambda row: u_ref[row], slabs_ref)


def inner_kernel(u_ref, vel_ref, dif_ref, part_ref):
    lane = lax.broadcasted_iota(jnp.int32, (4, 2048), 1)
    not_first, not_last = lane > 0, lane < 2047
    zero_row = jnp.zeros((1, 2048), F32)
    for x in range(X):
        v0, v1, v2, dif = vel_ref[x], vel_ref[X + x], vel_ref[2 * X + x], dif_ref[x]
        for f in range(F):
            row = f * X + x
            middle = u_ref[row]
            x_plus = u_ref[row + 1] if x < X - 1 else 0.0
            x_minus = u_ref[row - 1] if x > 0 else 0.0
            y_plus = jnp.concatenate([middle[1:4], zero_row], axis=0)
            y_minus = jnp.concatenate([zero_row, middle[0:3]], axis=0)
            z_plus = jnp.where(not_last, pltpu.roll(middle, 2047, 1), 0.0)
            z_minus = jnp.where(not_first, pltpu.roll(middle, 1, 1), 0.0)
            carried = v0 * (x_plus - x_minus) + v1 * (y_plus - y_minus) + v2 * (z_plus - z_minus)
            spread = x_plus + x_minus + y_plus + y_minus + z_plus + z_minus - 6.0 * middle
            part_ref[row] = middle - 0.5 * carried + dif * spread


def outer_kernel(last, place, part_ref, *refs):
    rxa, rxb, rya, ryb = refs[2:4] + refs[0:2] if last else refs[0:4]
    vel_ref, dif_ref, new_ref, *outs = refs[4:]
    gx, gy = place[0], place[1]
    odd_x, odd_y = gx % 2 == 1, gy % 2 == 1
    y_at = lax.broadcasted_iota(jnp.int32, (4, 2048), 0)
    up_on = (y_at == 3) & (gy != 15)
    down_on = (y_at == 0) & (gy != 0)
    for x in range(X):
        v0, v1, dif = vel_ref[x], vel_ref[X + x], dif_ref[x]
        up = jnp.where(up_on, dif - 0.5 * v1, 0.0)
        down = jnp.where(down_on, dif + 0.5 * v1, 0.0)
        side = None
        if x == X - 1:
            side = jnp.where(gx == 7, 0.0, dif - 0.5 * v0)
        if x == 0:
            side = jnp.where(gx == 0, 0.0, dif + 0.5 * v0)
        from_a = jnp.where(odd_y, down, up)
        from_b = jnp.where(odd_y, up, down)
        for f in range(F):
            row = f * X + x
            new = part_ref[row] + rya[f, x : x + 1, :] * from_a + ryb[f, x : x + 1, :] * from_b
            if x == X - 1:
                new = new + jnp.where(odd_x, rxb[f], rxa[f]) * side
            if x == 0:
                new = new + jnp.where(odd_x, rxa[f], rxb[f]) * side
            new_ref[row] = new
    get = lambda row: new_ref[row]
    if last:
        pack_slabs(get, outs[0])
    else:
        write_edges(get, odd_x, odd_y, *outs)


EDGES = [((F, X, 2048), F32)] * 4
SLABS = ((16, 2, 2 * F * X, Z), F32)


def exchange(edges, y_first):
    def pairs(n, second):
        partner = lambda i: (i ^ 1) if not second else ((i + 1) if i % 2 else (i - 1)) % n
        return [(i, partner(i)) for i in range(n)]

    xa, xb, ya, yb = edges
    along_x = lambda: [lax.ppermute(xa, "gx", pairs(8, False)), lax.ppermute(xb, "gx", pairs(8, True))]
    along_y = lambda: [lax.ppermute(ya, "gy", pairs(16, False)), lax.ppermute(yb, "gy", pairs(16, True))]
    return along_y() + along_x() if y_first else along_x() + along_y()


def patch_rows(slabs_ref, anchor, out_ref):
    out_ref[...] = jnp.zeros_like(out_ref)
    for k in range(PY):
        y = anchor + k
        both = slabs_ref[y // 2]
        rows = jnp.where(y % 2 == 1, both[F * X :], both[: F * X])
        out_ref[0 : F * X, k * Z : (k + 1) * Z] = rows


def z_shifted(cells, dz, lane):
    if dz == 0:
        return cells
    moved = pltpu.roll(cells, (-dz) % Z, 1)
    return jnp.where(lane == (Z - 1 if dz > 0 else 0), 0.0, moved)


def fill_taps(cells, out_ref, sign):
    rows = cells.shape[0]
    lane = lax.broadcasted_iota(jnp.int32, (rows, Z), 1)
    zero = jnp.zeros((rows, Z), F32)
    shifted = [[z_shifted(cells[:, k * Z : (k + 1) * Z], sign * (dz - 1), lane) for dz in range(3)] for k in range(PY)]
    for k in range(PY):
        parts = []
        for dy in range(3):
            at = k + sign * (dy - 1)
            for dz in range(3):
                parts.append(shifted[at][dz] if 0 <= at < PY else zero)
        parts.append(jnp.zeros((TALL - TAPS * rows, Z), F32))
        out_ref[:, k * Z : (k + 1) * Z] = jnp.concatenate(parts, axis=0).astype(BF)


def fill_z(cells, k, out_ref, sign):
    lane = lax.broadcasted_iota(jnp.int32, cells.shape, 1)
    for dz in range(3):
        moved = z_shifted(cells, sign * (dz - 1), lane)
        out_ref[dz * 128 : (dz + 1) * 128, (k + 1) * Z : (k + 2) * Z] = moved.astype(BF)


def clear_ends(ref):
    ref[:, 0:Z] = jnp.zeros((ref.shape[0], Z), ref.dtype)
    ref[:, (PY + 1) * Z :] = jnp.zeros((ref.shape[0], Z), ref.dtype)


def dot(a, b):
    return jnp.dot(a, b, preferred_element_type=F32)


def dot_t(a, b):
    return lax.dot_general(a, b, (((1,), (1,)), ((), ())), preferred_element_type=F32)


def activate(y):
    sig = 1.0 / (1.0 + jnp.exp(-y))
    return y * sig, sig * (1.0 + y * (1.0 - sig))


def band_rows(w_ref, flip, out_ref):
    out_ref[...] = jnp.zeros_like(out_ref)
    zero = jnp.zeros((1, C), F32)
    for t in range(TAPS):
        for f in range(F):
            for to in range(X):
                parts = []
                for x in range(X):
                    dx = x - to + 1 if flip else to - x + 1
                    parts.append(w_ref[(f * 3 + dx) * 3 + t // 3, t % 3 : t % 3 + 1, :] if 0 <= dx < 3 else zero)
                out_ref[pl.ds(t * ROWS + f * X + to, 1), :] = jnp.concatenate(parts, axis=1)


def prepare_kernel(*refs):
    params, outs, rows_ref, held, sems = refs[:6], refs[6:12], refs[12], refs[13:19], refs[19]
    w1_ref, w2_ref, w3_ref, b1_ref, b2_ref, b3_ref = held
    w1_out, fwd_ref, bwd_ref, w3_out, w3_turned, bias_ref = outs
    copies = [pltpu.make_async_copy(params[n], held[n], sems.at[n]) for n in range(6)]
    for copy in copies:
        copy.start()
    for copy in copies:
        copy.wait()
    band_rows(w1_ref, False, rows_ref)
    w1_out[...] = rows_ref[...].T[:, 0:TALL].astype(BF)
    band_rows(w3_ref, True, rows_ref)
    w3_out[...] = rows_ref[0:TALL].astype(BF)
    w3_turned[...] = rows_ref[...].T[:, 0:TALL].astype(BF)
    zero = jnp.zeros((C, C), F32)
    for dy in range(3):
        for dz in range(3):
            rows = []
            for xo in range(X):
                parts = []
                for xi in range(X):
                    dx = xi - xo + 1
                    parts.append(w2_ref[dx * 9 + dy * 3 + dz] if 0 <= dx < 3 else zero)
                rows.append(jnp.concatenate(parts, axis=1))
            block = jnp.concatenate(rows, axis=0)
            fwd_ref[dy, :, dz * 128 : (dz + 1) * 128] = block.astype(BF)
            bwd_ref[dy, :, dz * 128 : (dz + 1) * 128] = block.T.astype(BF)
    lane = lax.broadcasted_iota(jnp.int32, (1, 128), 1)
    third = jnp.zeros((1, 128), F32)
    for f in range(F):
        third = jnp.where(lane // X == f, b3_ref[:, f : f + 1], third)
    rows = [jnp.concatenate([b1_ref[...]] * X, axis=1), jnp.concatenate([b2_ref[...]] * X, axis=1), third]
    bias_ref[...] = jnp.concatenate(rows + [jnp.zeros((125, 128), F32)], axis=0).T


PARTS = 80
AT = {"sum": (0, PARTS), "first": (80, 32), "a1": (112, 128), "a2": (240, 128), "d1": (368, 128), "d2": (496, 128)}
KEPT = ((2, 16384, PY * Z), BF)
NAMES = ("sum", "d2", "a2", "a1", "first", "d1")
HELD = [pltpu.VMEM((2, AT[name][1], PY * Z), BF) for name in NAMES] + [pltpu.SemaphoreType.DMA((len(NAMES), 2))]


def transfers(kept_ref, held, sems):
    out = {}
    for n, name in enumerate(NAMES):
        for p in range(2):
            start, size = AT[name]
            out[name, p] = (kept_ref.at[p, pl.ds(start, size)], held[n].at[p], sems.at[n, p])
    return out


def forward_kernel(
    anchors, slabs_ref, w1_ref, w2_ref, w3_ref, bias_ref, kept_ref, *refs,
):
    b1, b2, b3 = bias_ref[:, 0:1], bias_ref[:, 1:2], bias_ref[0:ROWS, 2:3]
    held, sems, (first_ref, taps_ref, a1_ref) = refs[: len(NAMES)], refs[len(NAMES)], refs[len(NAMES) + 1 :]
    sum_ref, d2_ref, a2_ref, a1_kept, cells_ref, d1_ref = held
    plan = transfers(kept_ref, held, sems)
    copies = []

    def keep(name, p):
        to, of, sem = plan[name, p]
        copies.append(pltpu.make_async_copy(of, to, sem))
        copies[-1].start()

    for p in range(2):
        patch_rows(slabs_ref, anchors[p], first_ref.at[p])
        cells_ref[p] = jnp.concatenate([first_ref[p], jnp.zeros((32 - ROWS, PY * Z), F32)], axis=0).astype(BF)
        keep("first", p)
        fill_taps(first_ref[p], taps_ref.at[p], 1)
        y1 = dot(w1_ref[...], taps_ref[p])
        act, slope = activate(y1 + b1)
        d1_ref[p] = slope.astype(BF)
        keep("d1", p)
        a1_kept[p] = act.astype(BF)
        keep("a1", p)
        clear_ends(a1_ref.at[p])
        for k in range(PY):
            fill_z(act[:, k * Z : (k + 1) * Z], k, a1_ref.at[p], 1)
        y2 = b2 + dot(w2_ref[0], a1_ref[p, :, 0 : PY * Z])
        for dy in range(1, 3):
            y2 = y2 + dot(w2_ref[dy], a1_ref[p, :, dy * Z : (dy + PY) * Z])
        act, slope = activate(y2)
        d2_ref[p] = slope.astype(BF)
        a2_ref[p] = act.astype(BF)
        keep("d2", p)
        keep("a2", p)
        terms = dot(w3_ref[...], a2_ref[p])
        lane = lax.broadcasted_iota(jnp.int32, (ROWS, Z), 1)
        for k in range(PY):
            out = b3 + first_ref[p, :, k * Z : (k + 1) * Z]
            for dz in range(3):
                part = None
                for dy in range(3):
                    at = k + dy - 1
                    if 0 <= at < PY:
                        t = (dy * 3 + dz) * ROWS
                        term = terms[t : t + ROWS, at * Z : (at + 1) * Z]
                        part = term if part is None else part + term
                out = out + z_shifted(part, dz - 1, lane)
            high = out.astype(BF).astype(F32)
            mid = (out - high).astype(BF).astype(F32)
            low = out - high - mid
            pad = jnp.zeros((PARTS - 3 * ROWS, Z), F32)
            sum_ref[p, :, k * Z : (k + 1) * Z] = jnp.concatenate([high, mid, low, pad], axis=0).astype(BF)
        keep("sum", p)
    for copy in copies:
        copy.wait()


def half_of(place):
    gx, gy = place[0], place[1]
    return (gx // 2 + gx + gy // 4 + gy) % 2


def band_sum(full):
    lane = lax.broadcasted_iota(jnp.int32, (C, 256), 1)
    total = None
    for x in range(X):
        block = full[x * C : (x + 1) * C]
        block = jnp.concatenate([block, jnp.zeros((C, 256 - TALL), F32)], axis=1)
        moved = pltpu.roll(block, (1 - x) % 256, 1)
        e = lane % 4
        ok = (e < 3) & (x + e - 1 >= 0) & (x + e - 1 < X) & (lane < TAPS * ROWS)
        moved = jnp.where(ok, moved, 0.0)
        total = moved if total is None else total + moved
    out = None
    for f in range(F):
        part = jnp.where((lane % ROWS) // 4 == f, total, 0.0)
        part = pltpu.roll(part, (256 - f) % 256, 1)
        out = part if out is None else out + part
    return out


def backward_kernel(place, anchors, count, slabs_ref, w2_ref, w3_ref, kept_ref, keep_ref, send_ref, *refs):
    held, sems = refs[: len(NAMES)], refs[len(NAMES)]
    last_ref, taps_ref, a1_ref, g_ref, b_ref, grads_ref = refs[len(NAMES) + 1 :]
    sum_ref, d2_ref, a2_ref, a1_kept, cells_ref, d1_ref = held
    plan = transfers(kept_ref, held, sems)
    copies = {key: pltpu.make_async_copy(of, to, sem) for key, (of, to, sem) in plan.items()}
    for p in range(2):
        for name in NAMES:
            copies[name, p].start()
    db1 = jnp.zeros((128, 1), F32)
    db2 = jnp.zeros((128, 1), F32)
    db3 = jnp.zeros((ROWS, 1), F32)
    loss = jnp.zeros((ROWS, 1), F32)
    dw1 = jnp.zeros((128, TALL), F32)
    dw3 = jnp.zeros((128, TALL), F32)
    dw2 = [jnp.zeros((128, 384), F32) for _ in range(3)]
    for p in range(2):
        copies["sum", p].wait()
    for p in range(2):
        live = jnp.where(p < count[0], 1.0, 0.0).astype(F32)
        patch_rows(slabs_ref, anchors[p], last_ref.at[p])
        parts = sum_ref[p].astype(F32)
        err = parts[0:ROWS] + parts[ROWS : 2 * ROWS] + parts[2 * ROWS : 3 * ROWS] - last_ref[p]
        loss = loss + live * jnp.sum(err * err, axis=1, keepdims=True)
        err = err * (live * (2.0 / CELLS))
        db3 = db3 + jnp.sum(err, axis=1, keepdims=True)
        fill_taps(err, g_ref.at[p], -1)
    for name in NAMES[1:]:
        for p in range(2):
            copies[name, p].wait()
    for p in range(2):
        da2 = dot(w3_ref[...], g_ref[p])
        dw3 = dw3 + dot_t(a2_ref[p], g_ref[p])
        dy2 = da2 * d2_ref[p].astype(F32)
        db2 = db2 + jnp.sum(dy2, axis=1, keepdims=True)
        clear_ends(b_ref.at[p])
        for k in range(PY):
            fill_z(dy2[:, k * Z : (k + 1) * Z], k, b_ref.at[p], -1)
        clear_ends(a1_ref.at[p])
        for k in range(PY):
            fill_z(a1_kept[p, :, k * Z : (k + 1) * Z].astype(F32), k, a1_ref.at[p], 1)
        fill_taps(cells_ref[p].astype(F32)[0:ROWS], taps_ref.at[p], 1)
        middle = b_ref[p, 128:256, Z : (PY + 1) * Z]
        da1 = None
        for dy in range(3):
            dw2[dy] = dw2[dy] + dot_t(middle, a1_ref[p, :, dy * Z : (dy + PY) * Z])
            term = dot(w2_ref[dy], b_ref[p, :, (2 - dy) * Z : (2 - dy + PY) * Z])
            da1 = term if da1 is None else da1 + term
        dy1 = da1 * d1_ref[p].astype(F32)
        db1 = db1 + jnp.sum(dy1, axis=1, keepdims=True)
        dw1 = dw1 + dot_t(dy1.astype(BF), taps_ref[p])

    lane = lax.broadcasted_iota(jnp.int32, (C, 128), 1)
    small1, small3 = band_sum(dw1), band_sum(dw3)
    fold = lambda v: v[0:C] + v[C : 2 * C] + v[2 * C : 3 * C] + v[3 * C : 4 * C]
    by_field = [jnp.sum(db3[f * X : (f + 1) * X], axis=0, keepdims=True) for f in range(F)]
    db3 = jnp.concatenate(by_field + [jnp.zeros((C - F, 1), F32)], axis=0)
    loss = jnp.sum(loss, axis=0, keepdims=True) * (1.0 / CELLS)
    extras = {0: (fold(db1), fold(db2)), 1: (db3, loss), 2: (jnp.full((C, 1), 1.0, F32) * count[0].astype(F32), None)}
    for t in range(TAPS):
        dy, dz = t // 3, t % 3
        total = jnp.zeros((C, 128), F32)
        for xo in range(X):
            block = dw2[dy][xo * C : (xo + 1) * C, dz * 128 : (dz + 1) * 128]
            moved = pltpu.roll(block, ((1 - xo) * C) % 128, 1)
            dx = lane // C
            ok = (dx < 3) & (xo + dx - 1 >= 0) & (xo + dx - 1 < X)
            total = total + jnp.where(ok, moved, 0.0)
        one = pltpu.roll(small1, (96 - ROWS * t) % 256, 1)[:, 0:128]
        three = pltpu.roll(small3, (111 - ROWS * t) % 256, 1)[:, 0:128]
        total = jnp.where((lane >= 96) & (lane < 111), one, total)
        total = jnp.where((lane >= 111) & (lane < 126), three, total)
        if t in extras:
            a, b = extras[t]
            total = jnp.where(lane == 126, a, total)
            if b is not None:
                total = jnp.where(lane == 127, b, total)
        grads_ref[t * C : (t + 1) * C] = total
    second = half_of(place) == 1
    low, high = grads_ref[0:HALF], grads_ref[HALF:]
    keep_ref[...] = jnp.where(second, high, low)
    send_ref[...] = jnp.where(second, low, high)


def finish_kernel(
    place, mine_ref, other_ref, g1_ref, gb1_ref, g2_ref, gb2_ref, g3_ref, gb3_ref, loss_ref, grads_ref
):
    second = half_of(place) == 1
    at = jnp.where(second, HALF, 0)
    grads_ref[pl.ds(pl.multiple_of(at, 8), HALF)] = mine_ref[...]
    grads_ref[pl.ds(pl.multiple_of(HALF - at, 8), HALF)] = other_ref[...]
    rows = lambda t: grads_ref[t * C : (t + 1) * C]
    scale = 1.0 / rows(2)[0:1, 126:127]
    for t in range(TAPS):
        dy, dz = t // 3, t % 3
        block = rows(t) * scale
        for dx in range(3):
            g2_ref[dx * TAPS + t] = block[:, dx * C : (dx + 1) * C]
        turned = block.T
        for f in range(F):
            for dx in range(3):
                to = (f * 3 + dx) * 3 + dy
                at = 96 + f * 3 + dx
                g1_ref[to, dz : dz + 1, :] = turned[at : at + 1]
                at = 111 + f * 3 + 2 - dx
                g3_ref[to, dz : dz + 1, :] = turned[at : at + 1]
        if t == 0:
            gb1_ref[...] = turned[126:127]
            gb2_ref[...] = turned[127:128]
        if t == 1:
            gb3_ref[...] = turned[126:127, 0:F]
            loss_ref[...] = turned[127:128, 0:1]


def reduce_steps(order):
    def near(c):
        return c ^ 1

    def far(c):
        return 3 - c

    steps = []
    for n in range(6):
        pairs = []
        for gx in range(8):
            for gy in range(16):
                at = {"x": gx // 2, "y": gy // 4, "z": (gy // 2 % 2) * 2 + gx % 2}
                axis = order[n // 2]
                at[axis] = (near, far)[n % 2](at[axis])
                to = (at["x"] * 2 + at["z"] % 2) * 16 + at["y"] * 4 + (at["z"] // 2) * 2 + (gy + 1) % 2
                pairs.append((gx * 16 + gy, to))
        steps.append(pairs)
    return steps


def sum_all(keep, send):
    cores = [(i, i ^ 1) for i in range(16)]
    mine = keep + lax.ppermute(send, "gy", cores)
    parts = [mine[: HALF // 2], mine[HALF // 2 :]]
    for pairs in zip(reduce_steps("zyx"), reduce_steps("xzy")):
        moved = [lax.ppermute(part, ("gx", "gy"), p) for part, p in zip(parts, pairs)]
        parts = [part + m for part, m in zip(parts, moved)]
    mine = jnp.concatenate(parts)
    return mine, lax.ppermute(mine, "gy", cores)


def on_device(
    initial_fields, velocity, diffusivity, patch_anchor, patch_count,
    weight_one, bias_one, weight_two, bias_two, weight_three, bias_three,
):
    place = jnp.stack([lax.axis_index("gx"), lax.axis_index("gy")]).astype(jnp.int32)
    u = initial_fields.reshape(F * X, 4, 2048)
    vel = velocity.reshape(3 * X, 4, 2048)
    anchors = patch_anchor.reshape(2)
    count = patch_count.reshape(1)

    edges = call(edges_kernel, EDGES, ins=[SMEM, VMEM], nbytes=1_000_000)(place, u)
    params = (
        jnp.transpose(weight_one, (1, 2, 3, 4, 0)).reshape(45, 3, C),
        jnp.transpose(weight_two, (2, 3, 4, 0, 1)).reshape(27, C, C),
        jnp.transpose(weight_three, (0, 2, 3, 4, 1)).reshape(45, 3, C),
        bias_one.reshape(1, C),
        bias_two.reshape(1, C),
        bias_three.reshape(1, F),
    )
    (slabs,) = call(slabs_kernel, [SLABS], ins=[VMEM], nbytes=1_500_000)(u)
    first_slabs = lax.all_to_all(slabs, "gy", 0, 0, tiled=True).reshape(32, 2 * F * X, Z)
    w1_band, w2_fwd, w2_bwd, w3_band, w3_turned, biases = call(
        prepare_kernel,
        [
            ((128, TALL), BF),
            ((3, 128, 384), BF),
            ((3, 128, 384), BF),
            ((TALL, 128), BF),
            ((128, TALL), BF),
            ((128, 128), F32),
        ],
        scratch=[pltpu.VMEM((256, 128), F32)]
        + [pltpu.VMEM(p.shape, F32) for p in params]
        + [pltpu.SemaphoreType.DMA((len(params),))],
        ins=[ANY] * len(params),
        nbytes=1_000_000,
    )(*params)

    for step in range(STEPS):
        last = step == STEPS - 1
        outs = [((F * X, 4, 2048), F32)] + ([SLABS] if last else EDGES)
        received = exchange(edges, last)
        (part,) = call(inner_kernel, [((F * X, 4, 2048), F32)], ins=[VMEM] * 3, nbytes=4_000_000, flops=BESIDE)(u, vel, diffusivity)
        kernel = lambda *refs, last=last: outer_kernel(last, *refs)
        u, *edges = call(kernel, outs, ins=[SMEM] + [VMEM] * 7, nbytes=3_000_000, flops=BESIDE)(
            place, part, *received, vel, diffusivity
        )

    (kept,) = call(
        forward_kernel,
        [KEPT],
        scratch=HELD
        + [
            pltpu.VMEM((2, ROWS, PY * Z), F32),
            pltpu.VMEM((2, TALL, PY * Z), BF),
            pltpu.VMEM((2, 384, (PY + 2) * Z), BF),
        ],
        ins=[SMEM] + [VMEM] * 5,
        flops=2_000_000_000,
        nbytes=8_000_000,
        mib=24,
        out_space=HBM,
    )(anchors, first_slabs, w1_band, w2_fwd, w3_band, biases)

    last_slabs = lax.all_to_all(edges[0], "gy", 0, 0, tiled=True).reshape(32, 2 * F * X, Z)
    keep, send = call(
        backward_kernel,
        [((HALF, 128), F32)] * 2,
        scratch=HELD
        + [
            pltpu.VMEM((2, ROWS, PY * Z), F32),
            pltpu.VMEM((2, TALL, PY * Z), BF),
            pltpu.VMEM((2, 384, (PY + 2) * Z), BF),
            pltpu.VMEM((2, TALL, PY * Z), BF),
            pltpu.VMEM((2, 384, (PY + 2) * Z), BF),
            pltpu.VMEM((2 * HALF, 128), F32),
        ],
        ins=[SMEM] * 3 + [VMEM] * 3 + [HBM],
        flops=4_000_000_000,
        nbytes=10_000_000,
        mib=24,
    )(place, anchors, count, last_slabs, w2_bwd, w3_turned, kept)

    g1, gb1, g2, gb2, g3, gb3, loss = call(
        finish_kernel,
        [((45, 3, C), F32), ((1, C), F32), ((27, C, C), F32), ((1, C), F32), ((45, 3, C), F32), ((1, F), F32), ((1, 1), F32)],
        scratch=[pltpu.VMEM((2 * HALF, 128), F32)],
        ins=[SMEM, VMEM, VMEM],
        nbytes=1_000_000,
    )(place, *sum_all(keep, send))
    g1 = jnp.transpose(g1.reshape(F, 3, 3, 3, C), (4, 0, 1, 2, 3))
    g2 = jnp.transpose(g2.reshape(3, 3, 3, C, C), (3, 4, 0, 1, 2))
    g3 = jnp.transpose(g3.reshape(F, 3, 3, 3, C), (0, 4, 1, 2, 3))
    gb1, gb2, gb3, loss = gb1.reshape(C), gb2.reshape(C), gb3.reshape(F), loss.reshape(())
    return u.reshape(F, X, 4, 2048), g1, gb1, g2, gb2, g3, gb3, loss


def solution(mesh):
    return jax.shard_map(
        on_device,
        mesh=mesh,
        in_specs=(
            P(None, "gx", "gy", None),
            P(None, "gx", "gy", None),
            P("gx", "gy", None),
            P("gx", "gy", None),
            P("gx", "gy"),
            P(),
            P(),
            P(),
            P(),
            P(),
            P(),
        ),
        out_specs=(P(None, "gx", "gy", None), P(), P(), P(), P(), P(), P(), P()),
        check_vma=False,
    )
```

```python
import jax
import jax.numpy as jnp
from jax import lax
from jax.experimental import pallas as pl
from jax.experimental.pallas import tpu as pltpu
from jax.sharding import PartitionSpec as P

STEPS = 3
F = 5
C = 32
X = 4
PY = 8
Z = 128
ROWS = 24
HALF = 144
TAPS = 9
TALL = 224
CELLS = 20480.0
BF = jnp.bfloat16
F32 = jnp.float32
VMEM = pl.BlockSpec(memory_space=pltpu.VMEM)
SMEM = pl.BlockSpec(memory_space=pltpu.SMEM)
HBM = pl.BlockSpec(memory_space=pltpu.HBM)
ANY = pl.BlockSpec(memory_space=pl.ANY)
MIB = 1024 * 1024
BESIDE = 6_000_000_000


def call(kernel, outs, scratch=(), flops=0, nbytes=0, ins=(), mib=12, out_space=None):
    return pl.pallas_call(
        kernel,
        out_shape=[jax.ShapeDtypeStruct(s, d) for s, d in outs],
        in_specs=list(ins),
        out_specs=[out_space or VMEM] * len(outs),
        scratch_shapes=list(scratch),
        compiler_params=pltpu.CompilerParams(vmem_limit_bytes=mib * MIB),
        cost_estimate=pl.CostEstimate(flops=flops, bytes_accessed=nbytes, transcendentals=0),
    )


def pack_slabs(get, out_ref):
    for row in range(F * X):
        cells = get(row)
        for y in range(4):
            for j in range(16):
                out_ref[j, y // 2, pl.ds((y % 2) * F * X + row, 1), :] = cells[y : y + 1, j * Z : (j + 1) * Z]


def write_edges(get, odd_x, odd_y, xa_ref, xb_ref, ya_ref, yb_ref):
    for f in range(F):
        head, tail = get(f * X), get(f * X + X - 1)
        xa_ref[f] = jnp.where(odd_x, head, tail)
        xb_ref[f] = jnp.where(odd_x, tail, head)
    for row in range(F * X):
        cells = get(row)
        head, tail = cells[0:1], cells[3:4]
        f, x = row // X, row % X
        ya_ref[f, x : x + 1, :] = jnp.where(odd_y, head, tail)
        yb_ref[f, x : x + 1, :] = jnp.where(odd_y, tail, head)


def edges_kernel(place, u_ref, xa_ref, xb_ref, ya_ref, yb_ref):
    get = lambda row: u_ref[row]
    write_edges(get, place[0] % 2 == 1, place[1] % 2 == 1, xa_ref, xb_ref, ya_ref, yb_ref)


def slabs_kernel(u_ref, slabs_ref):
    pack_slabs(lambda row: u_ref[row], slabs_ref)


def inner_kernel(u_ref, vel_ref, dif_ref, part_ref):
    lane = lax.broadcasted_iota(jnp.int32, (4, 2048), 1)
    not_first, not_last = lane > 0, lane < 2047
    zero_row = jnp.zeros((1, 2048), F32)
    for x in range(X):
        v0, v1, v2, dif = vel_ref[x], vel_ref[X + x], vel_ref[2 * X + x], dif_ref[x]
        for f in range(F):
            row = f * X + x
            middle = u_ref[row]
            x_plus = u_ref[row + 1] if x < X - 1 else 0.0
            x_minus = u_ref[row - 1] if x > 0 else 0.0
            y_plus = jnp.concatenate([middle[1:4], zero_row], axis=0)
            y_minus = jnp.concatenate([zero_row, middle[0:3]], axis=0)
            z_plus = jnp.where(not_last, pltpu.roll(middle, 2047, 1), 0.0)
            z_minus = jnp.where(not_first, pltpu.roll(middle, 1, 1), 0.0)
            carried = v0 * (x_plus - x_minus) + v1 * (y_plus - y_minus) + v2 * (z_plus - z_minus)
            spread = x_plus + x_minus + y_plus + y_minus + z_plus + z_minus - 6.0 * middle
            part_ref[row] = middle - 0.5 * carried + dif * spread


def outer_kernel(last, place, part_ref, *refs):
    rxa, rxb, ryb, rya = refs[2:4] + refs[0:2] if last else refs[0:4]
    vel_ref, dif_ref, new_ref, *outs = refs[4:]
    gx, gy = place[0], place[1]
    odd_x, odd_y = gx % 2 == 1, gy % 2 == 1
    y_at = lax.broadcasted_iota(jnp.int32, (4, 2048), 0)
    up_on = (y_at == 3) & (gy != 15)
    down_on = (y_at == 0) & (gy != 0)
    for x in range(X):
        v0, v1, dif = vel_ref[x], vel_ref[X + x], dif_ref[x]
        up = jnp.where(up_on, dif - 0.5 * v1, 0.0)
        down = jnp.where(down_on, dif + 0.5 * v1, 0.0)
        side = None
        if x == X - 1:
            side = jnp.where(gx == 7, 0.0, dif - 0.5 * v0)
        if x == 0:
            side = jnp.where(gx == 0, 0.0, dif + 0.5 * v0)
        from_a = jnp.where(odd_y, down, up)
        from_b = jnp.where(odd_y, up, down)
        for f in range(F):
            row = f * X + x
            new = part_ref[row] + rya[f, x : x + 1, :] * from_a + ryb[f, x : x + 1, :] * from_b
            if x == X - 1:
                new = new + jnp.where(odd_x, rxb[f], rxa[f]) * side
            if x == 0:
                new = new + jnp.where(odd_x, rxa[f], rxb[f]) * side
            new_ref[row] = new
    get = lambda row: new_ref[row]
    if last:
        pack_slabs(get, outs[0])
    else:
        write_edges(get, odd_x, odd_y, *outs)


EDGES = [((F, X, 2048), F32)] * 4
SLABS = ((16, 2, 2 * F * X, Z), F32)


def exchange(edges, y_first):
    def pairs(n, second):
        partner = lambda i: (i ^ 1) if not second else ((i + 1) if i % 2 else (i - 1)) % n
        return [(i, partner(i)) for i in range(n)]

    xa, xb, ya, yb = edges
    along_x = lambda: [lax.ppermute(xa, "gx", pairs(8, False)), lax.ppermute(xb, "gx", pairs(8, True))]
    along_y = lambda: [lax.ppermute(yb, "gy", pairs(16, True)), lax.ppermute(ya, "gy", pairs(16, False))]
    return along_y() + along_x() if y_first else along_x() + along_y()


def patch_rows(slabs_ref, anchor, out_ref):
    out_ref[...] = jnp.zeros_like(out_ref)
    for k in range(PY):
        y = anchor + k
        both = slabs_ref[y // 2]
        rows = jnp.where(y % 2 == 1, both[F * X :], both[: F * X])
        out_ref[0 : F * X, k * Z : (k + 1) * Z] = rows


def z_shifted(cells, dz, lane):
    if dz == 0:
        return cells
    moved = pltpu.roll(cells, (-dz) % Z, 1)
    return jnp.where(lane == (Z - 1 if dz > 0 else 0), 0.0, moved)


def fill_taps(cells, out_ref, sign):
    rows = cells.shape[0]
    lane = lax.broadcasted_iota(jnp.int32, (rows, Z), 1)
    zero = jnp.zeros((rows, Z), F32)
    shifted = [[z_shifted(cells[:, k * Z : (k + 1) * Z], sign * (dz - 1), lane) for dz in range(3)] for k in range(PY)]
    for k in range(PY):
        parts = []
        for dy in range(3):
            at = k + sign * (dy - 1)
            for dz in range(3):
                parts.append(shifted[at][dz] if 0 <= at < PY else zero)
        parts.append(jnp.zeros((TALL - TAPS * rows, Z), F32))
        out_ref[:, k * Z : (k + 1) * Z] = jnp.concatenate(parts, axis=0).astype(BF)


def fill_z(cells, k, out_ref, sign):
    lane = lax.broadcasted_iota(jnp.int32, cells.shape, 1)
    for dz in range(3):
        moved = z_shifted(cells, sign * (dz - 1), lane)
        out_ref[dz * 128 : (dz + 1) * 128, (k + 1) * Z : (k + 2) * Z] = moved.astype(BF)


def clear_ends(ref):
    ref[:, 0:Z] = jnp.zeros((ref.shape[0], Z), ref.dtype)
    ref[:, (PY + 1) * Z :] = jnp.zeros((ref.shape[0], Z), ref.dtype)


def dot(a, b):
    return jnp.dot(a, b, preferred_element_type=F32)


def dot_t(a, b):
    return lax.dot_general(a, b, (((1,), (1,)), ((), ())), preferred_element_type=F32)


def activate(y):
    sig = 1.0 / (1.0 + jnp.exp(-y))
    return y * sig, sig * (1.0 + y * (1.0 - sig))


def band_rows(w_ref, flip, out_ref):
    out_ref[...] = jnp.zeros_like(out_ref)
    zero = jnp.zeros((1, C), F32)
    for t in range(TAPS):
        for f in range(F):
            for to in range(X):
                parts = []
                for x in range(X):
                    dx = x - to + 1 if flip else to - x + 1
                    parts.append(w_ref[(f * 3 + dx) * 3 + t // 3, t % 3 : t % 3 + 1, :] if 0 <= dx < 3 else zero)
                out_ref[pl.ds(t * ROWS + f * X + to, 1), :] = jnp.concatenate(parts, axis=1)


def prepare_kernel(*refs):
    params, outs, rows_ref, held, sems = refs[:6], refs[6:12], refs[12], refs[13:19], refs[19]
    w1_ref, w2_ref, w3_ref, b1_ref, b2_ref, b3_ref = held
    w1_out, fwd_ref, bwd_ref, w3_out, w3_turned, bias_ref = outs
    copies = [pltpu.make_async_copy(params[n], held[n], sems.at[n]) for n in range(6)]
    for copy in copies:
        copy.start()
    for copy in copies:
        copy.wait()
    band_rows(w1_ref, False, rows_ref)
    w1_out[...] = rows_ref[...].T[:, 0:TALL].astype(BF)
    band_rows(w3_ref, True, rows_ref)
    w3_out[...] = rows_ref[0:TALL].astype(BF)
    w3_turned[...] = rows_ref[...].T[:, 0:TALL].astype(BF)
    zero = jnp.zeros((C, C), F32)
    for dy in range(3):
        for dz in range(3):
            rows = []
            for xo in range(X):
                parts = []
                for xi in range(X):
                    dx = xi - xo + 1
                    parts.append(w2_ref[dx * 9 + dy * 3 + dz] if 0 <= dx < 3 else zero)
                rows.append(jnp.concatenate(parts, axis=1))
            block = jnp.concatenate(rows, axis=0)
            fwd_ref[dy, :, dz * 128 : (dz + 1) * 128] = block.astype(BF)
            bwd_ref[dy, :, dz * 128 : (dz + 1) * 128] = block.T.astype(BF)
    lane = lax.broadcasted_iota(jnp.int32, (1, 128), 1)
    third = jnp.zeros((1, 128), F32)
    for f in range(F):
        third = jnp.where(lane // X == f, b3_ref[:, f : f + 1], third)
    rows = [jnp.concatenate([b1_ref[...]] * X, axis=1), jnp.concatenate([b2_ref[...]] * X, axis=1), third]
    bias_ref[...] = jnp.concatenate(rows + [jnp.zeros((125, 128), F32)], axis=0).T


PARTS = 80
AT = {"sum": (0, PARTS), "first": (80, 32), "a1": (112, 128), "a2": (240, 128), "d1": (368, 128), "d2": (496, 128)}
KEPT = ((2, 16384, PY * Z), BF)
NAMES = ("sum", "d2", "a2", "a1", "first", "d1")
HELD = [pltpu.VMEM((2, AT[name][1], PY * Z), BF) for name in NAMES] + [pltpu.SemaphoreType.DMA((len(NAMES), 2))]


def transfers(kept_ref, held, sems):
    out = {}
    for n, name in enumerate(NAMES):
        for p in range(2):
            start, size = AT[name]
            out[name, p] = (kept_ref.at[p, pl.ds(start, size)], held[n].at[p], sems.at[n, p])
    return out


def forward_kernel(
    anchors, slabs_ref, w1_ref, w2_ref, w3_ref, bias_ref, kept_ref, *refs,
):
    b1, b2, b3 = bias_ref[:, 0:1], bias_ref[:, 1:2], bias_ref[0:ROWS, 2:3]
    held, sems, (first_ref, taps_ref, a1_ref) = refs[: len(NAMES)], refs[len(NAMES)], refs[len(NAMES) + 1 :]
    sum_ref, d2_ref, a2_ref, a1_kept, cells_ref, d1_ref = held
    plan = transfers(kept_ref, held, sems)
    copies = []

    def keep(name, p):
        to, of, sem = plan[name, p]
        copies.append(pltpu.make_async_copy(of, to, sem))
        copies[-1].start()

    for p in range(2):
        patch_rows(slabs_ref, anchors[p], first_ref.at[p])
        cells_ref[p] = jnp.concatenate([first_ref[p], jnp.zeros((32 - ROWS, PY * Z), F32)], axis=0).astype(BF)
        keep("first", p)
        fill_taps(first_ref[p], taps_ref.at[p], 1)
        y1 = dot(w1_ref[...], taps_ref[p])
        act, slope = activate(y1 + b1)
        d1_ref[p] = slope.astype(BF)
        keep("d1", p)
        a1_kept[p] = act.astype(BF)
        keep("a1", p)
        clear_ends(a1_ref.at[p])
        for k in range(PY):
            fill_z(act[:, k * Z : (k + 1) * Z], k, a1_ref.at[p], 1)
        y2 = b2 + dot(w2_ref[0], a1_ref[p, :, 0 : PY * Z])
        for dy in range(1, 3):
            y2 = y2 + dot(w2_ref[dy], a1_ref[p, :, dy * Z : (dy + PY) * Z])
        act, slope = activate(y2)
        d2_ref[p] = slope.astype(BF)
        a2_ref[p] = act.astype(BF)
        keep("d2", p)
        keep("a2", p)
        terms = dot(w3_ref[...], a2_ref[p])
        lane = lax.broadcasted_iota(jnp.int32, (ROWS, Z), 1)
        for k in range(PY):
            out = b3 + first_ref[p, :, k * Z : (k + 1) * Z]
            for dz in range(3):
                part = None
                for dy in range(3):
                    at = k + dy - 1
                    if 0 <= at < PY:
                        t = (dy * 3 + dz) * ROWS
                        term = terms[t : t + ROWS, at * Z : (at + 1) * Z]
                        part = term if part is None else part + term
                out = out + z_shifted(part, dz - 1, lane)
            high = out.astype(BF).astype(F32)
            mid = (out - high).astype(BF).astype(F32)
            low = out - high - mid
            pad = jnp.zeros((PARTS - 3 * ROWS, Z), F32)
            sum_ref[p, :, k * Z : (k + 1) * Z] = jnp.concatenate([high, mid, low, pad], axis=0).astype(BF)
        keep("sum", p)
    for copy in copies:
        copy.wait()


def half_of(place):
    gx, gy = place[0], place[1]
    return (gx // 2 + gx + gy // 4 + gy) % 2


def band_sum(full):
    lane = lax.broadcasted_iota(jnp.int32, (C, 256), 1)
    total = None
    for x in range(X):
        block = full[x * C : (x + 1) * C]
        block = jnp.concatenate([block, jnp.zeros((C, 256 - TALL), F32)], axis=1)
        moved = pltpu.roll(block, (1 - x) % 256, 1)
        e = lane % 4
        ok = (e < 3) & (x + e - 1 >= 0) & (x + e - 1 < X) & (lane < TAPS * ROWS)
        moved = jnp.where(ok, moved, 0.0)
        total = moved if total is None else total + moved
    out = None
    for f in range(F):
        part = jnp.where((lane % ROWS) // 4 == f, total, 0.0)
        part = pltpu.roll(part, (256 - f) % 256, 1)
        out = part if out is None else out + part
    return out


def backward_kernel(place, anchors, count, slabs_ref, w2_ref, w3_ref, kept_ref, keep_ref, send_ref, *refs):
    held, sems = refs[: len(NAMES)], refs[len(NAMES)]
    last_ref, taps_ref, a1_ref, g_ref, b_ref, grads_ref = refs[len(NAMES) + 1 :]
    sum_ref, d2_ref, a2_ref, a1_kept, cells_ref, d1_ref = held
    plan = transfers(kept_ref, held, sems)
    copies = {key: pltpu.make_async_copy(of, to, sem) for key, (of, to, sem) in plan.items()}
    for p in range(2):
        for name in NAMES:
            copies[name, p].start()
    db1 = jnp.zeros((128, 1), F32)
    db2 = jnp.zeros((128, 1), F32)
    db3 = jnp.zeros((ROWS, 1), F32)
    loss = jnp.zeros((ROWS, 1), F32)
    dw1 = jnp.zeros((128, TALL), F32)
    dw3 = jnp.zeros((128, TALL), F32)
    dw2 = [jnp.zeros((128, 384), F32) for _ in range(3)]
    for p in range(2):
        copies["sum", p].wait()
    for p in range(2):
        live = jnp.where(p < count[0], 1.0, 0.0).astype(F32)
        patch_rows(slabs_ref, anchors[p], last_ref.at[p])
        parts = sum_ref[p].astype(F32)
        err = parts[0:ROWS] + parts[ROWS : 2 * ROWS] + parts[2 * ROWS : 3 * ROWS] - last_ref[p]
        loss = loss + live * jnp.sum(err * err, axis=1, keepdims=True)
        err = err * (live * (2.0 / CELLS))
        db3 = db3 + jnp.sum(err, axis=1, keepdims=True)
        fill_taps(err, g_ref.at[p], -1)
    for name in NAMES[1:]:
        for p in range(2):
            copies[name, p].wait()
    for p in range(2):
        da2 = dot(w3_ref[...], g_ref[p])
        dw3 = dw3 + dot_t(a2_ref[p], g_ref[p])
        dy2 = da2 * d2_ref[p].astype(F32)
        db2 = db2 + jnp.sum(dy2, axis=1, keepdims=True)
        clear_ends(b_ref.at[p])
        for k in range(PY):
            fill_z(dy2[:, k * Z : (k + 1) * Z], k, b_ref.at[p], -1)
        clear_ends(a1_ref.at[p])
        for k in range(PY):
            fill_z(a1_kept[p, :, k * Z : (k + 1) * Z].astype(F32), k, a1_ref.at[p], 1)
        fill_taps(cells_ref[p].astype(F32)[0:ROWS], taps_ref.at[p], 1)
        middle = b_ref[p, 128:256, Z : (PY + 1) * Z]
        da1 = None
        for dy in range(3):
            dw2[dy] = dw2[dy] + dot_t(middle, a1_ref[p, :, dy * Z : (dy + PY) * Z])
            term = dot(w2_ref[dy], b_ref[p, :, (2 - dy) * Z : (2 - dy + PY) * Z])
            da1 = term if da1 is None else da1 + term
        dy1 = da1 * d1_ref[p].astype(F32)
        db1 = db1 + jnp.sum(dy1, axis=1, keepdims=True)
        dw1 = dw1 + dot_t(dy1.astype(BF), taps_ref[p])

    lane = lax.broadcasted_iota(jnp.int32, (C, 128), 1)
    small1, small3 = band_sum(dw1), band_sum(dw3)
    fold = lambda v: v[0:C] + v[C : 2 * C] + v[2 * C : 3 * C] + v[3 * C : 4 * C]
    by_field = [jnp.sum(db3[f * X : (f + 1) * X], axis=0, keepdims=True) for f in range(F)]
    db3 = jnp.concatenate(by_field + [jnp.zeros((C - F, 1), F32)], axis=0)
    loss = jnp.sum(loss, axis=0, keepdims=True) * (1.0 / CELLS)
    extras = {0: (fold(db1), fold(db2)), 1: (db3, loss), 2: (jnp.full((C, 1), 1.0, F32) * count[0].astype(F32), None)}
    for t in range(TAPS):
        dy, dz = t // 3, t % 3
        total = jnp.zeros((C, 128), F32)
        for xo in range(X):
            block = dw2[dy][xo * C : (xo + 1) * C, dz * 128 : (dz + 1) * 128]
            moved = pltpu.roll(block, ((1 - xo) * C) % 128, 1)
            dx = lane // C
            ok = (dx < 3) & (xo + dx - 1 >= 0) & (xo + dx - 1 < X)
            total = total + jnp.where(ok, moved, 0.0)
        one = pltpu.roll(small1, (96 - ROWS * t) % 256, 1)[:, 0:128]
        three = pltpu.roll(small3, (111 - ROWS * t) % 256, 1)[:, 0:128]
        total = jnp.where((lane >= 96) & (lane < 111), one, total)
        total = jnp.where((lane >= 111) & (lane < 126), three, total)
        if t in extras:
            a, b = extras[t]
            total = jnp.where(lane == 126, a, total)
            if b is not None:
                total = jnp.where(lane == 127, b, total)
        grads_ref[t * C : (t + 1) * C] = total
    second = half_of(place) == 1
    low, high = grads_ref[0:HALF], grads_ref[HALF:]
    keep_ref[...] = jnp.where(second, high, low)
    send_ref[...] = jnp.where(second, low, high)


def finish_kernel(
    place, mine_ref, other_ref, g1_ref, gb1_ref, g2_ref, gb2_ref, g3_ref, gb3_ref, loss_ref, grads_ref
):
    second = half_of(place) == 1
    at = jnp.where(second, HALF, 0)
    grads_ref[pl.ds(pl.multiple_of(at, 8), HALF)] = mine_ref[...]
    grads_ref[pl.ds(pl.multiple_of(HALF - at, 8), HALF)] = other_ref[...]
    rows = lambda t: grads_ref[t * C : (t + 1) * C]
    scale = 1.0 / rows(2)[0:1, 126:127]
    for t in range(TAPS):
        dy, dz = t // 3, t % 3
        block = rows(t) * scale
        for dx in range(3):
            g2_ref[dx * TAPS + t] = block[:, dx * C : (dx + 1) * C]
        turned = block.T
        for f in range(F):
            for dx in range(3):
                to = (f * 3 + dx) * 3 + dy
                at = 96 + f * 3 + dx
                g1_ref[to, dz : dz + 1, :] = turned[at : at + 1]
                at = 111 + f * 3 + 2 - dx
                g3_ref[to, dz : dz + 1, :] = turned[at : at + 1]
        if t == 0:
            gb1_ref[...] = turned[126:127]
            gb2_ref[...] = turned[127:128]
        if t == 1:
            gb3_ref[...] = turned[126:127, 0:F]
            loss_ref[...] = turned[127:128, 0:1]


def reduce_steps(order):
    def near(c):
        return c ^ 1

    def far(c):
        return 3 - c

    steps = []
    for n in range(6):
        pairs = []
        for gx in range(8):
            for gy in range(16):
                at = {"x": gx // 2, "y": gy // 4, "z": (gy // 2 % 2) * 2 + gx % 2}
                axis = order[n // 2]
                at[axis] = (near, far)[n % 2](at[axis])
                to = (at["x"] * 2 + at["z"] % 2) * 16 + at["y"] * 4 + (at["z"] // 2) * 2 + (gy + 1) % 2
                pairs.append((gx * 16 + gy, to))
        steps.append(pairs)
    return steps


def sum_all(keep, send):
    cores = [(i, i ^ 1) for i in range(16)]
    mine = keep + lax.ppermute(send, "gy", cores)
    parts = [mine[: HALF // 2], mine[HALF // 2 :]]
    for pairs in zip(reduce_steps("zyx"), reduce_steps("xzy")):
        moved = [lax.ppermute(part, ("gx", "gy"), p) for part, p in zip(parts, pairs)]
        parts = [part + m for part, m in zip(parts, moved)]
    mine = jnp.concatenate(parts)
    return mine, lax.ppermute(mine, "gy", cores)


def on_device(
    initial_fields, velocity, diffusivity, patch_anchor, patch_count,
    weight_one, bias_one, weight_two, bias_two, weight_three, bias_three,
):
    place = jnp.stack([lax.axis_index("gx"), lax.axis_index("gy")]).astype(jnp.int32)
    u = initial_fields.reshape(F * X, 4, 2048)
    vel = velocity.reshape(3 * X, 4, 2048)
    anchors = patch_anchor.reshape(2)
    count = patch_count.reshape(1)

    edges = call(edges_kernel, EDGES, ins=[SMEM, VMEM], nbytes=1_000_000)(place, u)
    params = (
        jnp.transpose(weight_one, (1, 2, 3, 4, 0)).reshape(45, 3, C),
        jnp.transpose(weight_two, (2, 3, 4, 0, 1)).reshape(27, C, C),
        jnp.transpose(weight_three, (0, 2, 3, 4, 1)).reshape(45, 3, C),
        bias_one.reshape(1, C),
        bias_two.reshape(1, C),
        bias_three.reshape(1, F),
    )
    (slabs,) = call(slabs_kernel, [SLABS], ins=[VMEM], nbytes=1_500_000)(u)
    first_slabs = lax.all_to_all(slabs, "gy", 0, 0, tiled=True).reshape(32, 2 * F * X, Z)
    w1_band, w2_fwd, w2_bwd, w3_band, w3_turned, biases = call(
        prepare_kernel,
        [
            ((128, TALL), BF),
            ((3, 128, 384), BF),
            ((3, 128, 384), BF),
            ((TALL, 128), BF),
            ((128, TALL), BF),
            ((128, 128), F32),
        ],
        scratch=[pltpu.VMEM((256, 128), F32)]
        + [pltpu.VMEM(p.shape, F32) for p in params]
        + [pltpu.SemaphoreType.DMA((len(params),))],
        ins=[ANY] * len(params),
        nbytes=1_000_000,
    )(*params)

    for step in range(STEPS):
        last = step == STEPS - 1
        outs = [((F * X, 4, 2048), F32)] + ([SLABS] if last else EDGES)
        received = exchange(edges, last)
        (part,) = call(inner_kernel, [((F * X, 4, 2048), F32)], ins=[VMEM] * 3, nbytes=4_000_000, flops=BESIDE)(u, vel, diffusivity)
        kernel = lambda *refs, last=last: outer_kernel(last, *refs)
        u, *edges = call(kernel, outs, ins=[SMEM] + [VMEM] * 7, nbytes=3_000_000, flops=BESIDE)(
            place, part, *received, vel, diffusivity
        )

    (kept,) = call(
        forward_kernel,
        [KEPT],
        scratch=HELD
        + [
            pltpu.VMEM((2, ROWS, PY * Z), F32),
            pltpu.VMEM((2, TALL, PY * Z), BF),
            pltpu.VMEM((2, 384, (PY + 2) * Z), BF),
        ],
        ins=[SMEM] + [VMEM] * 5,
        flops=2_000_000_000,
        nbytes=8_000_000,
        mib=24,
        out_space=HBM,
    )(anchors, first_slabs, w1_band, w2_fwd, w3_band, biases)

    last_slabs = lax.all_to_all(edges[0], "gy", 0, 0, tiled=True).reshape(32, 2 * F * X, Z)
    keep, send = call(
        backward_kernel,
        [((HALF, 128), F32)] * 2,
        scratch=HELD
        + [
            pltpu.VMEM((2, ROWS, PY * Z), F32),
            pltpu.VMEM((2, TALL, PY * Z), BF),
            pltpu.VMEM((2, 384, (PY + 2) * Z), BF),
            pltpu.VMEM((2, TALL, PY * Z), BF),
            pltpu.VMEM((2, 384, (PY + 2) * Z), BF),
            pltpu.VMEM((2 * HALF, 128), F32),
        ],
        ins=[SMEM] * 3 + [VMEM] * 3 + [HBM],
        flops=4_000_000_000,
        nbytes=10_000_000,
        mib=24,
    )(place, anchors, count, last_slabs, w2_bwd, w3_turned, kept)

    g1, gb1, g2, gb2, g3, gb3, loss = call(
        finish_kernel,
        [((45, 3, C), F32), ((1, C), F32), ((27, C, C), F32), ((1, C), F32), ((45, 3, C), F32), ((1, F), F32), ((1, 1), F32)],
        scratch=[pltpu.VMEM((2 * HALF, 128), F32)],
        ins=[SMEM, VMEM, VMEM],
        nbytes=1_000_000,
    )(place, *sum_all(keep, send))
    g1 = jnp.transpose(g1.reshape(F, 3, 3, 3, C), (4, 0, 1, 2, 3))
    g2 = jnp.transpose(g2.reshape(3, 3, 3, C, C), (3, 4, 0, 1, 2))
    g3 = jnp.transpose(g3.reshape(F, 3, 3, 3, C), (0, 4, 1, 2, 3))
    gb1, gb2, gb3, loss = gb1.reshape(C), gb2.reshape(C), gb3.reshape(F), loss.reshape(())
    return u.reshape(F, X, 4, 2048), g1, gb1, g2, gb2, g3, gb3, loss


def solution(mesh):
    return jax.shard_map(
        on_device,
        mesh=mesh,
        in_specs=(
            P(None, "gx", "gy", None),
            P(None, "gx", "gy", None),
            P("gx", "gy", None),
            P("gx", "gy", None),
            P("gx", "gy"),
            P(),
            P(),
            P(),
            P(),
            P(),
            P(),
        ),
        out_specs=(P(None, "gx", "gy", None), P(), P(), P(), P(), P(), P(), P()),
        check_vma=False,
    )
```

```python
import jax
import jax.numpy as jnp
from jax import lax
from jax.experimental import pallas as pl
from jax.experimental.pallas import tpu as pltpu
from jax.sharding import PartitionSpec as P

STEPS = 3
F = 5
C = 32
X = 4
PY = 8
Z = 128
ROWS = 24
HALF = 144
TAPS = 9
TALL = 224
CELLS = 20480.0
BF = jnp.bfloat16
F32 = jnp.float32
VMEM = pl.BlockSpec(memory_space=pltpu.VMEM)
SMEM = pl.BlockSpec(memory_space=pltpu.SMEM)
HBM = pl.BlockSpec(memory_space=pltpu.HBM)
ANY = pl.BlockSpec(memory_space=pl.ANY)
MIB = 1024 * 1024
BESIDE = 6_000_000_000


def call(kernel, outs, scratch=(), flops=0, nbytes=0, ins=(), mib=12, out_space=None):
    return pl.pallas_call(
        kernel,
        out_shape=[jax.ShapeDtypeStruct(s, d) for s, d in outs],
        in_specs=list(ins),
        out_specs=[out_space or VMEM] * len(outs),
        scratch_shapes=list(scratch),
        compiler_params=pltpu.CompilerParams(vmem_limit_bytes=mib * MIB),
        cost_estimate=pl.CostEstimate(flops=flops, bytes_accessed=nbytes, transcendentals=0),
    )


def pack_slabs(get, out_ref):
    for row in range(F * X):
        cells = get(row)
        for y in range(4):
            for j in range(16):
                out_ref[j, y // 2, pl.ds((y % 2) * F * X + row, 1), :] = cells[y : y + 1, j * Z : (j + 1) * Z]


def write_edges(get, odd_x, odd_y, xa_ref, xb_ref, ya_ref, yb_ref):
    for f in range(F):
        head, tail = get(f * X), get(f * X + X - 1)
        xa_ref[f] = jnp.where(odd_x, head, tail)
        xb_ref[f] = jnp.where(odd_x, tail, head)
    for row in range(F * X):
        cells = get(row)
        head, tail = cells[0:1], cells[3:4]
        f, x = row // X, row % X
        ya_ref[f, x : x + 1, :] = jnp.where(odd_y, head, tail)
        yb_ref[f, x : x + 1, :] = jnp.where(odd_y, tail, head)


def edges_kernel(place, u_ref, xa_ref, xb_ref, ya_ref, yb_ref):
    get = lambda row: u_ref[row]
    write_edges(get, place[0] % 2 == 1, place[1] % 2 == 1, xa_ref, xb_ref, ya_ref, yb_ref)


def slabs_kernel(u_ref, slabs_ref):
    pack_slabs(lambda row: u_ref[row], slabs_ref)


def inner_kernel(u_ref, vel_ref, dif_ref, part_ref):
    lane = lax.broadcasted_iota(jnp.int32, (4, 2048), 1)
    not_first, not_last = lane > 0, lane < 2047
    zero_row = jnp.zeros((1, 2048), F32)
    for x in range(X):
        v0, v1, v2, dif = vel_ref[x], vel_ref[X + x], vel_ref[2 * X + x], dif_ref[x]
        for f in range(F):
            row = f * X + x
            middle = u_ref[row]
            x_plus = u_ref[row + 1] if x < X - 1 else 0.0
            x_minus = u_ref[row - 1] if x > 0 else 0.0
            y_plus = jnp.concatenate([middle[1:4], zero_row], axis=0)
            y_minus = jnp.concatenate([zero_row, middle[0:3]], axis=0)
            z_plus = jnp.where(not_last, pltpu.roll(middle, 2047, 1), 0.0)
            z_minus = jnp.where(not_first, pltpu.roll(middle, 1, 1), 0.0)
            carried = v0 * (x_plus - x_minus) + v1 * (y_plus - y_minus) + v2 * (z_plus - z_minus)
            spread = x_plus + x_minus + y_plus + y_minus + z_plus + z_minus - 6.0 * middle
            part_ref[row] = middle - 0.5 * carried + dif * spread


def outer_kernel(last, place, part_ref, *refs):
    rxa, rxb, ryb, rya = refs[2:4] + refs[0:2] if last else refs[0:4]
    vel_ref, dif_ref, new_ref, *outs = refs[4:]
    gx, gy = place[0], place[1]
    odd_x, odd_y = gx % 2 == 1, gy % 2 == 1
    y_at = lax.broadcasted_iota(jnp.int32, (4, 2048), 0)
    up_on = (y_at == 3) & (gy != 15)
    down_on = (y_at == 0) & (gy != 0)
    for x in range(X):
        v0, v1, dif = vel_ref[x], vel_ref[X + x], dif_ref[x]
        up = jnp.where(up_on, dif - 0.5 * v1, 0.0)
        down = jnp.where(down_on, dif + 0.5 * v1, 0.0)
        side = None
        if x == X - 1:
            side = jnp.where(gx == 7, 0.0, dif - 0.5 * v0)
        if x == 0:
            side = jnp.where(gx == 0, 0.0, dif + 0.5 * v0)
        from_a = jnp.where(odd_y, down, up)
        from_b = jnp.where(odd_y, up, down)
        for f in range(F):
            row = f * X + x
            new = part_ref[row] + rya[f, x : x + 1, :] * from_a + ryb[f, x : x + 1, :] * from_b
            if x == X - 1:
                new = new + jnp.where(odd_x, rxb[f], rxa[f]) * side
            if x == 0:
                new = new + jnp.where(odd_x, rxa[f], rxb[f]) * side
            new_ref[row] = new
    get = lambda row: new_ref[row]
    if last:
        pack_slabs(get, outs[0])
    else:
        write_edges(get, odd_x, odd_y, *outs)


EDGES = [((F, X, 2048), F32)] * 4
SLABS = ((16, 2, 2 * F * X, Z), F32)


def exchange(edges, y_first):
    def pairs(n, second):
        partner = lambda i: (i ^ 1) if not second else ((i + 1) if i % 2 else (i - 1)) % n
        return [(i, partner(i)) for i in range(n)]

    xa, xb, ya, yb = edges
    along_x = lambda: [lax.ppermute(xa, "gx", pairs(8, False)), lax.ppermute(xb, "gx", pairs(8, True))]
    along_y = lambda: [lax.ppermute(yb, "gy", pairs(16, True)), lax.ppermute(ya, "gy", pairs(16, False))]
    return along_y() + along_x() if y_first else along_x() + along_y()


def patch_rows(slabs_ref, anchor, out_ref):
    out_ref[...] = jnp.zeros_like(out_ref)
    for k in range(PY):
        y = anchor + k
        both = slabs_ref[y // 2]
        rows = jnp.where(y % 2 == 1, both[F * X :], both[: F * X])
        out_ref[0 : F * X, k * Z : (k + 1) * Z] = rows


def z_shifted(cells, dz, lane):
    if dz == 0:
        return cells
    moved = pltpu.roll(cells, (-dz) % Z, 1)
    return jnp.where(lane == (Z - 1 if dz > 0 else 0), 0.0, moved)


def fill_taps(cells, out_ref, sign):
    rows = cells.shape[0]
    lane = lax.broadcasted_iota(jnp.int32, (rows, Z), 1)
    zero = jnp.zeros((rows, Z), F32)
    shifted = [[z_shifted(cells[:, k * Z : (k + 1) * Z], sign * (dz - 1), lane) for dz in range(3)] for k in range(PY)]
    for k in range(PY):
        parts = []
        for dy in range(3):
            at = k + sign * (dy - 1)
            for dz in range(3):
                parts.append(shifted[at][dz] if 0 <= at < PY else zero)
        parts.append(jnp.zeros((TALL - TAPS * rows, Z), F32))
        out_ref[:, k * Z : (k + 1) * Z] = jnp.concatenate(parts, axis=0).astype(BF)


def fill_z(cells, k, out_ref, sign):
    lane = lax.broadcasted_iota(jnp.int32, cells.shape, 1)
    for dz in range(3):
        moved = z_shifted(cells, sign * (dz - 1), lane)
        out_ref[dz * 128 : (dz + 1) * 128, (k + 1) * Z : (k + 2) * Z] = moved.astype(BF)


def clear_ends(ref):
    ref[:, 0:Z] = jnp.zeros((ref.shape[0], Z), ref.dtype)
    ref[:, (PY + 1) * Z :] = jnp.zeros((ref.shape[0], Z), ref.dtype)


def dot(a, b):
    return jnp.dot(a, b, preferred_element_type=F32)


def dot_t(a, b):
    return lax.dot_general(a, b, (((1,), (1,)), ((), ())), preferred_element_type=F32)


def activate(y):
    sig = 1.0 / (1.0 + jnp.exp(-y))
    return y * sig, sig * (1.0 + y * (1.0 - sig))


def band_rows(w_ref, flip, out_ref):
    out_ref[...] = jnp.zeros_like(out_ref)
    zero = jnp.zeros((1, C), F32)
    for t in range(TAPS):
        for f in range(F):
            for to in range(X):
                parts = []
                for x in range(X):
                    dx = x - to + 1 if flip else to - x + 1
                    parts.append(w_ref[(f * 3 + dx) * 3 + t // 3, t % 3 : t % 3 + 1, :] if 0 <= dx < 3 else zero)
                out_ref[pl.ds(t * ROWS + f * X + to, 1), :] = jnp.concatenate(parts, axis=1)


def prepare_kernel(*refs):
    params, outs, rows_ref, held, sems = refs[:6], refs[6:12], refs[12], refs[13:19], refs[19]
    w1_ref, w2_ref, w3_ref, b1_ref, b2_ref, b3_ref = held
    w1_out, fwd_ref, bwd_ref, w3_out, w3_turned, bias_ref = outs
    copies = [pltpu.make_async_copy(params[n], held[n], sems.at[n]) for n in range(6)]
    for copy in copies:
        copy.start()
    for copy in copies:
        copy.wait()
    band_rows(w1_ref, False, rows_ref)
    w1_out[...] = rows_ref[...].T[:, 0:TALL].astype(BF)
    band_rows(w3_ref, True, rows_ref)
    w3_out[...] = rows_ref[0:TALL].astype(BF)
    w3_turned[...] = rows_ref[...].T[:, 0:TALL].astype(BF)
    zero = jnp.zeros((C, C), F32)
    for dy in range(3):
        for dz in range(3):
            rows = []
            for xo in range(X):
                parts = []
                for xi in range(X):
                    dx = xi - xo + 1
                    parts.append(w2_ref[dx * 9 + dy * 3 + dz] if 0 <= dx < 3 else zero)
                rows.append(jnp.concatenate(parts, axis=1))
            block = jnp.concatenate(rows, axis=0)
            fwd_ref[dy, :, dz * 128 : (dz + 1) * 128] = block.astype(BF)
            bwd_ref[dy, :, dz * 128 : (dz + 1) * 128] = block.T.astype(BF)
    lane = lax.broadcasted_iota(jnp.int32, (1, 128), 1)
    third = jnp.zeros((1, 128), F32)
    for f in range(F):
        third = jnp.where(lane // X == f, b3_ref[:, f : f + 1], third)
    rows = [jnp.concatenate([b1_ref[...]] * X, axis=1), jnp.concatenate([b2_ref[...]] * X, axis=1), third]
    bias_ref[...] = jnp.concatenate(rows + [jnp.zeros((125, 128), F32)], axis=0).T


PARTS = 80
AT = {"sum": (0, PARTS), "first": (80, 32), "a1": (112, 128), "a2": (240, 128), "d1": (368, 128), "d2": (496, 128)}
KEPT = ((2, 16384, PY * Z), BF)
NAMES = ("sum", "d2", "a2", "a1", "first", "d1")
HELD = [pltpu.VMEM((2, AT[name][1], PY * Z), BF) for name in NAMES] + [pltpu.SemaphoreType.DMA((len(NAMES), 2))]


def transfers(kept_ref, held, sems):
    out = {}
    for n, name in enumerate(NAMES):
        for p in range(2):
            start, size = AT[name]
            out[name, p] = (kept_ref.at[p, pl.ds(start, size)], held[n].at[p], sems.at[n, p])
    return out


def forward_kernel(
    anchors, slabs_ref, w1_ref, w2_ref, w3_ref, bias_ref, kept_ref, *refs,
):
    b1, b2, b3 = bias_ref[:, 0:1], bias_ref[:, 1:2], bias_ref[0:ROWS, 2:3]
    held, sems, (first_ref, taps_ref, a1_ref) = refs[: len(NAMES)], refs[len(NAMES)], refs[len(NAMES) + 1 :]
    sum_ref, d2_ref, a2_ref, a1_kept, cells_ref, d1_ref = held
    plan = transfers(kept_ref, held, sems)
    copies = []

    def keep(name, p):
        to, of, sem = plan[name, p]
        copies.append(pltpu.make_async_copy(of, to, sem))
        copies[-1].start()

    for p in range(2):
        patch_rows(slabs_ref, anchors[p], first_ref.at[p])
        cells_ref[p] = jnp.concatenate([first_ref[p], jnp.zeros((32 - ROWS, PY * Z), F32)], axis=0).astype(BF)
        keep("first", p)
        fill_taps(first_ref[p], taps_ref.at[p], 1)
        y1 = dot(w1_ref[...], taps_ref[p])
        act, slope = activate(y1 + b1)
        d1_ref[p] = slope.astype(BF)
        keep("d1", p)
        a1_kept[p] = act.astype(BF)
        keep("a1", p)
        clear_ends(a1_ref.at[p])
        for k in range(PY):
            fill_z(act[:, k * Z : (k + 1) * Z], k, a1_ref.at[p], 1)
        y2 = b2 + dot(w2_ref[0], a1_ref[p, :, 0 : PY * Z])
        for dy in range(1, 3):
            y2 = y2 + dot(w2_ref[dy], a1_ref[p, :, dy * Z : (dy + PY) * Z])
        act, slope = activate(y2)
        d2_ref[p] = slope.astype(BF)
        a2_ref[p] = act.astype(BF)
        keep("d2", p)
        keep("a2", p)
        terms = dot(w3_ref[...], a2_ref[p])
        lane = lax.broadcasted_iota(jnp.int32, (ROWS, Z), 1)
        for k in range(PY):
            out = b3 + first_ref[p, :, k * Z : (k + 1) * Z]
            for dz in range(3):
                part = None
                for dy in range(3):
                    at = k + dy - 1
                    if 0 <= at < PY:
                        t = (dy * 3 + dz) * ROWS
                        term = terms[t : t + ROWS, at * Z : (at + 1) * Z]
                        part = term if part is None else part + term
                out = out + z_shifted(part, dz - 1, lane)
            high = out.astype(BF).astype(F32)
            mid = (out - high).astype(BF).astype(F32)
            low = out - high - mid
            pad = jnp.zeros((PARTS - 3 * ROWS, Z), F32)
            sum_ref[p, :, k * Z : (k + 1) * Z] = jnp.concatenate([high, mid, low, pad], axis=0).astype(BF)
        keep("sum", p)
    for copy in copies:
        copy.wait()


def half_of(place):
    gx, gy = place[0], place[1]
    return (gx // 2 + gx + gy // 4 + gy) % 2


def band_sum(full):
    lane = lax.broadcasted_iota(jnp.int32, (C, 256), 1)
    total = None
    for x in range(X):
        block = full[x * C : (x + 1) * C]
        block = jnp.concatenate([block, jnp.zeros((C, 256 - TALL), F32)], axis=1)
        moved = pltpu.roll(block, (1 - x) % 256, 1)
        e = lane % 4
        ok = (e < 3) & (x + e - 1 >= 0) & (x + e - 1 < X) & (lane < TAPS * ROWS)
        moved = jnp.where(ok, moved, 0.0)
        total = moved if total is None else total + moved
    out = None
    for f in range(F):
        part = jnp.where((lane % ROWS) // 4 == f, total, 0.0)
        part = pltpu.roll(part, (256 - f) % 256, 1)
        out = part if out is None else out + part
    return out


def backward_kernel(place, anchors, count, slabs_ref, w2_ref, w3_ref, kept_ref, keep_ref, send_ref, *refs):
    held, sems = refs[: len(NAMES)], refs[len(NAMES)]
    last_ref, taps_ref, a1_ref, g_ref, b_ref, grads_ref = refs[len(NAMES) + 1 :]
    sum_ref, d2_ref, a2_ref, a1_kept, cells_ref, d1_ref = held
    plan = transfers(kept_ref, held, sems)
    copies = {key: pltpu.make_async_copy(of, to, sem) for key, (of, to, sem) in plan.items()}
    for p in range(2):
        for name in NAMES:
            copies[name, p].start()
    db1 = jnp.zeros((128, 1), F32)
    db2 = jnp.zeros((128, 1), F32)
    db3 = jnp.zeros((ROWS, 1), F32)
    loss = jnp.zeros((ROWS, 1), F32)
    dw1 = jnp.zeros((128, TALL), F32)
    dw3 = jnp.zeros((128, TALL), F32)
    dw2 = [jnp.zeros((128, 384), F32) for _ in range(3)]
    for p in range(2):
        patch_rows(slabs_ref, anchors[p], last_ref.at[p])
        clear_ends(b_ref.at[p])
        clear_ends(a1_ref.at[p])
    for p in range(2):
        copies["sum", p].wait()
    for p in range(2):
        live = jnp.where(p < count[0], 1.0, 0.0).astype(F32)
        parts = sum_ref[p].astype(F32)
        err = parts[0:ROWS] + parts[ROWS : 2 * ROWS] + parts[2 * ROWS : 3 * ROWS] - last_ref[p]
        loss = loss + live * jnp.sum(err * err, axis=1, keepdims=True)
        err = err * (live * (2.0 / CELLS))
        db3 = db3 + jnp.sum(err, axis=1, keepdims=True)
        fill_taps(err, g_ref.at[p], -1)
    for name in NAMES[1:]:
        for p in range(2):
            copies[name, p].wait()
    for p in range(2):
        da2 = dot(w3_ref[...], g_ref[p])
        dw3 = dw3 + dot_t(a2_ref[p], g_ref[p])
        dy2 = da2 * d2_ref[p].astype(F32)
        db2 = db2 + jnp.sum(dy2, axis=1, keepdims=True)
        for k in range(PY):
            fill_z(dy2[:, k * Z : (k + 1) * Z], k, b_ref.at[p], -1)
        for k in range(PY):
            fill_z(a1_kept[p, :, k * Z : (k + 1) * Z].astype(F32), k, a1_ref.at[p], 1)
        fill_taps(cells_ref[p].astype(F32)[0:ROWS], taps_ref.at[p], 1)
        middle = b_ref[p, 128:256, Z : (PY + 1) * Z]
        da1 = None
        for dy in range(3):
            dw2[dy] = dw2[dy] + dot_t(middle, a1_ref[p, :, dy * Z : (dy + PY) * Z])
            term = dot(w2_ref[dy], b_ref[p, :, (2 - dy) * Z : (2 - dy + PY) * Z])
            da1 = term if da1 is None else da1 + term
        dy1 = da1 * d1_ref[p].astype(F32)
        db1 = db1 + jnp.sum(dy1, axis=1, keepdims=True)
        dw1 = dw1 + dot_t(dy1.astype(BF), taps_ref[p])

    lane = lax.broadcasted_iota(jnp.int32, (C, 128), 1)
    small1, small3 = band_sum(dw1), band_sum(dw3)
    fold = lambda v: v[0:C] + v[C : 2 * C] + v[2 * C : 3 * C] + v[3 * C : 4 * C]
    by_field = [jnp.sum(db3[f * X : (f + 1) * X], axis=0, keepdims=True) for f in range(F)]
    db3 = jnp.concatenate(by_field + [jnp.zeros((C - F, 1), F32)], axis=0)
    loss = jnp.sum(loss, axis=0, keepdims=True) * (1.0 / CELLS)
    extras = {0: (fold(db1), fold(db2)), 1: (db3, loss), 2: (jnp.full((C, 1), 1.0, F32) * count[0].astype(F32), None)}
    for t in range(TAPS):
        dy, dz = t // 3, t % 3
        total = jnp.zeros((C, 128), F32)
        for xo in range(X):
            block = dw2[dy][xo * C : (xo + 1) * C, dz * 128 : (dz + 1) * 128]
            moved = pltpu.roll(block, ((1 - xo) * C) % 128, 1)
            dx = lane // C
            ok = (dx < 3) & (xo + dx - 1 >= 0) & (xo + dx - 1 < X)
            total = total + jnp.where(ok, moved, 0.0)
        one = pltpu.roll(small1, (96 - ROWS * t) % 256, 1)[:, 0:128]
        three = pltpu.roll(small3, (111 - ROWS * t) % 256, 1)[:, 0:128]
        total = jnp.where((lane >= 96) & (lane < 111), one, total)
        total = jnp.where((lane >= 111) & (lane < 126), three, total)
        if t in extras:
            a, b = extras[t]
            total = jnp.where(lane == 126, a, total)
            if b is not None:
                total = jnp.where(lane == 127, b, total)
        grads_ref[t * C : (t + 1) * C] = total
    second = half_of(place) == 1
    low, high = grads_ref[0:HALF], grads_ref[HALF:]
    keep_ref[...] = jnp.where(second, high, low)
    send_ref[...] = jnp.where(second, low, high)


def finish_kernel(
    place, mine_ref, other_ref, g1_ref, gb1_ref, g2_ref, gb2_ref, g3_ref, gb3_ref, loss_ref, grads_ref
):
    second = half_of(place) == 1
    at = jnp.where(second, HALF, 0)
    grads_ref[pl.ds(pl.multiple_of(at, 8), HALF)] = mine_ref[...]
    grads_ref[pl.ds(pl.multiple_of(HALF - at, 8), HALF)] = other_ref[...]
    rows = lambda t: grads_ref[t * C : (t + 1) * C]
    scale = 1.0 / rows(2)[0:1, 126:127]
    for t in range(TAPS):
        dy, dz = t // 3, t % 3
        block = rows(t) * scale
        for dx in range(3):
            g2_ref[dx * TAPS + t] = block[:, dx * C : (dx + 1) * C]
        turned = block.T
        for f in range(F):
            for dx in range(3):
                to = (f * 3 + dx) * 3 + dy
                at = 96 + f * 3 + dx
                g1_ref[to, dz : dz + 1, :] = turned[at : at + 1]
                at = 111 + f * 3 + 2 - dx
                g3_ref[to, dz : dz + 1, :] = turned[at : at + 1]
        if t == 0:
            gb1_ref[...] = turned[126:127]
            gb2_ref[...] = turned[127:128]
        if t == 1:
            gb3_ref[...] = turned[126:127, 0:F]
            loss_ref[...] = turned[127:128, 0:1]


def reduce_steps(order):
    def near(c):
        return c ^ 1

    def far(c):
        return 3 - c

    steps = []
    for n in range(6):
        pairs = []
        for gx in range(8):
            for gy in range(16):
                at = {"x": gx // 2, "y": gy // 4, "z": (gy // 2 % 2) * 2 + gx % 2}
                axis = order[n // 2]
                at[axis] = (near, far)[n % 2](at[axis])
                to = (at["x"] * 2 + at["z"] % 2) * 16 + at["y"] * 4 + (at["z"] // 2) * 2 + (gy + 1) % 2
                pairs.append((gx * 16 + gy, to))
        steps.append(pairs)
    return steps


def sum_all(keep, send):
    cores = [(i, i ^ 1) for i in range(16)]
    mine = keep + lax.ppermute(send, "gy", cores)
    parts = [mine[: HALF // 2], mine[HALF // 2 :]]
    for pairs in zip(reduce_steps("zyx"), reduce_steps("xzy")):
        moved = [lax.ppermute(part, ("gx", "gy"), p) for part, p in zip(parts, pairs)]
        parts = [part + m for part, m in zip(parts, moved)]
    mine = jnp.concatenate(parts)
    return mine, lax.ppermute(mine, "gy", cores)


def on_device(
    initial_fields, velocity, diffusivity, patch_anchor, patch_count,
    weight_one, bias_one, weight_two, bias_two, weight_three, bias_three,
):
    place = jnp.stack([lax.axis_index("gx"), lax.axis_index("gy")]).astype(jnp.int32)
    u = initial_fields.reshape(F * X, 4, 2048)
    vel = velocity.reshape(3 * X, 4, 2048)
    anchors = patch_anchor.reshape(2)
    count = patch_count.reshape(1)

    edges = call(edges_kernel, EDGES, ins=[SMEM, VMEM], nbytes=1_000_000)(place, u)
    params = (
        jnp.transpose(weight_one, (1, 2, 3, 4, 0)).reshape(45, 3, C),
        jnp.transpose(weight_two, (2, 3, 4, 0, 1)).reshape(27, C, C),
        jnp.transpose(weight_three, (0, 2, 3, 4, 1)).reshape(45, 3, C),
        bias_one.reshape(1, C),
        bias_two.reshape(1, C),
        bias_three.reshape(1, F),
    )
    (slabs,) = call(slabs_kernel, [SLABS], ins=[VMEM], nbytes=1_500_000)(u)
    first_slabs = lax.all_to_all(slabs, "gy", 0, 0, tiled=True).reshape(32, 2 * F * X, Z)
    w1_band, w2_fwd, w2_bwd, w3_band, w3_turned, biases = call(
        prepare_kernel,
        [
            ((128, TALL), BF),
            ((3, 128, 384), BF),
            ((3, 128, 384), BF),
            ((TALL, 128), BF),
            ((128, TALL), BF),
            ((128, 128), F32),
        ],
        scratch=[pltpu.VMEM((256, 128), F32)]
        + [pltpu.VMEM(p.shape, F32) for p in params]
        + [pltpu.SemaphoreType.DMA((len(params),))],
        ins=[ANY] * len(params),
        nbytes=1_000_000,
    )(*params)

    for step in range(STEPS):
        last = step == STEPS - 1
        outs = [((F * X, 4, 2048), F32)] + ([SLABS] if last else EDGES)
        received = exchange(edges, last)
        (part,) = call(inner_kernel, [((F * X, 4, 2048), F32)], ins=[VMEM] * 3, nbytes=4_000_000, flops=BESIDE)(u, vel, diffusivity)
        kernel = lambda *refs, last=last: outer_kernel(last, *refs)
        u, *edges = call(kernel, outs, ins=[SMEM] + [VMEM] * 7, nbytes=3_000_000, flops=BESIDE)(
            place, part, *received, vel, diffusivity
        )

    (kept,) = call(
        forward_kernel,
        [KEPT],
        scratch=HELD
        + [
            pltpu.VMEM((2, ROWS, PY * Z), F32),
            pltpu.VMEM((2, TALL, PY * Z), BF),
            pltpu.VMEM((2, 384, (PY + 2) * Z), BF),
        ],
        ins=[SMEM] + [VMEM] * 5,
        flops=2_000_000_000,
        nbytes=8_000_000,
        mib=24,
        out_space=HBM,
    )(anchors, first_slabs, w1_band, w2_fwd, w3_band, biases)

    last_slabs = lax.all_to_all(edges[0], "gy", 0, 0, tiled=True).reshape(32, 2 * F * X, Z)
    keep, send = call(
        backward_kernel,
        [((HALF, 128), F32)] * 2,
        scratch=HELD
        + [
            pltpu.VMEM((2, ROWS, PY * Z), F32),
            pltpu.VMEM((2, TALL, PY * Z), BF),
            pltpu.VMEM((2, 384, (PY + 2) * Z), BF),
            pltpu.VMEM((2, TALL, PY * Z), BF),
            pltpu.VMEM((2, 384, (PY + 2) * Z), BF),
            pltpu.VMEM((2 * HALF, 128), F32),
        ],
        ins=[SMEM] * 3 + [VMEM] * 3 + [HBM],
        flops=4_000_000_000,
        nbytes=10_000_000,
        mib=24,
    )(place, anchors, count, last_slabs, w2_bwd, w3_turned, kept)

    g1, gb1, g2, gb2, g3, gb3, loss = call(
        finish_kernel,
        [((45, 3, C), F32), ((1, C), F32), ((27, C, C), F32), ((1, C), F32), ((45, 3, C), F32), ((1, F), F32), ((1, 1), F32)],
        scratch=[pltpu.VMEM((2 * HALF, 128), F32)],
        ins=[SMEM, VMEM, VMEM],
        nbytes=1_000_000,
    )(place, *sum_all(keep, send))
    g1 = jnp.transpose(g1.reshape(F, 3, 3, 3, C), (4, 0, 1, 2, 3))
    g2 = jnp.transpose(g2.reshape(3, 3, 3, C, C), (3, 4, 0, 1, 2))
    g3 = jnp.transpose(g3.reshape(F, 3, 3, 3, C), (0, 4, 1, 2, 3))
    gb1, gb2, gb3, loss = gb1.reshape(C), gb2.reshape(C), gb3.reshape(F), loss.reshape(())
    return u.reshape(F, X, 4, 2048), g1, gb1, g2, gb2, g3, gb3, loss


def solution(mesh):
    return jax.shard_map(
        on_device,
        mesh=mesh,
        in_specs=(
            P(None, "gx", "gy", None),
            P(None, "gx", "gy", None),
            P("gx", "gy", None),
            P("gx", "gy", None),
            P("gx", "gy"),
            P(),
            P(),
            P(),
            P(),
            P(),
            P(),
        ),
        out_specs=(P(None, "gx", "gy", None), P(), P(), P(), P(), P(), P(), P()),
        check_vma=False,
    )
```
